32 devices in a mesh: dp: 8 (over z, x), head: 4 (over y, core).
Axes of the slice: x: 2, y: 2, z: 4, core: 2. Of those that a mesh axis runs over, the one named last changes fastest.
Arguments:
- hidden_in: bfloat16 [8192, 768], P(('dp', 'head')), may hold values from -6 to 6
- out_cotangent: bfloat16 [8192, 768], P(('dp', 'head')), may hold values from -6 to 6
- labels: int32 [64], P(('dp', 'head')), may hold values from 0 to 2
- qkv_weight: bfloat16 [2, 3, 768, 768], P(None, None, None, 'head'), may hold values from -6 to 6
- qkv_bias: bfloat16 [2, 2, 768], P(None, None, 'head'), may hold values from -6 to 6
- out_weight: bfloat16 [2, 768, 768], P(None, 'head'), may hold values from -6 to 6
- out_bias: bfloat16 [2, 768], P(None, 'head'), may hold values from -6 to 6
- norm_gain: bfloat16 [2, 2, 768], P(None, None, 'head'), may hold values from 0.099609375 to 1.8984375
- norm_shift: bfloat16 [2, 2, 768], P(None, None, 'head'), may hold values from -6 to 6
- ffn_in: bfloat16 [2, 768, 3072], P(None, 'head'), may hold values from -6 to 6
- ffn_in_bias: bfloat16 [2, 3072], P(None, 'head'), may hold values from -6 to 6
- ffn_out: bfloat16 [2, 3072, 768], P(None, 'head'), may hold values from -6 to 6
- ffn_out_bias: bfloat16 [2, 768], P(None, 'head'), may hold values from -6 to 6
- pool_weight: bfloat16 [2, 768, 768], P(None, 'head'), may hold values from -6 to 6
- pool_bias: bfloat16 [2, 768], P(None, 'head'), may hold values from -6 to 6
- class_weight: bfloat16 [2, 768, 3], P(None, 'head'), may hold values from -6 to 6
- class_bias: bfloat16 [2, 3], replicated, may hold values from -6 to 6
Outputs:
- block_outputs: bfloat16 [2, 8192, 768], P(None, ('dp', 'head'))
- ramp_logits: float32 [2, 64, 3], P(None, ('dp', 'head'))
- input_grad: bfloat16 [8192, 768], P(('dp', 'head'))
- qkv_weight_grad: float32 [2, 3, 768, 768], P(None, None, None, 'head')
- qkv_bias_grad: float32 [2, 2, 768], P(None, None, 'head')
- out_weight_grad: float32 [2, 768, 768], P(None, 'head')
- out_bias_grad: float32 [2, 768], P(None, 'head')
- norm_gain_grad: float32 [2, 2, 768], P(None, None, 'head')
- norm_shift_grad: float32 [2, 2, 768], P(None, None, 'head')
- ffn_in_grad: float32 [2, 768, 3072], P(None, 'head')
- ffn_in_bias_grad: float32 [2, 3072], P(None, 'head')
- ffn_out_grad: float32 [2, 3072, 768], P(None, 'head')
- ffn_out_bias_grad: float32 [2, 768], P(None, 'head')
- pool_weight_grad: float32 [2, 768, 768], P(None, 'head')
- pool_bias_grad: float32 [2, 768], P(None, 'head')
- class_weight_grad: float32 [2, 768, 3], P(None, 'head')
- class_bias_grad: float32 [2, 3], replicated
The draws below stay inside these ranges and needn't reach their ends.
All inputs are finite; a program needn't handle non-finite values.
Results may differ from the reference program's by a relative error of at most 0.015.
Values may be sent and summed in bfloat16 or wider, within the bound.
No kernel may reach another device: no remote copies, remote signals or barrier semaphores. Data moves between devices by JAX's collectives and lax.ppermute only.
A program may use at most 256 MiB of HBM per device.

```python
import math
import jax
import jax.numpy as jnp
from jax import lax

D = 768
FF = 3072
HEADS = 12
HEAD_DIM = 64
SEQ = 128
CLASSES = 3
LAYERS = 2
TOKENS = 8192
SEQS = 64


def normal_part(key, shape, scale, bound):
    return jnp.clip(jax.random.normal(key, shape, jnp.float32) * scale, -bound, bound).astype(jnp.bfloat16)


def draw_hidden_in(key, part):
    key = jax.random.fold_in(key, 11)
    return normal_part(key, (TOKENS, D), 1.0, 4.0)


def draw_out_cotangent(key, part):
    key = jax.random.fold_in(key, 12)
    return normal_part(key, (TOKENS, D), 1.0, 4.0)


def draw_qkv_weight(key, part):
    key = jax.random.fold_in(key, 13)
    scale = D ** (-0.5)
    return normal_part(key, (LAYERS, 3, D, D), scale, 4.0 * scale)


def draw_qkv_bias(key, part):
    key = jax.random.fold_in(key, 14)
    return normal_part(key, (LAYERS, 2, D), 0.5, 2.0)


def draw_out_weight(key, part):
    key = jax.random.fold_in(key, 15)
    scale = (D // 16) ** (-0.5)
    return normal_part(key, (LAYERS, D, D), scale, 4.0 * scale)


def draw_out_bias(key, part):
    key = jax.random.fold_in(key, 16)
    return normal_part(key, (LAYERS, D), 0.5, 2.0)


def draw_norm_shift(key, part):
    key = jax.random.fold_in(key, 17)
    return normal_part(key, (LAYERS, 2, D), 0.3, 1.2)


def draw_ffn_in(key, part):
    key = jax.random.fold_in(key, 18)
    scale = D ** (-0.5)
    return normal_part(key, (LAYERS, D, FF), scale, 4.0 * scale)


def draw_ffn_in_bias(key, part):
    key = jax.random.fold_in(key, 19)
    return normal_part(key, (LAYERS, FF), 0.5, 2.0)


def draw_ffn_out(key, part):
    key = jax.random.fold_in(key, 20)
    scale = FF ** (-0.5)
    return normal_part(key, (LAYERS, FF, D), scale, 4.0 * scale)


def draw_ffn_out_bias(key, part):
    key = jax.random.fold_in(key, 21)
    return normal_part(key, (LAYERS, D), 0.5, 2.0)


def draw_pool_weight(key, part):
    key = jax.random.fold_in(key, 22)
    scale = D ** (-0.5)
    return normal_part(key, (LAYERS, D, D), scale, 4.0 * scale)


def draw_pool_bias(key, part):
    key = jax.random.fold_in(key, 23)
    return normal_part(key, (LAYERS, D), 0.5, 2.0)


def draw_class_weight(key, part):
    key = jax.random.fold_in(key, 24)
    scale = (D // 8) ** (-0.5)
    return normal_part(key, (LAYERS, D, CLASSES), scale, 4.0 * scale)


def draw_class_bias(key, part):
    key = jax.random.fold_in(key, 25)
    return normal_part(key, (LAYERS, CLASSES), 1.0, 3.0)


def place_ends(result, stream_key, least, top_value):
    longest = result.shape.index(max(result.shape))
    spots = []
    for shift in (0, 1):
        where = [jax.random.randint(jax.random.fold_in(stream_key, axis), (), 0, length) for axis, length in enumerate(result.shape)]
        where[longest] = (where[longest] + shift) % result.shape[longest]
        spots.append(tuple(where))
    return result.at[spots[0]].set(least).at[spots[1]].set(top_value)


def setup_inputs(seed: int = 0) -> dict:
    key_of = jax.random.split(jax.random.key(seed), 18)
    return {
        "hidden_in": draw_hidden_in(jax.random.fold_in(key_of[17], 71), 0),
        "out_cotangent": draw_out_cotangent(jax.random.fold_in(key_of[17], 71), 0),
        "labels": place_ends(jax.random.randint(key_of[2], (SEQS,), 0, CLASSES), jax.random.fold_in(key_of[2], 1), 0, CLASSES - 1).astype(jnp.int32),
        "qkv_weight": draw_qkv_weight(jax.random.fold_in(key_of[17], 71), 0),
        "qkv_bias": draw_qkv_bias(jax.random.fold_in(key_of[17], 71), 0),
        "out_weight": draw_out_weight(jax.random.fold_in(key_of[17], 71), 0),
        "out_bias": draw_out_bias(jax.random.fold_in(key_of[17], 71), 0),
        "norm_gain": jnp.clip(1.0 + 0.18 * jax.random.normal(key_of[7], (LAYERS, 2, D), jnp.float32), 0.099609375, 1.8984375).astype(jnp.bfloat16),
        "norm_shift": draw_norm_shift(jax.random.fold_in(key_of[17], 71), 0),
        "ffn_in": draw_ffn_in(jax.random.fold_in(key_of[17], 71), 0),
        "ffn_in_bias": draw_ffn_in_bias(jax.random.fold_in(key_of[17], 71), 0),
        "ffn_out": draw_ffn_out(jax.random.fold_in(key_of[17], 71), 0),
        "ffn_out_bias": draw_ffn_out_bias(jax.random.fold_in(key_of[17], 71), 0),
        "pool_weight": draw_pool_weight(jax.random.fold_in(key_of[17], 71), 0),
        "pool_bias": draw_pool_bias(jax.random.fold_in(key_of[17], 71), 0),
        "class_weight": draw_class_weight(jax.random.fold_in(key_of[17], 71), 0),
        "class_bias": draw_class_bias(jax.random.fold_in(key_of[17], 71), 0),
    }


@jax.custom_vjp
def low(v):
    return lax.optimization_barrier(v.astype(jnp.bfloat16)).astype(jnp.float32)

@jax.custom_vjp
def low_back(v):
    return v

def low_keep(v):
    return (low(v), None)

def low_pass(kept, grad):
    return (grad,)

def back_keep(v):
    return (v, None)

def back_low(kept, grad):
    return (low(grad),)
low.defvjp(low_keep, low_pass)
low_back.defvjp(back_keep, back_low)
EPS = 1e-12
HIGHEST = lax.Precision.HIGHEST

def matmul(left, right):
    return jnp.dot(left, right, precision=HIGHEST, preferred_element_type=jnp.float32)

def layer_norm(resid, gain_row, shift_row):
    average = lax.optimization_barrier(jnp.mean(resid, -1, keepdims=True))
    centred = resid - average
    return centred * lax.rsqrt(lax.optimization_barrier(jnp.mean(centred * centred, -1, keepdims=True)) + EPS) * gain_row + shift_row

def one_layer(hidden, params, seq_count):
    qkv_w, qkv_b, out_w, out_b, gains, shifts, in_w, in_b, down_w, down_b, pool_w, pool_b, class_w, class_b = params
    tokens = hidden.shape[0]
    projected = jnp.einsum('td,sde->ste', hidden, qkv_w, precision=HIGHEST)
    bias_rows = jnp.stack([qkv_b[0], jnp.zeros_like(qkv_b[0]), qkv_b[1]])
    qkv = low_back(low(projected + bias_rows[:, None, :]))
    split_qkv = qkv.reshape(3, seq_count, SEQ, HEADS, HEAD_DIM)
    scores = jnp.einsum('bqhe,bkhe->bhqk', split_qkv[0], split_qkv[1], precision=HIGHEST) * HEAD_DIM ** (-0.5)
    scores = low_back(scores)
    shifted = jnp.exp(scores - lax.optimization_barrier(jnp.max(scores, -1, keepdims=True)))
    probs = shifted / lax.optimization_barrier(jnp.sum(shifted, -1, keepdims=True))
    context = jnp.einsum('bhqk,bkhe->bqhe', low(probs), split_qkv[2], precision=HIGHEST)
    context = low_back(low(context.reshape(tokens, HEADS * HEAD_DIM)))
    attn_out = low_back(matmul(context, out_w) + out_b)
    middle = layer_norm(hidden + attn_out, gains[0], shifts[0])
    pre_act = low_back(matmul(low(middle), in_w) + in_b)
    ffn_res = low_back(matmul(low(jax.nn.gelu(pre_act, approximate=False)), down_w) + down_b)
    output = low(layer_norm(middle + ffn_res, gains[1], shifts[1]))
    first_rows = output.reshape(seq_count, SEQ, output.shape[1])[:, 0]
    pooled = low(jnp.tanh(low_back(matmul(first_rows, pool_w) + pool_b)))
    logits = low_back(matmul(pooled, class_w) + class_b)
    return (output, logits)

def ramp_loss(logits, label_rows):
    classes = lax.broadcasted_iota(jnp.int32, logits.shape, 1)
    picked = lax.optimization_barrier(jnp.sum(jnp.where(classes == label_rows[:, None], logits, 0.0), -1))
    return jnp.sum(jax.nn.logsumexp(logits, axis=-1) - picked)

def reference(hidden_in, out_cotangent, labels, qkv_weight, qkv_bias, out_weight, out_bias, norm_gain, norm_shift, ffn_in, ffn_in_bias, ffn_out, ffn_out_bias, pool_weight, pool_bias, class_weight, class_bias):
    weights = tuple((member.astype(jnp.float32) for member in (qkv_weight, qkv_bias, out_weight, out_bias, norm_gain, norm_shift, ffn_in, ffn_in_bias, ffn_out, ffn_out_bias, pool_weight, pool_bias, class_weight, class_bias)))
    seq_total = hidden_in.shape[0] // SEQ
    block_seqs = math.gcd(seq_total, max(1, 4096 // SEQ))
    blocks = seq_total // block_seqs
    block_tokens = block_seqs * SEQ
    inputs = hidden_in.astype(jnp.float32).reshape(blocks, block_tokens, D)
    cotangents = out_cotangent.astype(jnp.float32).reshape(blocks, block_tokens, D)
    label_blocks = labels.reshape(blocks, block_seqs)

    def block_loss(params, hidden, cotangent, label_rows):
        running = jnp.zeros((), jnp.float32)
        outputs = []
        logit_rows = []
        for layer_idx in range(LAYERS):
            hidden, logits = one_layer(hidden, tuple((member[layer_idx] for member in params)), block_seqs)
            running = running + ramp_loss(logits, label_rows)
            outputs.append(hidden)
            logit_rows.append(logits)
        running = running + jnp.sum(hidden * cotangent)
        return (running, (jnp.stack(outputs), jnp.stack(logit_rows)))

    def step(carry, block):
        hidden, cotangent, label_rows = block
        loss_value, pullback, extras = jax.vjp(lambda params, rows: block_loss(params, rows, cotangent, label_rows), weights, hidden, has_aux=True)
        grads, hidden_grad = pullback(jnp.ones_like(loss_value))
        carry = jax.tree.map(lambda running, update: running + update, carry, grads)
        return (carry, (extras[0], extras[1], hidden_grad))
    initial = jax.tree.map(jnp.zeros_like, weights)
    totals, (outputs, logits, hidden_grads) = lax.scan(step, initial, (inputs, cotangents, label_blocks))
    block_outputs = jnp.transpose(outputs, (1, 0, 2, 3)).reshape(LAYERS, blocks * block_tokens, D).astype(jnp.bfloat16)
    ramp_logits = jnp.transpose(logits, (1, 0, 2, 3)).reshape(LAYERS, seq_total, CLASSES)
    input_grad = hidden_grads.reshape(blocks * block_tokens, D).astype(jnp.bfloat16)
    return (block_outputs, ramp_logits, input_grad, totals[0], totals[1], totals[2], totals[3], totals[4], totals[5], totals[6], totals[7], totals[8], totals[9], totals[10], totals[11], totals[12], totals[13])
```

```python
import functools

import jax
import jax.numpy as jnp
from jax import lax
from jax.experimental import pallas as pl
from jax.experimental.pallas import tpu as pltpu
from jax.sharding import PartitionSpec as P

D = 768
FF = 3072
HEAD_DIM = 64
SEQ = 128
LAYERS = 2
SHARDS = 4
PART = D // SHARDS
POOL_PART = PART // 4
PIECES = 8
CLASSES = 3
EPS = 1e-12
ROOT_HALF = 0.7071067811865476
DENSITY_SCALE = 0.3989422804014327
F32 = jnp.float32
BF16 = jnp.bfloat16
AXES = ("dp", "head")
VMEM_LIMIT = 58 * 1024 * 1024

QB, VB, OB, G0, G1, S0, S1, FB, PB, CW = 0, 1, 2, 3, 4, 5, 6, 11, 12, 13


def dot(left, right, dims):
    return lax.dot_general(left, right, ((dims[:1], dims[1:]), ((), ())), preferred_element_type=F32)


def nn(left, right):
    return dot(left, right, (1, 0))


def nt(left, right):
    return dot(left, right, (1, 1))


def tn(left, right):
    return dot(left, right, (0, 0))


def normalise(resid):
    centred = resid - jnp.mean(resid, -1, keepdims=True)
    rstd = lax.rsqrt(jnp.mean(centred * centred, -1, keepdims=True) + EPS)
    return centred * rstd, rstd


def norm_back(incoming, normed, rstd, gain):
    scaled = incoming * gain
    back = rstd * (
        scaled
        - jnp.mean(scaled, -1, keepdims=True)
        - normed * jnp.mean(scaled * normed, -1, keepdims=True)
    )
    gain_grad = jnp.sum(incoming * normed, 0, keepdims=True)
    shift_grad = jnp.sum(incoming, 0, keepdims=True)
    return back, gain_grad, shift_grad


def cost(micros):
    return pl.CostEstimate(flops=0, bytes_accessed=int(micros * 3.5e6), transcendentals=0)


def shard_index():
    return lax.axis_index("head")


def quarter_index():
    return lax.axis_index("dp") & 3


def piece_index():
    place = lax.axis_index("dp")
    return ((place & 1) << 2) | (place & 2) | ((place >> 2) & 1)


def pack_attn_kernel(qkv_ref, out_ref, own_ref, quarter_ref):
    for part in range(3):
        own_ref[part] = qkv_ref[part].T
    own_ref[3] = out_ref[...]
    quarter_ref[...] = own_ref[quarter_index()]


def pack_attn(layer, qkv_weight, out_weight):
    return pl.pallas_call(
        pack_attn_kernel,
        grid=(1,),
        out_shape=(
            jax.ShapeDtypeStruct((4, PART, D), BF16),
            jax.ShapeDtypeStruct((PART, D), BF16),
        ),
        in_specs=[layer_block(layer, shape) for shape in ((3, D, PART), (PART, D))],
        out_specs=(
            pl.BlockSpec((4, PART, D), lambda step: (0, 0, 0)),
            pl.BlockSpec((PART, D), lambda step: (0, 0)),
        ),
        compiler_params=pltpu.CompilerParams(vmem_limit_bytes=VMEM_LIMIT),
        cost_estimate=cost(3),
        name="pack_attn%d" % layer,
    )(qkv_weight, out_weight)


FFN_ROWS = 2 * PART + POOL_PART


def pack_ffn_kernel(in_ref, down_ref, pool_ref, own_ref, quarter_ref):
    for index in range(4):
        own_ref[index, 0:PART] = in_ref[:, index * D : (index + 1) * D]
        own_ref[index, PART : 2 * PART] = down_ref[index * PART : (index + 1) * PART]
        own_ref[index, 2 * PART : FFN_ROWS] = pool_ref[
            index * POOL_PART : (index + 1) * POOL_PART
        ]
    quarter_ref[...] = own_ref[quarter_index()]


def layer_block(layer, shape):
    zeros = (0,) * len(shape)
    return pl.BlockSpec((None, *shape), lambda step: (layer, *zeros))


def pack_ffn(layer, ffn_in, ffn_out, pool_weight):
    return pl.pallas_call(
        pack_ffn_kernel,
        grid=(1,),
        out_shape=(
            jax.ShapeDtypeStruct((4, FFN_ROWS, D), BF16),
            jax.ShapeDtypeStruct((FFN_ROWS, D), BF16),
        ),
        in_specs=[layer_block(layer, shape) for shape in ((PART, FF), (D, D), (PART, D))],
        out_specs=(
            pl.BlockSpec((4, FFN_ROWS, D), lambda step: (0, 0, 0)),
            pl.BlockSpec((FFN_ROWS, D), lambda step: (0, 0)),
        ),
        compiler_params=pltpu.CompilerParams(vmem_limit_bytes=VMEM_LIMIT),
        cost_estimate=cost(3),
        name="pack_ffn%d" % layer,
    )(ffn_in, ffn_out, pool_weight)


def flip(mesh, axis, bit):
    dp, head = mesh.shape["dp"], mesh.shape["head"]
    pairs = []
    for place in range(dp):
        for shard in range(head):
            to_place = place ^ bit if axis == "dp" else place
            to_shard = shard ^ bit if axis == "head" else shard
            pairs.append((place * head + shard, to_place * head + to_shard))
    return pairs


class Moves:
    def __init__(self, mesh):
        self.mesh = mesh

    def core(self, value):
        return lax.ppermute(value, AXES, flip(self.mesh, "head", 1))

    def row(self, value):
        return lax.ppermute(value, AXES, flip(self.mesh, "head", 2))

    def place(self, value, bit):
        return lax.ppermute(value, AXES, flip(self.mesh, "dp", bit))


    def gather(self, value):
        for axis in ("head", "dp"):
            bit = 1
            while bit < self.mesh.shape[axis]:
                came = lax.ppermute(value, AXES, flip(self.mesh, axis, bit))
                value = jnp.concatenate([value, came], 0)
                bit *= 2
        return value


def gather_weights(moves, own, quarter, last_bit):
    near = moves.core(own)
    far = [None] * 4
    far[0] = moves.row(quarter)
    far[1] = moves.place(far[0], 1)
    far[2] = moves.place(far[0], 2)
    far[3] = moves.place(far[2], 1) if last_bit == 1 else moves.place(far[1], 2)
    return (own, near, *far, *[moves.core(piece) for piece in far])


def load_attn_weights(refs, slots, sems):
    here = quarter_index()
    own, near, *pieces = refs
    copies = [
        [pltpu.make_async_copy(own, slots.at[0], sems.at[0])],
        [pltpu.make_async_copy(near, slots.at[1], sems.at[1])],
        [],
        [],
    ]
    for index, piece in enumerate(pieces):
        slot, relative = 2 + index // 4, index % 4
        copies[slot].append(
            pltpu.make_async_copy(piece, slots.at[slot, here ^ relative], sems.at[2 + index])
        )
    for group in copies:
        for item in group:
            item.start()
    return copies


def attn_forward_kernel(layer, x_ref, shard_small, small, *refs):
    weights = refs[:10]
    qkv_ref, probs_ref, context_ref, context_send_ref = refs[10:14]
    normed_ref, rstd_ref, low_ref, parts_ref, parts_send_ref = refs[14:19]
    slots, all_parts, sems = refs[19:]
    copies = load_attn_weights(weights, slots, sems)
    shard = shard_index()
    x = x_ref[...]
    total = x.astype(F32) + small[layer, OB : OB + 1].astype(F32)
    for slot in range(4):
        for item in copies[slot]:
            item.wait()
        biases = shard_small[shard ^ slot, layer]
        parts = []
        for part in range(3):
            value = nt(x, slots[slot, part])
            if part != 1:
                row = QB if part == 0 else VB
                value = value + biases[row : row + 1].astype(F32)
            value = value.astype(BF16)
            qkv_ref[slot, part] = value
            parts.append(value)
        query, key, val = parts
        seq_rows = []
        for seq in range(2):
            rows = slice(seq * SEQ, (seq + 1) * SEQ)
            heads = []
            for head in range(PART // HEAD_DIM):
                cols = slice(head * HEAD_DIM, (head + 1) * HEAD_DIM)
                scores = nt(query[rows, cols], key[rows, cols]) * HEAD_DIM ** (-0.5)
                shifted = jnp.exp(scores - jnp.max(scores, -1, keepdims=True))
                probs = shifted / jnp.sum(shifted, -1, keepdims=True)
                probs_ref[slot, seq * 3 + head] = probs
                heads.append(nn(probs.astype(BF16), val[rows, cols]))
            seq_rows.append(jnp.concatenate(heads, -1))
        context = jnp.concatenate(seq_rows, 0).astype(BF16)
        target = context_send_ref if slot & 1 else context_ref
        target[slot >> 1] = context
        total = total + nn(context, slots[slot, 3])
    normed, rstd = normalise(total)
    normed_ref[...] = normed
    rstd_ref[...] = rstd
    middle = normed * small[layer, G0 : G0 + 1].astype(F32) + small[layer, S0 : S0 + 1].astype(F32)
    low = middle.astype(BF16)
    low_ref[...] = low
    for part in range(SHARDS):
        all_parts[part] = low[:, part * PART : (part + 1) * PART]
    for slot in range(4):
        target = parts_send_ref if slot & 1 else parts_ref
        target[slot >> 1] = all_parts[shard ^ slot]


def vmem():
    return pl.BlockSpec(memory_space=pltpu.VMEM)


def anywhere():
    return pl.BlockSpec(memory_space=pl.ANY)


def attn_forward(layer, x, shard_small, small, weights):
    tokens = x.shape[0]
    shapes = (
        ((4, 3, tokens, PART), BF16),
        ((4, 6, SEQ, SEQ), F32),
        ((2, tokens, PART), BF16),
        ((2, tokens, PART), BF16),
        ((tokens, D), F32),
        ((tokens, 1), F32),
        ((tokens, D), BF16),
        ((2, tokens, PART), BF16),
        ((2, tokens, PART), BF16),
    )
    return pl.pallas_call(
        functools.partial(attn_forward_kernel, layer),
        out_shape=tuple(jax.ShapeDtypeStruct(*item) for item in shapes),
        in_specs=[vmem()] * 3 + [anywhere()] * 10,
        out_specs=tuple(vmem() for _ in shapes),
        scratch_shapes=[
            pltpu.VMEM((4, 4, PART, D), BF16),
            pltpu.VMEM((SHARDS, tokens, PART), BF16),
            pltpu.SemaphoreType.DMA((10,)),
        ],
        compiler_params=pltpu.CompilerParams(vmem_limit_bytes=VMEM_LIMIT),
        cost_estimate=cost(13),
        name="attn_forward%d" % layer,
    )(x, shard_small, small, *weights)


def load_ffn_weights(refs, up, down, pool, sems):
    here = quarter_index()
    shard = shard_index()
    own, near, *pieces = refs
    copies = []

    def copy(src, dst):
        copies.append(pltpu.make_async_copy(src, dst, sems.at[len(copies)]))
        copies[-1].start()

    def rows_of(owner):
        return pl.ds(pl.multiple_of(owner * PART, PART), PART)

    for slot, whole in ((0, own), (1, near)):
        owner = shard ^ slot
        copy(whole.at[:, 0:PART], up.at[:, rows_of(owner)])
        copy(whole.at[:, PART : 2 * PART], down.at[owner])
        if pool is not None:
            copy(whole.at[:, 2 * PART : FFN_ROWS], pool.at[owner])
    for index, piece in enumerate(pieces):
        owner, block = shard ^ (2 + index // 4), here ^ (index % 4)
        copy(piece.at[0:PART], up.at[block, rows_of(owner)])
        copy(piece.at[PART : 2 * PART], down.at[owner, block])
        if pool is not None:
            copy(piece.at[2 * PART : FFN_ROWS], pool.at[owner, block])
    return copies


def ffn_forward_kernel(layer, labels_ref, class_bias_ref, normed_ref, low_ref, small, in_bias, *refs):
    weights = refs[:10]
    act_ref, act_send_ref, slope_ref, normed_two_ref, rstd_two_ref, out_ref = refs[10:16]
    logits_ref, ramp_ref, first_grad_ref = refs[16:19]
    up, down, pool, acts, sems = refs[19:]
    copies = load_ffn_weights(weights, up, down, pool, sems)
    normed = normed_ref[...]
    low = low_ref[...]

    def row(index):
        return small[layer, index : index + 1].astype(F32)

    total = normed * row(G0) + row(S0) + row(FB)
    for item in copies:
        item.wait()
    for block in range(4):
        pre_act = nn(low, up[block]) + in_bias[layer, block : block + 1].astype(F32)
        cumulative = 0.5 * (1.0 + lax.erf(pre_act * ROOT_HALF))
        act = (pre_act * cumulative).astype(BF16)
        density = jnp.exp(-0.5 * pre_act * pre_act) * DENSITY_SCALE
        acts[block] = act
        slope_ref[block] = cumulative + pre_act * density
        total = total + nn(act, down[block].reshape(D, D))
    shard = shard_index()
    for slot in range(4):
        target = act_send_ref if slot & 1 else act_ref
        target[slot >> 1] = acts[shard ^ slot]
    normed_two, rstd_two = normalise(total)
    normed_two_ref[...] = normed_two
    rstd_two_ref[...] = rstd_two
    output = (normed_two * row(G1) + row(S1)).astype(BF16)
    out_ref[...] = output

    first = jnp.concatenate([output[0:1], output[SEQ : SEQ + 1]], 0).astype(F32)
    first = jnp.concatenate([first, jnp.zeros((14, D), F32)], 0).astype(BF16)
    pool_weight = pool[...].reshape(D, D)
    pooled = jnp.tanh(nn(first, pool_weight) + row(PB))
    pooled_low = pooled.astype(BF16)
    wide = pooled_low.astype(F32)
    lanes = lax.broadcasted_iota(jnp.int32, (16, 128), 1)
    rows = lax.broadcasted_iota(jnp.int32, (16, 128), 0)
    logits = jnp.zeros((16, 128), F32)
    for cls in range(CLASSES):
        value = jnp.sum(wide * row(CW + cls), -1, keepdims=True)
        value = value + class_bias_ref[layer, cls]
        logits = jnp.where(lanes == cls, value, logits)
    logits_ref[...] = logits[0:8]
    valid = lanes < CLASSES
    peak = jnp.max(jnp.where(valid, logits, -jnp.inf), -1, keepdims=True)
    shifted = jnp.where(valid, jnp.exp(logits - peak), 0.0)
    soft = shifted / jnp.sum(shifted, -1, keepdims=True)
    label = jnp.where(rows == 0, labels_ref[0], labels_ref[1])
    logit_grad = (soft - (lanes == label).astype(F32)).astype(BF16)
    logit_wide = logit_grad.astype(F32)
    back = jnp.zeros((16, D), F32)
    for cls in range(CLASSES):
        picked = jnp.sum(jnp.where(lanes == cls, logit_wide, 0.0), -1, keepdims=True)
        back = back + picked * row(CW + cls)
    pool_grad = (back * (1.0 - pooled * pooled)).astype(BF16)
    first_grad_ref[...] = nt(pool_grad, pool_weight)[0:8]
    padded = jnp.concatenate([logit_wide[0:2], jnp.zeros((2, D - 128), F32)], -1)
    ramp_ref[...] = jnp.concatenate(
        [first.astype(F32)[0:2], pool_grad.astype(F32)[0:2], wide[0:2], padded], 0
    ).astype(BF16)


def ffn_forward(layer, labels, class_bias, normed, low, small, in_bias, weights):
    tokens = low.shape[0]
    shapes = (
        ((2, tokens, D), BF16),
        ((2, tokens, D), BF16),
        ((4, tokens, D), F32),
        ((tokens, D), F32),
        ((tokens, 1), F32),
        ((tokens, D), BF16),
        ((8, 128), F32),
        ((8, D), BF16),
        ((8, D), F32),
    )
    smem = pl.BlockSpec(memory_space=pltpu.SMEM)
    return pl.pallas_call(
        functools.partial(ffn_forward_kernel, layer),
        out_shape=tuple(jax.ShapeDtypeStruct(*item) for item in shapes),
        in_specs=[smem, smem] + [vmem()] * 4 + [anywhere()] * 10,
        out_specs=tuple(vmem() for _ in shapes),
        scratch_shapes=[
            pltpu.VMEM((4, D, D), BF16),
            pltpu.VMEM((SHARDS, 4, PART, D), BF16),
            pltpu.VMEM((SHARDS, 4, POOL_PART, D), BF16),
            pltpu.VMEM((4, tokens, D), BF16),
            pltpu.SemaphoreType.DMA((30,)),
        ],
        compiler_params=pltpu.CompilerParams(vmem_limit_bytes=VMEM_LIMIT),
        cost_estimate=cost(11),
        name="ffn_forward%d" % layer,
    )(labels, class_bias, normed, low, small, in_bias, *weights)


def ffn_backward_kernel(
    layer, grad_ref, first_ref, normed_two_ref, rstd_two_ref, slope_ref, normed_ref, rstd_ref, small,
    *refs
):
    weights = refs[:10]
    pairs_ref, rows_ref, low_ref, smalls_ref = refs[10:14]
    up, down, sems = refs[14:]
    copies = load_ffn_weights(weights, up, down, None, sems)

    def row(index):
        return small[layer, index : index + 1].astype(F32)

    grad = grad_ref[...].astype(F32)
    index = lax.broadcasted_iota(jnp.int32, grad.shape, 0)
    grad = grad + jnp.where(index == 0, first_ref[0:1], 0.0)
    grad = grad + jnp.where(index == SEQ, first_ref[1:2], 0.0)
    res_two, gain_two, shift_two = norm_back(grad, normed_two_ref[...], rstd_two_ref[...], row(G1))
    ffn_grad = res_two.astype(BF16)
    pairs_ref[4] = ffn_grad
    for item in copies:
        item.wait()
    middle_grad = res_two
    for block in range(4):
        act_grad = nt(ffn_grad, down[block].reshape(D, D))
        pre_grad = (act_grad * slope_ref[block]).astype(BF16)
        pairs_ref[block] = pre_grad
        smalls_ref[block : block + 1] = jnp.sum(pre_grad.astype(F32), 0, keepdims=True)
        middle_grad = middle_grad + nt(pre_grad, up[block])
    res_one, gain_one, shift_one = norm_back(middle_grad, normed_ref[...], rstd_ref[...], row(G0))
    rows_ref[...] = res_one
    low = res_one.astype(BF16)
    low_ref[...] = low
    smalls_ref[4:5] = jnp.sum(ffn_grad.astype(F32), 0, keepdims=True)
    smalls_ref[5:6] = jnp.sum(low.astype(F32), 0, keepdims=True)
    smalls_ref[6:7] = gain_one
    smalls_ref[7:8] = gain_two
    smalls_ref[8:9] = shift_one
    smalls_ref[9:10] = shift_two


def ffn_backward(
    layer, grad, first_grad, normed_two, rstd_two, slope, normed, rstd, small, weights
):
    tokens = grad.shape[0]
    shapes = (
        ((5, tokens, D), BF16),
        ((tokens, D), F32),
        ((tokens, D), BF16),
        ((10, D), F32),
    )
    return pl.pallas_call(
        functools.partial(ffn_backward_kernel, layer),
        out_shape=tuple(jax.ShapeDtypeStruct(*item) for item in shapes),
        in_specs=[vmem()] * 8 + [anywhere()] * 10,
        out_specs=tuple(vmem() for _ in shapes),
        scratch_shapes=[
            pltpu.VMEM((4, D, D), BF16),
            pltpu.VMEM((SHARDS, 4, PART, D), BF16),
            pltpu.SemaphoreType.DMA((20,)),
        ],
        compiler_params=pltpu.CompilerParams(vmem_limit_bytes=VMEM_LIMIT),
        cost_estimate=cost(9),
        name="ffn_backward%d" % layer,
    )(grad, first_grad, normed_two, rstd_two, slope, normed, rstd, small, *weights)


def ffn_weights_kernel(
    act_ref, act_near_ref, parts_ref, parts_near_ref, pairs_ref, pairs_near_ref, keep_ref, send_ref
):
    place = piece_index()
    for slot in range(2):
        target = send_ref if slot else keep_ref
        down_grad = tn(act_ref[slot], pairs_ref[4]) + tn(act_near_ref[slot], pairs_near_ref[4])
        down_grad = down_grad.astype(BF16)
        for block in range(4):
            target[(4 + block) ^ place] = down_grad[block * PART : (block + 1) * PART]
            up_grad = tn(parts_ref[slot], pairs_ref[block])
            up_grad = up_grad + tn(parts_near_ref[slot], pairs_near_ref[block])
            target[block ^ place] = up_grad.astype(BF16)


def ffn_weight_grads(layer, act, act_near, parts, parts_near, pairs, pairs_near):
    shape = jax.ShapeDtypeStruct((PIECES, PART, D), BF16)
    return pl.pallas_call(
        ffn_weights_kernel,
        out_shape=(shape, shape),
        compiler_params=pltpu.CompilerParams(vmem_limit_bytes=VMEM_LIMIT),
        cost_estimate=cost(8),
        name="ffn_weight_grads%d" % layer,
    )(act, act_near, parts, parts_near, pairs, pairs_near)


def attn_backward_kernel(res_ref, grad_ref, qkv_ref, probs_ref, *refs):
    weights = refs[:10]
    pairs_ref, pairs_send_ref, rows_ref, biases_ref = refs[10:14]
    slots, sems = refs[14:]
    copies = load_attn_weights(weights, slots, sems)
    shard = shard_index()
    grad = grad_ref[...]
    total = res_ref[...]
    for slot in range(4):
        for item in copies[slot]:
            item.wait()
        target = pairs_send_ref if slot & 1 else pairs_ref
        context_grad = nt(grad, slots[slot, 3]).astype(BF16)
        seq_rows = [[], [], []]
        for seq in range(2):
            rows = slice(seq * SEQ, (seq + 1) * SEQ)
            heads = [[], [], []]
            for head in range(PART // HEAD_DIM):
                cols = slice(head * HEAD_DIM, (head + 1) * HEAD_DIM)
                query = qkv_ref[slot, 0, rows, cols]
                key = qkv_ref[slot, 1, rows, cols]
                val = qkv_ref[slot, 2, rows, cols]
                probs = probs_ref[slot, seq * 3 + head]
                back = context_grad[rows, cols]
                prob_grad = nt(back, val)
                mean = jnp.sum(prob_grad * probs, -1, keepdims=True)
                score_grad = (probs * (prob_grad - mean)).astype(BF16)
                heads[0].append(nn(score_grad, key) * HEAD_DIM ** (-0.5))
                heads[1].append(tn(score_grad, query) * HEAD_DIM ** (-0.5))
                heads[2].append(tn(probs.astype(BF16), back))
            for part in range(3):
                seq_rows[part].append(jnp.concatenate(heads[part], -1))
        bias_rows = []
        for part in range(3):
            value = jnp.concatenate(seq_rows[part], 0).astype(BF16)
            target[slot >> 1, part] = value
            if part != 1:
                bias_rows.append(jnp.sum(value.astype(F32), 0, keepdims=True))
            total = total + nn(value, slots[slot, part])
        biases_ref[shard ^ slot] = jnp.concatenate(bias_rows, 0)
    rows_ref[...] = total.astype(rows_ref.dtype)


def attn_backward(layer, res, grad, qkv, probs, weights):
    tokens = grad.shape[0]
    shapes = (
        ((2, 3, tokens, PART), BF16),
        ((2, 3, tokens, PART), BF16),
        ((tokens, D), BF16 if layer == 0 else F32),
        ((SHARDS, 2, PART), F32),
    )
    return pl.pallas_call(
        attn_backward_kernel,
        out_shape=tuple(jax.ShapeDtypeStruct(*item) for item in shapes),
        in_specs=[vmem()] * 4 + [anywhere()] * 10,
        out_specs=tuple(vmem() for _ in shapes),
        scratch_shapes=[pltpu.VMEM((4, 4, PART, D), BF16), pltpu.SemaphoreType.DMA((10,))],
        compiler_params=pltpu.CompilerParams(vmem_limit_bytes=VMEM_LIMIT),
        cost_estimate=cost(12),
        name="attn_backward%d" % layer,
    )(res, grad, qkv, probs, *weights)


def attn_weights_kernel(
    x_ref, x_near_ref, grad_ref, grad_near_ref, context_ref, context_near_ref, pairs_ref,
    pairs_near_ref, keep_ref, send_ref
):
    place = piece_index()
    half = PART // 2
    for slot in range(2):
        target = send_ref if slot else keep_ref
        for unit in range(4):
            if unit == 3:
                value = tn(context_ref[slot], grad_ref[...])
                value = value + tn(context_near_ref[slot], grad_near_ref[...])
            else:
                value = tn(pairs_ref[slot, unit], x_ref[...])
                value = value + tn(pairs_near_ref[slot, unit], x_near_ref[...])
            value = value.astype(BF16)
            for part in range(2):
                target[(2 * unit + part) ^ place] = value[part * half : (part + 1) * half]


def attn_weight_grads(layer, *operands):
    shape = jax.ShapeDtypeStruct((PIECES, PART // 2, D), BF16)
    return pl.pallas_call(
        attn_weights_kernel,
        out_shape=(shape, shape),
        compiler_params=pltpu.CompilerParams(vmem_limit_bytes=VMEM_LIMIT),
        cost_estimate=cost(6),
        name="attn_weight_grads%d" % layer,
    )(*operands)


def reduce_pieces(moves, mine, theirs):
    came = moves.row(theirs)
    dp = moves.mesh.shape["dp"]
    count = PIECES
    for bit in (1, 2, 4):
        count //= 2
        low, high = mine[:count] + came[:count], mine[count:] + came[count:]
        mine, came = low, moves.place(high, bit)
    mine = mine + came
    bit = 8
    while bit < dp:
        mine = mine + moves.place(mine, bit)
        bit *= 2
    mine = jnp.concatenate([mine, moves.place(mine, 4)], 0)
    mine = jnp.concatenate([mine, moves.place(mine, 2)], 0)
    return mine, moves.place(mine, 1)


def stacked_call(kernel, layer, pieces, shapes, previous, scratch, name):
    prior = () if previous is None else tuple(previous)
    return pl.pallas_call(
        kernel,
        out_shape=tuple(jax.ShapeDtypeStruct(shape, F32) for shape in shapes),
        in_specs=[vmem()] * 2 + [anywhere()] * len(prior),
        out_specs=tuple(anywhere() for _ in shapes),
        input_output_aliases={2 + index: index for index in range(len(prior))},
        scratch_shapes=scratch,
        compiler_params=pltpu.CompilerParams(vmem_limit_bytes=VMEM_LIMIT),
        cost_estimate=cost(3),
        name=name,
    )(*pieces, *prior)


def natural_order(near_ref, far_ref, whole):
    place = piece_index()
    for index in range(4):
        whole[index ^ place] = near_ref[index].astype(F32)
        whole[(4 + index) ^ place] = far_ref[index].astype(F32)


def ffn_unpack_kernel(layer, near_ref, far_ref, *refs):
    in_ref, down_ref, whole, sems = refs[-4:]
    natural_order(near_ref, far_ref, whole)
    copies = []
    for block in range(4):
        copies.append((whole.at[block], in_ref.at[layer, :, block * D : (block + 1) * D]))
        copies.append(
            (whole.at[4 + block], down_ref.at[layer, block * PART : (block + 1) * PART])
        )
    copies = [
        pltpu.make_async_copy(src, dst, sems.at[index]) for index, (src, dst) in enumerate(copies)
    ]
    for item in copies:
        item.start()
    for item in copies:
        item.wait()


def ffn_unpack(layer, pieces, previous):
    return stacked_call(
        functools.partial(ffn_unpack_kernel, layer),
        layer,
        pieces,
        ((LAYERS, PART, FF), (LAYERS, D, D)),
        previous,
        [pltpu.VMEM((PIECES, PART, D), F32), pltpu.SemaphoreType.DMA((8,))],
        "ffn_unpack%d" % layer,
    )


def attn_unpack_kernel(layer, near_ref, far_ref, *refs):
    qkv_ref, out_ref, whole, turned, sems = refs[-5:]
    natural_order(near_ref, far_ref, whole)
    half = PART // 2
    copies = [
        pltpu.make_async_copy(
            whole.at[6 + part], out_ref.at[layer, part * half : (part + 1) * half], sems.at[part]
        )
        for part in range(2)
    ]
    for item in copies:
        item.start()
    for unit in range(3):
        turned[unit] = whole[2 * unit : 2 * unit + 2].reshape(PART, D).T
        copies.append(
            pltpu.make_async_copy(turned.at[unit], qkv_ref.at[layer, unit], sems.at[2 + unit])
        )
        copies[-1].start()
    for item in copies:
        item.wait()


def attn_unpack(layer, pieces, previous):
    return stacked_call(
        functools.partial(attn_unpack_kernel, layer),
        layer,
        pieces,
        ((LAYERS, 3, D, PART), (LAYERS, PART, D)),
        previous,
        [
            pltpu.VMEM((PIECES, PART // 2, D), F32),
            pltpu.VMEM((3, D, PART), F32),
            pltpu.SemaphoreType.DMA((5,)),
        ],
        "attn_unpack%d" % layer,
    )


def on_device(
    mesh,
    hidden_in,
    out_cotangent,
    labels,
    qkv_weight,
    qkv_bias,
    out_weight,
    out_bias,
    norm_gain,
    norm_shift,
    ffn_in,
    ffn_in_bias,
    ffn_out,
    ffn_out_bias,
    pool_weight,
    pool_bias,
    class_weight,
    class_bias,
):
    moves = Moves(mesh)
    shard = shard_index()
    packed = jnp.concatenate(
        [
            qkv_bias,
            out_bias[:, None],
            norm_gain,
            norm_shift,
            ffn_in_bias.reshape(LAYERS, 4, PART),
            ffn_out_bias[:, None],
            pool_bias[:, None],
            jnp.swapaxes(class_weight, 1, 2),
        ],
        1,
    )
    shard_small = lax.all_gather(packed, "head", axis=0)
    small = jnp.transpose(shard_small, (1, 2, 0, 3)).reshape(LAYERS, 16, D)
    in_bias = jnp.transpose(shard_small[:, :, 7:11], (1, 0, 2, 3)).reshape(LAYERS, SHARDS, D)
    class_bias_wide = class_bias.astype(F32)

    attn_weights, ffn_weights = [], []
    for layer in range(LAYERS):
        attn_weights.append(
            gather_weights(moves, *pack_attn(layer, qkv_weight, out_weight), 2)
        )
        ffn_weights.append(
            gather_weights(moves, *pack_ffn(layer, ffn_in, ffn_out, pool_weight), 1)
        )

    x = hidden_in
    kept, outputs, logits, ramps = [], [], [], []
    for layer in range(LAYERS):
        x_near = moves.core(x)
        qkv, probs, context, context_send, normed, rstd, low, parts, parts_send = attn_forward(
            layer, x, shard_small, small, attn_weights[layer]
        )
        context_near, parts_near = moves.core(context_send), moves.core(parts_send)
        act, act_send, slope, normed_two, rstd_two, output, logit, ramp, first_grad = ffn_forward(
            layer, labels, class_bias_wide, normed, low, small, in_bias, ffn_weights[layer]
        )
        act_near = moves.core(act_send)
        kept.append(
            (
                (x, x_near),
                (qkv, probs, (context, context_near), normed, rstd, (parts, parts_near)),
                ((act, act_near), slope, normed_two, rstd_two, first_grad),
            )
        )
        outputs.append(output)
        logits.append(logit[0:2, 0:CLASSES])
        ramps.append(ramp)
        x = output

    grad = out_cotangent
    attn_parts, ffn_parts, smalls = [None] * LAYERS, [None] * LAYERS, [None] * LAYERS
    for layer in reversed(range(LAYERS)):
        xs, attn_kept, ffn_kept = kept[layer]
        qkv, probs, contexts, normed, rstd, parts = attn_kept
        acts, slope, normed_two, rstd_two, first_grad = ffn_kept
        pairs, res_one, low, rows = ffn_backward(
            layer, grad, first_grad, normed_two, rstd_two, slope, normed, rstd, small,
            ffn_weights[layer],
        )
        pairs_near, low_near = moves.core(pairs), moves.core(low)
        attn_pairs, attn_pairs_send, grad, biases = attn_backward(
            layer, res_one, low, qkv, probs, attn_weights[layer]
        )
        attn_pairs_near = moves.core(attn_pairs_send)
        ffn_parts[layer] = reduce_pieces(
            moves, *ffn_weight_grads(layer, *acts, *parts, pairs, pairs_near)
        )
        attn_parts[layer] = reduce_pieces(
            moves,
            *attn_weight_grads(
                layer, *xs, low, low_near, *contexts, attn_pairs, attn_pairs_near
            ),
        )
        smalls[layer] = jnp.concatenate(
            [rows, jnp.transpose(biases, (1, 0, 2)).reshape(2, D)], 0
        )

    ffn_grads, attn_grads = None, None
    for layer in reversed(range(LAYERS)):
        ffn_grads = ffn_unpack(layer, ffn_parts[layer], ffn_grads)
        attn_grads = attn_unpack(layer, attn_parts[layer], attn_grads)
    in_grad, down_grad = ffn_grads
    qkv_grad, out_grad = attn_grads

    ramp = moves.gather(jnp.stack(ramps)[None])
    ramp = ramp.reshape(ramp.shape[0], LAYERS, 4, 2, D)
    ramp = jnp.transpose(ramp, (1, 2, 0, 3, 4)).reshape(LAYERS, 4, -1, D)
    first, pool_grad, pooled, logit_grad = (ramp[:, part] for part in range(4))
    logit_grad = logit_grad[:, :, 0:CLASSES]
    own_first = lax.dynamic_slice_in_dim(first, shard * PART, PART, 2)
    own_pooled = lax.dynamic_slice_in_dim(pooled, shard * PART, PART, 2)
    pool_weight_grad = jnp.einsum("lnd,lne->lde", own_first, pool_grad, preferred_element_type=F32)
    class_weight_grad = jnp.einsum(
        "lnd,lnc->ldc", own_pooled, logit_grad, preferred_element_type=F32
    )
    class_bias_grad = jnp.sum(logit_grad.astype(F32), 1)
    own_pool = lax.dynamic_slice_in_dim(pool_grad, shard * PART, PART, 2)
    pool_bias_grad = jnp.sum(own_pool.astype(F32), 1)

    total = lax.psum(jnp.stack(smalls), AXES)
    in_bias_grad = lax.dynamic_index_in_dim(total[:, 0:4], shard, 1, keepdims=False)
    total = lax.dynamic_slice_in_dim(total[:, 4:], shard * PART, PART, 2)
    return (
        jnp.stack(outputs),
        jnp.stack(logits),
        grad,
        qkv_grad,
        total[:, 6:8],
        out_grad,
        total[:, 1],
        total[:, 2:4],
        total[:, 4:6],
        in_grad,
        in_bias_grad,
        down_grad,
        total[:, 0],
        pool_weight_grad,
        pool_bias_grad,
        class_weight_grad,
        class_bias_grad,
    )


def solution(mesh):
    return jax.shard_map(
        functools.partial(on_device, mesh),
        mesh=mesh,
        in_specs=(
            P(("dp", "head"), None),
            P(("dp", "head"), None),
            P(("dp", "head")),
            P(None, None, None, "head"),
            P(None, None, "head"),
            P(None, "head", None),
            P(None, "head"),
            P(None, None, "head"),
            P(None, None, "head"),
            P(None, "head", None),
            P(None, "head"),
            P(None, "head", None),
            P(None, "head"),
            P(None, "head", None),
            P(None, "head"),
            P(None, "head", None),
            P(),
        ),
        out_specs=(
            P(None, ("dp", "head"), None),
            P(None, ("dp", "head"), None),
            P(("dp", "head"), None),
            P(None, None, None, "head"),
            P(None, None, "head"),
            P(None, "head", None),
            P(None, "head"),
            P(None, None, "head"),
            P(None, None, "head"),
            P(None, "head", None),
            P(None, "head"),
            P(None, "head", None),
            P(None, "head"),
            P(None, "head", None),
            P(None, "head"),
            P(None, "head", None),
            P(),
        ),
        check_vma=False,
    )
```

```python
import functools

import jax
import jax.numpy as jnp
from jax import lax
from jax.experimental import pallas as pl
from jax.experimental.pallas import tpu as pltpu
from jax.sharding import PartitionSpec as P

D = 768
FF = 3072
HEAD_DIM = 64
SEQ = 128
LAYERS = 2
SHARDS = 4
PART = D // SHARDS
POOL_PART = PART // 4
CLASSES = 3
EPS = 1e-12
ROOT_HALF = 0.7071067811865476
DENSITY_SCALE = 0.3989422804014327
F32 = jnp.float32
BF16 = jnp.bfloat16
AXES = ("dp", "head")
VMEM_LIMIT = 58 * 1024 * 1024
TALL = PART + 16
FFN_ROWS = 2 * PART + POOL_PART
WIDE = 1024

QB, VB, OB, G0, G1, S0, S1, FB, PB, CW = 0, 1, 2, 3, 4, 5, 6, 11, 12, 13


def dot(left, right, dims):
    return lax.dot_general(left, right, ((dims[:1], dims[1:]), ((), ())), preferred_element_type=F32)


def nn(left, right):
    return dot(left, right, (1, 0))


def nt(left, right):
    return dot(left, right, (1, 1))


def tn(left, right):
    return dot(left, right, (0, 0))


def normalise(resid):
    centred = resid - jnp.mean(resid, -1, keepdims=True)
    rstd = lax.rsqrt(jnp.mean(centred * centred, -1, keepdims=True) + EPS)
    return centred * rstd, rstd


def norm_back(incoming, normed, rstd, gain):
    scaled = incoming * gain
    back = rstd * (
        scaled
        - jnp.mean(scaled, -1, keepdims=True)
        - normed * jnp.mean(scaled * normed, -1, keepdims=True)
    )
    gain_grad = jnp.sum(incoming * normed, 0, keepdims=True)
    shift_grad = jnp.sum(incoming, 0, keepdims=True)
    return back, gain_grad, shift_grad


def cost(micros):
    return pl.CostEstimate(flops=int(micros * 1e10), bytes_accessed=0, transcendentals=0)


def shard_index():
    return lax.axis_index("head")


def quarter_index():
    return lax.axis_index("dp") & 3


def rows_at(index, count):
    return pl.ds(pl.multiple_of(index * count, count), count)


def vmem():
    return pl.BlockSpec(memory_space=pltpu.VMEM)


def anywhere():
    return pl.BlockSpec(memory_space=pl.ANY)


class Line:
    def __init__(self):
        self.waits = ()

    def call(self, name, micros, kernel, ins, outs, scratch=(), aliases=None, after=()):
        waits = tuple(self.waits) + tuple(after)
        count = len(ins)

        def body(*refs):
            kernel(*refs[:count], *refs[count + len(waits) :])

        result = pl.pallas_call(
            body,
            out_shape=tuple(jax.ShapeDtypeStruct(shape, dtype) for shape, dtype, _ in outs),
            in_specs=[spec for _, spec in ins] + [anywhere()] * len(waits),
            out_specs=tuple(spec for _, _, spec in outs),
            scratch_shapes=list(scratch),
            input_output_aliases=aliases or {},
            compiler_params=pltpu.CompilerParams(vmem_limit_bytes=VMEM_LIMIT),
            cost_estimate=cost(micros),
            name=name,
        )(*[value for value, _ in ins], *waits)
        self.waits = (result[0],)
        return result


    def gate(self, *values):
        count = len(values)

        def body(*refs):
            pass

        result = pl.pallas_call(
            body,
            out_shape=tuple(jax.ShapeDtypeStruct(value.shape, value.dtype) for value in values),
            in_specs=[anywhere()] * (count + len(self.waits)),
            out_specs=(anywhere(),) * count,
            input_output_aliases={index: index for index in range(count)},
            cost_estimate=cost(0.1),
            name="gate",
        )(*values, *self.waits)
        self.waits = (result[0],)
        return result


def near(*values):
    return [(value, vmem()) for value in values]


def away(*values):
    return [(value, anywhere()) for value in values]


def made(*shapes):
    return [(shape, dtype, vmem()) for shape, dtype in shapes]


def sent(*shapes):
    return [(shape, dtype, anywhere()) for shape, dtype in shapes]


def run_copies(pairs, sems, start):
    copies = [
        pltpu.make_async_copy(src, dst, sems.at[start + index])
        for index, (src, dst) in enumerate(pairs)
    ]
    for item in copies:
        item.start()
    return copies


def wait_copies(copies):
    for item in copies:
        item.wait()


def flip(mesh, axis, bit):
    dp, head = mesh.shape["dp"], mesh.shape["head"]
    pairs = []
    for place in range(dp):
        for shard in range(head):
            to_place = place ^ bit if axis == "dp" else place
            to_shard = shard ^ bit if axis == "head" else shard
            pairs.append((place * head + shard, to_place * head + to_shard))
    return pairs


DIMS = {"c": ("head", 1), "y": ("head", 2), "d": ("head", 3), "x": ("dp", 1), "a": ("dp", 2), "b": ("dp", 4)}


class Moves:
    def __init__(self, mesh):
        self.mesh = mesh

    def __call__(self, dim, value):
        return lax.ppermute(value, AXES, flip(self.mesh, *DIMS[dim]))

    def more(self):
        bit = 8
        while bit < self.mesh.shape["dp"]:
            yield bit
            bit *= 2

    def place(self, bit, value):
        return lax.ppermute(value, AXES, flip(self.mesh, "dp", bit))


def stack_kernel(one, two, three, follow_in, stack_ref, follow_ref, sems):
    pairs = [(ref, stack_ref.at[index]) for index, ref in enumerate((one, two, three))]
    wait_copies(run_copies(pairs, sems, 0))


class Spread:
    def __init__(self, line, moves, quarter, last):
        self.line, self.moves, self.last = line, moves, last
        self.far = [moves("y", quarter)]

    def second(self):
        self.far = list(self.line.gate(*self.far))
        self.far += [self.moves("x", self.far[0]), self.moves("a", self.far[0])]

    def third(self):
        follow = 2 if self.last == "x" else 1
        shape = self.far[0].shape
        count = len(self.line.waits)
        stack, self.far[follow] = pl.pallas_call(
            lambda *refs: stack_kernel(*refs[:4], *refs[4 + count :]),
            out_shape=(
                jax.ShapeDtypeStruct((3, *shape), BF16),
                jax.ShapeDtypeStruct(shape, BF16),
            ),
            in_specs=[anywhere()] * (4 + count),
            out_specs=(vmem(), anywhere()),
            scratch_shapes=[pltpu.SemaphoreType.DMA((3,))],
            input_output_aliases={3: 1},
            cost_estimate=cost(0.1),
            name="stack",
        )(*self.far, self.far[follow], *self.line.waits)
        self.line.waits = (stack,)
        self.stack = self.moves("c", stack)
        self.far.append(self.moves(self.last, self.far[follow]))

    def fourth(self):
        self.far[3] = self.line.gate(self.far[3])[0]
        self.near = self.moves("c", self.far[3])

    def pieces(self):
        return [*self.far, self.stack, self.near]


def pack_attn_kernel(layer, qkv_ref, out_ref, own_ref, sems):
    pairs = [(qkv_ref.at[layer], own_ref.at[0:3]), (out_ref.at[layer], own_ref.at[3])]
    wait_copies(run_copies(pairs, sems, 0))


def pack_attn(line, layer, qkv, out):
    return line.call(
        "pack_attn%d" % layer,
        2,
        functools.partial(pack_attn_kernel, layer),
        away(qkv, out),
        made(((4, PART, D), BF16)),
        [pltpu.SemaphoreType.DMA((2,))],
    )[0]


def pack_ffn_kernel(in_ref, down_ref, pool_ref, own_ref, quarter_ref):
    for index in range(4):
        own_ref[index, 0:PART] = in_ref[:, index * D : (index + 1) * D]
        own_ref[index, PART : 2 * PART] = down_ref[index * PART : (index + 1) * PART]
        own_ref[index, 2 * PART : FFN_ROWS] = pool_ref[
            index * POOL_PART : (index + 1) * POOL_PART
        ]
    quarter_ref[...] = own_ref[quarter_index()]


def pack_ffn(line, layer, ffn_in, ffn_out, pool):
    shapes = ((PART, FF), (D, D), (PART, D))
    count = len(line.waits)
    result = pl.pallas_call(
        lambda *refs: pack_ffn_kernel(*refs[:3], *refs[3 + count :]),
        grid=(1,),
        out_shape=(
            jax.ShapeDtypeStruct((4, FFN_ROWS, D), BF16),
            jax.ShapeDtypeStruct((FFN_ROWS, D), BF16),
        ),
        in_specs=[
            pl.BlockSpec((None, *shape), lambda step: (layer, 0, 0)) for shape in shapes
        ]
        + [anywhere()] * count,
        out_specs=(
            pl.BlockSpec((4, FFN_ROWS, D), lambda step: (0, 0, 0)),
            pl.BlockSpec((FFN_ROWS, D), lambda step: (0, 0)),
        ),
        compiler_params=pltpu.CompilerParams(vmem_limit_bytes=VMEM_LIMIT),
        cost_estimate=cost(3),
        name="pack_ffn%d" % layer,
    )(ffn_in, ffn_out, pool, *line.waits)
    line.waits = (result[1],)
    return result


def pack_small_kernel(
    qkv_bias, out_bias, gain, shift, in_bias, down_bias, pool_bias, class_weight, packed_ref
):
    for layer in range(LAYERS):
        packed_ref[layer, QB : VB + 1] = qkv_bias[layer].astype(F32)
        packed_ref[layer, OB : OB + 1] = out_bias[layer : layer + 1].astype(F32)
        packed_ref[layer, G0 : G1 + 1] = gain[layer].astype(F32)
        packed_ref[layer, S0 : S1 + 1] = shift[layer].astype(F32)
        for index in range(4):
            value = in_bias[layer : layer + 1, index * PART : (index + 1) * PART]
            packed_ref[layer, 7 + index : 8 + index] = value.astype(F32)
        packed_ref[layer, FB : FB + 1] = down_bias[layer : layer + 1].astype(F32)
        packed_ref[layer, PB : PB + 1] = pool_bias[layer : layer + 1].astype(F32)
        for cls in range(CLASSES):
            value = class_weight[cls, layer : layer + 1].astype(F32)
            packed_ref[layer, CW + cls : CW + cls + 1] = value


def arrange_kernel(own, core, row, both, shards_ref, small_ref, bias_ref):
    shard = shard_index()
    for slot, ref in enumerate((own, core, row, both)):
        shards_ref[shard ^ slot] = ref[...]
    for part in range(SHARDS):
        for layer in range(LAYERS):
            lanes = slice(part * PART, (part + 1) * PART)
            small_ref[layer, :, lanes] = shards_ref[part, layer]
            for index in range(4):
                target = slice(index * PART, (index + 1) * PART)
                value = shards_ref[part, layer, 7 + index : 8 + index]
                bias_ref[layer, part : part + 1, target] = value


def arrange(line, moves, packed):
    core, row = moves("c", packed), moves("y", packed)
    return line.call(
        "arrange",
        1,
        arrange_kernel,
        near(packed, core, row, moves("d", packed)),
        made(
            ((SHARDS, LAYERS, 16, PART), F32),
            ((LAYERS, 16, D), F32),
            ((LAYERS, SHARDS, D), F32),
        ),
    )


def load_attn_weights(refs, slots, sems, start=0):
    here = quarter_index()
    copies = []
    for slot in range(2):
        if len(refs) == 2:
            pairs = [(refs[slot], slots.at[slot])]
        else:
            pieces = refs[0:4] if slot == 0 else [refs[4].at[0], refs[4].at[1], refs[4].at[2], refs[5]]
            pairs = [(piece, slots.at[slot, here ^ index]) for index, piece in enumerate(pieces)]
        copies.append(run_copies(pairs, sems, start + len(pairs) * slot))
    return copies


def attn_forward_kernel(layer, half, x_ref, *refs):
    if half:
        (shard_small, small, total_in), refs = refs[:3], refs[3:]
        count = 2
        weights, refs = refs[:count], refs[count:]
        qkv_ref, probs_ref, context_ref, normed_ref, rstd_ref, low_ref, slots, sems = refs
    else:
        shard_small, weights, refs = refs[0], refs[1:3], refs[3:]
        qkv_ref, probs_ref, context_ref, total_ref, slots, sems = refs
    copies = load_attn_weights(weights, slots, sems)
    shard = shard_index()
    x = x_ref[...]
    if half:
        total = total_in[...] + small[layer, OB : OB + 1].astype(F32)
    else:
        total = x.astype(F32)
    for slot in range(2):
        wait_copies(copies[slot])
        biases = shard_small[shard ^ (2 * half + slot), layer]
        parts = []
        for part in range(3):
            value = nt(x, slots[slot, part])
            if part != 1:
                row = QB if part == 0 else VB
                value = value + biases[row : row + 1].astype(F32)
            value = value.astype(BF16)
            qkv_ref[slot, part] = value
            parts.append(value)
        query, key, val = parts
        places = [
            (
                slice(seq * SEQ, (seq + 1) * SEQ),
                slice(head * HEAD_DIM, (head + 1) * HEAD_DIM),
            )
            for seq in range(2)
            for head in range(PART // HEAD_DIM)
        ]
        scores = jnp.stack([nt(query[at], key[at]) for at in places]) * HEAD_DIM ** (-0.5)
        shifted = jnp.exp(scores - jnp.max(scores, -1, keepdims=True))
        probs = shifted * (1.0 / jnp.sum(shifted, -1, keepdims=True))
        probs_ref[slot] = probs
        low = probs.astype(BF16)
        heads = [nn(low[index], val[at]) for index, at in enumerate(places)]
        half_heads = len(heads) // 2
        context = jnp.concatenate(
            [
                jnp.concatenate(heads[:half_heads], -1),
                jnp.concatenate(heads[half_heads:], -1),
            ],
            0,
        ).astype(BF16)
        context_ref[slot] = context
        total = total + nn(context, slots[slot, 3])
    if half == 0:
        total_ref[...] = total
        return
    normed, rstd = normalise(total)
    normed_ref[...] = normed
    rstd_ref[...] = rstd
    middle = normed * small[layer, G0 : G0 + 1].astype(F32) + small[layer, S0 : S0 + 1].astype(F32)
    low_ref[...] = middle.astype(BF16)


def attn_forward(line, layer, half, x, inputs, weights):
    tokens = x.shape[0]
    outs = [
        ((2, 3, tokens, PART), BF16),
        ((2, 6, SEQ, SEQ), F32),
        ((2, tokens, PART), BF16),
        ((tokens, D), F32),
    ]
    if half:
        outs += [((tokens, 1), F32), ((tokens, D), BF16)]
    return line.call(
        "attn_forward%d%d" % (layer, half),
        7,
        functools.partial(attn_forward_kernel, layer, half),
        near(x, *inputs) + away(*weights),
        made(*outs),
        [pltpu.VMEM((2, 4, PART, D), BF16), pltpu.SemaphoreType.DMA((8,))],
    )


def load_ffn_weights(refs, up, down, pool, sems, down_first=False):
    here = quarter_index()
    shard = shard_index()
    ups, downs, pools = [], [], []

    def block_of(source, owner, block):
        ups.append((source.at[0:PART], up.at[block, rows_at(owner, PART)]))
        downs.append((source.at[PART : 2 * PART], down.at[owner, rows_at(block, PART)]))
        if pool is not None:
            target = pool.at[rows_at(owner * 4 + block, POOL_PART)]
            pools.append((source.at[2 * PART : FFN_ROWS], target))

    wholes = refs if len(refs) == 4 else refs[:2]
    for slot, whole in enumerate(wholes):
        for block in range(4):
            block_of(whole.at[block], shard ^ slot, block)
    if len(refs) == 8:
        pieces = [*refs[2:6], refs[6].at[0], refs[6].at[1], refs[6].at[2], refs[7]]
        for index, piece in enumerate(pieces):
            block_of(piece, shard ^ (2 + index // 4), here ^ (index % 4))
    order = (downs, ups, pools) if down_first else (ups, downs, pools)
    first = run_copies(order[0], sems, 0)
    second = run_copies(order[1], sems, len(ups))
    return first, second, run_copies(pools, sems, 2 * len(ups))


def ffn_forward_kernel(
    layer, labels_ref, class_bias_ref, x_ref, normed_ref, low_ref, small, in_bias, *refs
):
    count = 8
    weights, refs = refs[:count], refs[count:]
    if layer:
        (prior_out, prior_logits, prior_ramp), refs = refs[:3], refs[3:]
    act_ref, act_send_ref, slope_ref, normed_two_ref, rstd_two_ref, first_grad_ref = refs[:6]
    out_ref, logits_ref, ramp_ref, up, down, pool, acts, lows, slopes, sems, out_sems = refs[6:]
    ups, downs, pools = load_ffn_weights(weights, up, down, pool, sems)
    leaving = run_copies([(x_ref, act_send_ref.at[2, :, 0:D])], out_sems, 0)
    normed = normed_ref[...]
    low = low_ref[...]

    def row(index):
        return small[layer, index : index + 1].astype(F32)

    total = normed * row(G0) + row(S0) + row(FB)
    for part in range(4):
        lows[part, :, 0:PART] = low[:, part * PART : (part + 1) * PART]
        lows[part, :, PART:] = jnp.zeros((low.shape[0], WIDE - D - PART), BF16)
    wait_copies(ups)
    for block in range(4):
        pre_act = nn(low, up[block]) + in_bias[layer, block : block + 1].astype(F32)
        cumulative = 0.5 * (1.0 + lax.erf(pre_act * ROOT_HALF))
        act = (pre_act * cumulative).astype(BF16)
        density = jnp.exp(-0.5 * pre_act * pre_act) * DENSITY_SCALE
        acts[block] = act
        slopes[block] = cumulative + pre_act * density
        leaving += run_copies([(slopes.at[block], slope_ref.at[block])], out_sems, 1 + block)
        if block == 0:
            wait_copies(downs)
        total = total + nn(act, down[block])
    shard = shard_index()
    pairs = []
    for slot in range(4):
        target = (act_send_ref if slot & 1 else act_ref).at[slot >> 1]
        pairs.append((acts.at[shard ^ slot], target.at[:, 0:D]))
        pairs.append((lows.at[shard ^ slot], target.at[:, D:WIDE]))
    leaving += run_copies(pairs, out_sems, 5)
    wait_copies(pools)
    normed_two, rstd_two = normalise(total)
    normed_two_ref[...] = normed_two
    rstd_two_ref[...] = rstd_two
    output = (normed_two * row(G1) + row(S1)).astype(BF16)

    first = jnp.concatenate([output[0:1], output[SEQ : SEQ + 1]], 0).astype(F32)
    first = jnp.concatenate([first, jnp.zeros((14, D), F32)], 0).astype(BF16)
    pool_weight = pool[...]
    pooled = jnp.tanh(nn(first, pool_weight) + row(PB))
    wide = pooled.astype(BF16).astype(F32)
    lanes = lax.broadcasted_iota(jnp.int32, (16, 128), 1)
    rows = lax.broadcasted_iota(jnp.int32, (16, 128), 0)
    logits = jnp.zeros((16, 128), F32)
    for cls in range(CLASSES):
        value = jnp.sum(wide * row(CW + cls), -1, keepdims=True)
        value = value + class_bias_ref[layer, cls]
        logits = jnp.where(lanes == cls, value, logits)
    valid = lanes < CLASSES
    peak = jnp.max(jnp.where(valid, logits, -jnp.inf), -1, keepdims=True)
    shifted = jnp.where(valid, jnp.exp(logits - peak), 0.0)
    soft = shifted / jnp.sum(shifted, -1, keepdims=True)
    label = jnp.where(rows == 0, labels_ref[0], labels_ref[1])
    logit_grad = (soft - (lanes == label).astype(F32)).astype(BF16)
    logit_wide = logit_grad.astype(F32)
    back = jnp.zeros((16, D), F32)
    for cls in range(CLASSES):
        picked = jnp.sum(jnp.where(lanes == cls, logit_wide, 0.0), -1, keepdims=True)
        back = back + picked * row(CW + cls)
    pool_grad = (back * (1.0 - pooled * pooled)).astype(BF16)
    first_grad_ref[...] = nt(pool_grad, pool_weight)[0:8]
    padded = jnp.concatenate([logit_wide[0:2], jnp.zeros((2, D - 128), F32)], -1)
    ramp = jnp.concatenate(
        [first.astype(F32)[0:2], pool_grad.astype(F32)[0:2], wide[0:2], padded], 0
    ).astype(BF16)
    if layer:
        out_ref[0] = prior_out[...]
        logits_ref[0] = prior_logits[...]
        ramp_ref[0] = prior_ramp[...]
        out_ref[1] = output
        logits_ref[1] = logits[0:8]
        ramp_ref[1] = ramp
    else:
        out_ref[...] = output
        logits_ref[...] = logits[0:8]
        ramp_ref[...] = ramp
    wait_copies(leaving)


def ffn_forward(line, layer, labels, class_bias, x, normed, low, small, in_bias, weights, prior):
    tokens = low.shape[0]
    smem = pl.BlockSpec(memory_space=pltpu.SMEM)
    stack = (2,) if layer else ()
    return line.call(
        "ffn_forward%d" % layer,
        12,
        functools.partial(ffn_forward_kernel, layer),
        [(labels, smem), (class_bias, smem)]
        + near(x, normed, low, small, in_bias)
        + away(*weights)
        + near(*prior),
        sent(
            ((2, tokens, WIDE), BF16),
            ((3, tokens, WIDE), BF16),
            ((4, tokens, D), F32),
        )
        + made(
            ((tokens, D), F32),
            ((tokens, 1), F32),
            ((8, D), F32),
            ((*stack, tokens, D), BF16),
            ((*stack, 8, 128), F32),
            ((*stack, 8, D), BF16),
        ),
        [
            pltpu.VMEM((4, D, D), BF16),
            pltpu.VMEM((SHARDS, D, D), BF16),
            pltpu.VMEM((D, D), BF16),
            pltpu.VMEM((4, tokens, D), BF16),
            pltpu.VMEM((4, tokens, WIDE - D), BF16),
            pltpu.VMEM((4, tokens, D), F32),
            pltpu.SemaphoreType.DMA((48,)),
            pltpu.SemaphoreType.DMA((13,)),
        ],
    )


def ffn_backward_kernel(
    layer, grad_ref, first_ref, normed_two_ref, rstd_two_ref, slope_ref, normed_ref, rstd_ref,
    small, *refs
):
    pairs_ref, rows_ref, low_ref, smalls_ref, up, down, pairs, sems, out_sems = refs[-9:]
    downs, ups, _ = load_ffn_weights(refs[:-9], up, down, None, sems, True)

    def row(index):
        return small[layer, index : index + 1].astype(F32)

    grad = grad_ref[...].astype(F32)
    index = lax.broadcasted_iota(jnp.int32, grad.shape, 0)
    grad = grad + jnp.where(index == 0, first_ref[0:1], 0.0)
    grad = grad + jnp.where(index == SEQ, first_ref[1:2], 0.0)
    res_two, gain_two, shift_two = norm_back(grad, normed_two_ref[...], rstd_two_ref[...], row(G1))
    ffn_grad = res_two.astype(BF16)
    pairs[4] = ffn_grad
    leaving = run_copies([(pairs.at[4], pairs_ref.at[4])], out_sems, 4)
    wait_copies(downs)
    middle_grad = res_two
    for block in range(4):
        act_grad = nt(ffn_grad, down[block])
        pre_grad = (act_grad * slope_ref[block]).astype(BF16)
        pairs[block] = pre_grad
        leaving += run_copies([(pairs.at[block], pairs_ref.at[block])], out_sems, block)
        if block == 0:
            wait_copies(ups)
        smalls_ref[block : block + 1] = jnp.sum(pre_grad.astype(F32), 0, keepdims=True)
        middle_grad = middle_grad + nt(pre_grad, up[block])
    res_one, gain_one, shift_one = norm_back(middle_grad, normed_ref[...], rstd_ref[...], row(G0))
    rows_ref[...] = res_one
    low = res_one.astype(BF16)
    low_ref[...] = low
    smalls_ref[4:5] = jnp.sum(ffn_grad.astype(F32), 0, keepdims=True)
    smalls_ref[5:6] = jnp.sum(low.astype(F32), 0, keepdims=True)
    smalls_ref[6:7] = gain_one
    smalls_ref[7:8] = gain_two
    smalls_ref[8:9] = shift_one
    smalls_ref[9:10] = shift_two
    wait_copies(leaving)


def ffn_backward(
    line, layer, grad, first_grad, normed_two, rstd_two, slope, normed, rstd, small, weights
):
    tokens = grad.shape[0]
    return line.call(
        "ffn_backward%d" % layer,
        11,
        functools.partial(ffn_backward_kernel, layer),
        near(grad, first_grad, normed_two, rstd_two, slope, normed, rstd, small)
        + away(*weights),
        sent(((5, tokens, D), BF16))
        + made(
            ((tokens, D), F32),
            ((tokens, D), BF16),
            ((10, D), F32),
        ),
        [
            pltpu.VMEM((4, D, D), BF16),
            pltpu.VMEM((SHARDS, D, D), BF16),
            pltpu.VMEM((5, tokens, D), BF16),
            pltpu.SemaphoreType.DMA((32,)),
            pltpu.SemaphoreType.DMA((5,)),
        ],
    )


def place_pieces(groups, natural, outs, y, sems):
    here = quarter_index()
    pairs = []
    for index, (order, first, count) in enumerate(groups):
        keep_ref, send_ref = outs[2 * index : 2 * index + 2]
        rows = slice(first, first + count)
        for x in range(2):
            for a in range(2):
                if not order:
                    target, unit, place = (send_ref if y else keep_ref), 2 * a + x, 2 * a + x
                else:
                    bits = {"y": y, "x": x, "a": a}
                    outer, middle, inner = (bits[dim] for dim in order)
                    target = send_ref if outer else keep_ref
                    unit, place = (2 * a + x) ^ here, 2 * middle + inner
                pairs.append((natural.at[y, unit, rows], target.at[place]))
    return run_copies(pairs, sems, y * len(pairs))


def piece_shapes(groups):
    shapes = []
    for _, _, count in groups:
        shapes += [((4, count, D), BF16)] * 2
    return shapes


def ffn_weights_kernel(groups, act_ref, act_near_ref, pairs_ref, pairs_near_ref, *refs):
    outs, (natural, sems) = refs[:-2], refs[-2:]
    leaving = []
    for slot in (1, 0):
        mine, other = act_ref[slot], act_near_ref[slot]
        down = tn(mine[:, 0:D], pairs_ref[4]) + tn(other[:, 0:D], pairs_near_ref[4])
        down = down.astype(BF16)
        for block in range(4):
            natural[slot, block, PART : 2 * PART] = down[block * PART : (block + 1) * PART]
            up = tn(mine[:, D : D + PART], pairs_ref[block])
            up = up + tn(other[:, D : D + PART], pairs_near_ref[block])
            natural[slot, block, 0:PART] = up.astype(BF16)
        leaving += place_pieces(groups, natural, outs, slot, sems)
    wait_copies(leaving)


def ffn_weight_grads(line, layer, groups, act, act_near, pairs, pairs_near):
    return line.call(
        "ffn_weight_grads%d" % layer,
        8,
        functools.partial(ffn_weights_kernel, groups),
        near(act, act_near, pairs, pairs_near),
        sent(*piece_shapes(groups)),
        [pltpu.VMEM((2, 4, 2 * PART, D), BF16), pltpu.SemaphoreType.DMA((8 * len(groups),))],
    )


def attn_weights_kernel(
    groups, x_ref, acts_near_ref, grad_ref, pairs_ref, near_ref, *refs
):
    outs, (natural, sems) = refs[-2 - 2 * len(groups) : -2], refs[-2:]
    leaving = []
    cut = 3 * PART
    tokens = x_ref.shape[0]
    x_near = acts_near_ref[2, :, 0:D]
    grad_near = near_ref[2 * tokens : 3 * tokens]
    if len(refs) > 2 + 2 * len(groups):
        smalls_ref, by_shard = refs[0], refs[-3]
        outs = refs[1:-3]
        smalls = []
        for layer in range(LAYERS):
            start = 3 * tokens + 32 * layer
            high = near_ref[start : start + 16].astype(F32)
            rest = near_ref[start + 16 : start + 32].astype(F32)
            smalls.append(smalls_ref[layer] + (high + rest)[0:12])
        for part in range(SHARDS):
            lanes = slice(part * PART, (part + 1) * PART)
            for layer in range(LAYERS):
                row = 3 * layer
                by_shard[part, row : row + 1] = smalls[layer][part : part + 1]
                for item in range(8):
                    target = slice((item % 4) * PART, (item % 4 + 1) * PART)
                    value = smalls[layer][4 + item : 5 + item, lanes]
                    by_shard[part, row + 1 + item // 4 : row + 2 + item // 4, target] = value
            by_shard[part, 6:16] = jnp.zeros((10, D), F32)
        shard = shard_index()
        for slot in range(2):
            natural[slot, 0, PART:TALL] = by_shard[shard ^ (2 * slot)].astype(BF16)
            for unit in range(1, 4):
                natural[slot, unit, PART:TALL] = jnp.zeros((TALL - PART, D), BF16)
    for slot in (1, 0):
        mine, other = pairs_ref[slot], near_ref[slot * tokens : (slot + 1) * tokens]
        value = tn(mine[:, 0:cut], x_ref[...]) + tn(other[:, 0:cut], x_near)
        value = value.astype(BF16)
        for unit in range(3):
            natural[slot, unit, 0:PART] = value[unit * PART : (unit + 1) * PART]
        value = tn(mine[:, cut:D], grad_ref[...]) + tn(other[:, cut:D], grad_near)
        natural[slot, 3, 0:PART] = value.astype(BF16)
        leaving += place_pieces(groups, natural, outs, slot, sems)
    wait_copies(leaving)


def attn_weight_grads(line, layer, groups, *operands):
    return line.call(
        "attn_weight_grads%d" % layer,
        5,
        functools.partial(attn_weights_kernel, groups),
        near(*operands),
        sent(*piece_shapes(groups)),
        ([pltpu.VMEM((SHARDS, 16, D), F32)] if len(operands) > 5 else [])
        + [
            pltpu.VMEM((2, 4, groups[0][2], D), BF16),
            pltpu.SemaphoreType.DMA((8 * len(groups),)),
        ],
    )


def attn_backward_kernel(
    layer, res_ref, grad_ref, smalls_in_ref, *refs
):
    count = 10
    kept, weights, refs = refs[:6], refs[6:count], refs[count:]
    if layer == 0:
        prior, refs = refs[0], refs[1:]
    pairs_ref, pairs_send_ref, rows_ref, smalls_ref, slots, sems, sums = refs
    tokens = grad_ref.shape[0]
    copies = load_attn_weights(weights[:2], slots.at[0:2], sems)
    copies += load_attn_weights(weights[2:], slots.at[2:4], sems, 2)
    shard = shard_index()
    grad = grad_ref[...]
    total = res_ref[...]
    for slot in range(4):
        wait_copies(copies[slot])
        half, index = slot >> 1, slot & 1
        qkv_ref, probs_ref, context_ref = kept[3 * half : 3 * half + 3]
        context_grad = nt(grad, slots[slot, 3]).astype(BF16)
        places = [
            (
                slice(seq * SEQ, (seq + 1) * SEQ),
                slice(head * HEAD_DIM, (head + 1) * HEAD_DIM),
            )
            for seq in range(2)
            for head in range(PART // HEAD_DIM)
        ]
        query, key, val = (qkv_ref[index, part] for part in range(3))
        probs = probs_ref[index]
        prob_grad = jnp.stack([nt(context_grad[at], val[at]) for at in places])
        mean = jnp.sum(prob_grad * probs, -1, keepdims=True)
        score_grad = (probs * (prob_grad - mean)).astype(BF16)
        probs_low = probs.astype(BF16)
        scale = HEAD_DIM ** (-0.5)
        heads = [
            [nn(score_grad[i], key[at]) * scale for i, at in enumerate(places)],
            [tn(score_grad[i], query[at]) * scale for i, at in enumerate(places)],
            [tn(probs_low[i], context_grad[at]) for i, at in enumerate(places)],
        ]
        half_heads = len(places) // 2
        seq_rows = [
            [jnp.concatenate(group[:half_heads], -1), jnp.concatenate(group[half_heads:], -1)]
            for group in heads
        ]
        for part in range(3):
            value = jnp.concatenate(seq_rows[part], 0).astype(BF16)
            if slot & 1:
                rows = slice(half * tokens, (half + 1) * tokens)
                pairs_send_ref[rows, part * PART : (part + 1) * PART] = value
            else:
                pairs_ref[half, :, part * PART : (part + 1) * PART] = value
            if part != 1:
                sums[shard ^ slot, part // 2] = jnp.sum(value.astype(F32), 0, keepdims=True)
            total = total + nn(value, slots[slot, part])
        if slot & 1:
            pairs_send_ref[half * tokens : (half + 1) * tokens, 3 * PART : D] = context_ref[index]
        else:
            pairs_ref[half, :, 3 * PART : D] = context_ref[index]
    pairs_send_ref[2 * tokens : 3 * tokens] = grad
    rows_ref[...] = total.astype(rows_ref.dtype)
    own = [
        jnp.concatenate([sums[part, index] for part in range(SHARDS)], -1) for index in range(2)
    ]
    if layer:
        smalls_ref[0:10] = smalls_in_ref[...]
        smalls_ref[10:11] = own[0]
        smalls_ref[11:12] = own[1]
    else:
        smalls_ref[1] = prior[...]
        smalls_ref[0, 0:10] = smalls_in_ref[...]
        smalls_ref[0, 10:11] = own[0]
        smalls_ref[0, 11:12] = own[1]
        for index in range(LAYERS):
            value = smalls_ref[index]
            high = value.astype(BF16)
            rest = (value - high.astype(F32)).astype(BF16)
            start = 3 * tokens + 32 * index
            pairs_send_ref[start : start + 16] = jnp.concatenate(
                [high, jnp.zeros((4, D), BF16)], 0
            )
            pairs_send_ref[start + 16 : start + 32] = jnp.concatenate(
                [rest, jnp.zeros((4, D), BF16)], 0
            )


def attn_backward(line, layer, res, grad, kept, smalls, weights, prior):
    tokens = grad.shape[0]
    return line.call(
        "attn_backward%d" % layer,
        15,
        functools.partial(attn_backward_kernel, layer),
        near(res, grad, smalls, *kept) + away(*weights) + near(*prior),
        made(
            ((2, tokens, D), BF16),
            ((3 * tokens + (0 if layer else 64), D), BF16),
            ((tokens, D), F32 if layer else BF16),
            ((12, D) if layer else (2, 12, D), F32),
        ),
        [
            pltpu.VMEM((4, 4, PART, D), BF16),
            pltpu.SemaphoreType.DMA((12,)),
            pltpu.VMEM((SHARDS, 2, 1, PART), F32),
        ],
    )


def halve_kernel(keep_ref, came_ref, low_ref, high_ref):
    half = low_ref.shape[0]
    low_ref[...] = keep_ref[0:half] + came_ref[0:half]
    high_ref[...] = keep_ref[half:] + came_ref[half:]


def add_kernel(keep_ref, came_ref, sum_ref):
    sum_ref[...] = keep_ref[...] + came_ref[...]


def reduction(line, moves, name, order, back, keep, send):
    shape = keep.shape
    micros = 1 + shape[1] / 192
    if not order:
        came = moves("y", send)
        yield
        total = line.call(
            "add_%s" % name, micros, add_kernel, near(keep, came), made((shape, BF16))
        )[0]
        yield (back, lax.psum(total, "dp"))
    came = moves(order[0], send)
    for step, dim in enumerate(order[1:]):
        yield
        half = (keep.shape[0] // 2, *shape[1:])
        keep, send = line.call(
            "halve_%s%d" % (name, step), micros, halve_kernel, near(keep, came),
            made((half, BF16), (half, BF16)),
        )
        came = moves(dim, send)
    yield
    keep, came = keep[0], came[0]
    total = line.call(
        "add_%s" % name, micros, add_kernel, near(keep, came), made((shape[1:], BF16))
    )[0]
    came = moves("b", total)
    for bit in moves.more():
        yield
        total = line.call(
            "more_%s%d" % (name, bit), micros, add_kernel, near(total, came),
            made((shape[1:], BF16)),
        )[0]
        came = moves.place(bit, total)
    yield
    total = line.call(
        "last_%s" % name, micros, add_kernel, near(total, came), made((shape[1:], BF16))
    )[0]
    came = moves(back[0], total)
    yield
    both = line.call(
        "both_%s" % name, micros, both_kernel, near(total, came), made(((2, *shape[1:]), BF16))
    )[0]
    yield (back, both, moves(back[1], both))


def join_kernel(one_ref, two_ref, joint_ref):
    count = one_ref.shape[0]
    joint_ref[0:count] = one_ref[...]
    joint_ref[count : 2 * count] = two_ref[...]


def join(line, one, two):
    shape = (2 * one.shape[0], *one.shape[1:])
    return line.call("join%d" % shape[0], 1, join_kernel, near(one, two), made((shape, BF16)))[0]


def both_kernel(one_ref, two_ref, both_ref):
    both_ref[0] = one_ref[...]
    both_ref[1] = two_ref[...]


def unpack_kernel(back, first, targets, prior, *refs):
    values = 2 if back else 1
    quarters = refs[:values]
    outs = refs[values + prior : -2]
    whole, sems = refs[-2:]
    here = quarter_index()
    count = whole.shape[1]
    for index in range(4):
        if not back:
            whole[index] = quarters[0][index, first : first + count].astype(F32)
            continue
        bits = {back[0]: index & 1, back[1]: index >> 1}
        relative = 2 * bits["a"] + bits["x"]
        quarter = quarters[index >> 1][index & 1, first : first + count]
        whole[relative ^ here] = quarter.astype(F32)
    if count == TALL:
        qkv_bias, out_bias, gain, shift, in_bias, down_bias = outs[len(targets) :]
        for layer in range(LAYERS):
            row = PART + 3 * layer

            def item(index):
                at = row + 1 + index // 4
                return whole[0, at : at + 1, (index % 4) * PART : (index % 4 + 1) * PART]

            in_bias[layer : layer + 1] = whole[0, row : row + 1]
            down_bias[layer : layer + 1] = item(0)
            out_bias[layer : layer + 1] = item(1)
            for index in range(2):
                gain[layer, index : index + 1] = item(2 + index)
                shift[layer, index : index + 1] = item(4 + index)
                qkv_bias[layer, index : index + 1] = item(6 + index)
    pairs = [
        (whole.at[unit, 0:PART], outs[which].at[where])
        for unit, which, where in targets_of(targets)
    ]
    wait_copies(run_copies(pairs, sems, 0))


def targets_of(targets):
    return [(unit, which, where) for which, places in enumerate(targets) for unit, where in places]


SMALL_SHAPES = (
    (LAYERS, 2, PART), (LAYERS, PART), (LAYERS, 2, PART), (LAYERS, 2, PART), (LAYERS, D), (LAYERS, PART)
)


def unpack(line, name, quarters, first, shapes, targets, prior):
    back, *values = quarters
    aliases = {len(values) + index: index for index in range(len(prior))}
    count = TALL if values[0].shape[1] == TALL else PART
    outs = [(shape, F32, anywhere()) for shape in shapes]
    if count == TALL:
        outs += made(*[(shape, F32) for shape in SMALL_SHAPES])
    return line.call(
        name,
        3,
        functools.partial(unpack_kernel, back, first, targets, len(prior)),
        near(*values) + away(*prior),
        outs,
        [pltpu.VMEM((4, count, D), F32), pltpu.SemaphoreType.DMA((4,))],
        aliases,
    )


def unpack_up(line, layer, quarters, first, prior):
    places = [(unit, (layer, slice(None), slice(unit * D, (unit + 1) * D))) for unit in range(4)]
    return unpack(
        line, "unpack_up%d" % layer, quarters, first, [(LAYERS, PART, FF)], [places], prior
    )


def unpack_down(line, layer, quarters, first, prior):
    places = [(unit, (layer, slice(unit * PART, (unit + 1) * PART))) for unit in range(4)]
    return unpack(
        line, "unpack_down%d" % layer, quarters, first, [(LAYERS, D, D)], [places], prior
    )


def unpack_attn(line, layer, quarters, first, prior):
    return unpack(
        line,
        "unpack_attn%d" % layer,
        quarters,
        first,
        [(LAYERS, 3, PART, D), (LAYERS, PART, D)],
        [[(unit, (layer, unit)) for unit in range(3)], [(3, (layer,))]],
        prior,
    )


def pool_grads(ramp, shard):
    ramp = ramp.reshape(ramp.shape[0], LAYERS, 4, 2, D)
    ramp = jnp.transpose(ramp, (1, 2, 0, 3, 4)).reshape(LAYERS, 4, -1, D)
    first, pool_grad, pooled, logit_grad = (ramp[:, part] for part in range(4))
    logit_grad = logit_grad[:, :, 0:CLASSES]
    own_first = lax.dynamic_slice_in_dim(first, shard * PART, PART, 2)
    own_pooled = lax.dynamic_slice_in_dim(pooled, shard * PART, PART, 2)
    pool_weight_grad = jnp.einsum("lnd,lne->lde", own_first, pool_grad, preferred_element_type=F32)
    class_weight_grad = jnp.einsum(
        "lnd,lnc->ldc", own_pooled, logit_grad, preferred_element_type=F32
    )
    class_bias_grad = jnp.sum(logit_grad.astype(F32), 1)
    own_pool = lax.dynamic_slice_in_dim(pool_grad, shard * PART, PART, 2)
    pool_bias_grad = jnp.sum(own_pool.astype(F32), 1)
    return pool_weight_grad, pool_bias_grad, class_weight_grad, class_bias_grad


ROUTES = {
    "f1": ("yxa", "ax"),
    "a1": ("axy", "ax"),
    "f0": ("axy", "ax"),
    "a0": ("yxa", "xa"),
}
SCHEDULE = """
F1 A1 FW1 AW1 F0 a1 A0 FW0 AW0 f1 a1 a0 f1 a1 f0 a0 f1 a1 f0 a1 f1 f0 a0 Ua1 a0 R0 R1 f1
R1 a0 f0 R1 Ua0 f0 R1 Uf1 R1 P1 Uf0
""".split()


def on_device(
    mesh,
    hidden_in,
    out_cotangent,
    labels,
    qkv_weight,
    qkv_bias,
    out_weight,
    out_bias,
    norm_gain,
    norm_shift,
    ffn_in,
    ffn_in_bias,
    ffn_out,
    ffn_out_bias,
    pool_weight,
    pool_bias,
    class_weight,
    class_bias,
):
    moves = Moves(mesh)
    line = Line()
    shard = shard_index()
    qkv_turned = jnp.swapaxes(qkv_weight, 2, 3)

    packed = line.call(
        "pack_small",
        1,
        pack_small_kernel,
        near(
            qkv_bias, out_bias, norm_gain, norm_shift, ffn_in_bias, ffn_out_bias, pool_bias,
            jnp.transpose(class_weight, (2, 0, 1)),
        ),
        made(((LAYERS, 16, PART), F32)),
    )[0]
    first_pack, ffn_quarter = pack_ffn(line, 0, ffn_in, ffn_out, pool_weight)
    ffn_far = [Spread(line, moves, ffn_quarter, "x")]
    own = pack_attn(line, 0, qkv_turned, out_weight)
    attn_own = [[own, moves("c", own)]]
    class_bias_wide = class_bias.astype(F32)
    shard_small, small, in_bias = arrange(line, moves, packed)

    far = moves("y", line.gate(attn_own[0][0])[0])

    x = hidden_in
    kept, nears = [], []
    prior = ()
    for layer in range(LAYERS):
        *attn_near, total = attn_forward(line, layer, 0, x, (shard_small,), attn_own[layer])
        if layer == 0:
            ffn_far[0].second()
            ffn_pack, ffn_quarter = pack_ffn(line, 1, ffn_in, ffn_out, pool_weight)
            ffn_far.append(Spread(line, moves, ffn_quarter, "a"))
            ffn_far[0].third()
            far, first_pack = line.gate(far, first_pack)
            ffn_own = [[first_pack, moves("c", first_pack)]]
            attn_far = [[far, moves("c", far)]]
        else:
            far, ffn_pack = line.gate(far, ffn_pack)
            ffn_own.append([ffn_pack, moves("c", ffn_pack)])
            attn_far.append([far, moves("c", far)])
        *attn_rest, normed, rstd, low = attn_forward(
            line, layer, 1, x, (shard_small, small, total), attn_far[layer]
        )
        if layer == 0:
            line.waits = (*line.waits, ffn_own[0][1], ffn_far[0].stack)
            own = pack_attn(line, 1, qkv_turned, out_weight)
            ffn_far[1].second()
            far = moves("y", line.gate(own)[0])
            ffn_far[0].fourth()
            attn_own.append([own, moves("c", own)])
            line.waits = (*line.waits, attn_own[1][1])
            ffn_weights = [ffn_own[0] + ffn_far[0].pieces()]
        else:
            line.waits = (*line.waits, nears[0])
            ffn_far[1].fourth()
            ffn_weights.append(ffn_own[1] + ffn_far[1].pieces())
        act, act_send, slope, normed_two, rstd_two, first_grad, *prior = ffn_forward(
            line, layer, labels, class_bias_wide, x, normed, low, small, in_bias,
            ffn_weights[layer], prior,
        )
        if layer == 0:
            ffn_far[1].third()
        act_near = moves("c", act_send)
        nears.append(act_near)
        kept.append(
            (
                x,
                (attn_near + attn_rest, normed, rstd),
                (act, act_near),
                (slope, normed_two, rstd_two, first_grad),
            )
        )
        x = prior[0]
    block_outputs, logits, ramp = prior

    chains, results, state = {}, {}, {"grad": out_cotangent, "prior": ()}
    ramp_value = [ramp[None]]
    ramp_steps = [("head", 1), ("head", 2)]
    bit = 1
    while bit < mesh.shape["dp"]:
        ramp_steps.append(("dp", bit))
        bit *= 2

    def begin(names, pieces):
        for index, name in enumerate(names):
            keep, send = pieces[2 * index : 2 * index + 2]
            chains[name] = reduction(line, moves, name, *ROUTES[name], keep, send)
            next(chains[name])

    def step(name):
        layer = int(name[-1])
        if name == "R0":
            ramp_value[0] = line.gate(ramp_value[0])[0]
        elif name[:-1] == "F":
            _, (_, normed, rstd), _, (slope, normed_two, rstd_two, first_grad) = kept[layer]
            pairs, res, low, rows = ffn_backward(
                line, layer, state["grad"], first_grad, normed_two, rstd_two, slope, normed, rstd,
                small, ffn_weights[layer],
            )
            state["ffn"] = (pairs, moves("c", pairs))
            state["low"] = low
            state["res"], state["rows"] = res, rows
            line.waits = (*line.waits, nears[layer])
        elif name[:-1] == "A":
            pairs, send, grad, smalls = attn_backward(
                line, layer, state["res"], state["low"], kept[layer][1][0], state["rows"],
                attn_own[layer] + attn_far[layer], state["prior"],
            )
            state["attn"] = (pairs, moves("c", send))
            state["grad"], state["prior"] = grad, (smalls,)
        elif name[:-1] == "FW":
            names = [key for key in ROUTES if key[-1] == name[-1] and key[0] != "a"]
            spans = {"f": (0, 2 * PART), "u": (0, PART), "d": (PART, PART)}
            groups = [(ROUTES[key][0], *spans[key[0]]) for key in names]
            begin(names, ffn_weight_grads(line, layer, groups, *kept[layer][2], *state["ffn"]))
        elif name[:-1] == "AW":
            key = "a" + name[-1]
            groups = [(ROUTES[key][0], 0, PART if layer else TALL)]
            operands = (kept[layer][0], kept[layer][2][1], state["low"], *state["attn"])
            if layer == 0:
                operands += state["prior"]
            begin([key], attn_weight_grads(line, layer, groups, *operands))
        elif name == "R1":
            for _ in range(max(1, len(ramp_steps) - 4)):
                axis, bit = ramp_steps.pop(0)
                came = lax.ppermute(ramp_value[0], AXES, flip(mesh, axis, bit))
                ramp_value[0] = join(line, ramp_value[0], came)
        elif name == "P1":
            state["pool"] = pool_grads(ramp_value[0], shard)
            line.waits = (*line.waits, *state["pool"])
        elif name[0] == "U":
            key = name[1:]
            while key not in results:
                results[key] = next(chains[key])
                if results[key] is None:
                    del results[key]
            if key[0] in "uf":
                state["up"] = unpack_up(line, layer, results[key], 0, state.get("up", ()))
            if key[0] in "df":
                first = PART if key[0] == "f" else 0
                state["down"] = unpack_down(line, layer, results[key], first, state.get("down", ()))
            if key[0] == "a":
                state["attn_out"] = unpack_attn(
                    line, layer, results[key], 0, state.get("attn_out", ())
                )
        else:
            result = next(chains[name], None)
            if result is not None:
                results[name] = result

    for name in SCHEDULE:
        step(name)
    qkv_grad, out_grad, qkv_bias_grad, out_bias_grad, *smalls = state["attn_out"]
    gain_grad, shift_grad, in_bias_grad, down_bias_grad = smalls
    pool_weight_grad, pool_bias_grad, class_weight_grad, class_bias_grad = state["pool"]
    return (
        block_outputs,
        logits[:, 0:2, 0:CLASSES],
        state["grad"],
        jnp.swapaxes(qkv_grad, 2, 3),
        qkv_bias_grad,
        out_grad,
        out_bias_grad,
        gain_grad,
        shift_grad,
        state["up"][0],
        in_bias_grad,
        state["down"][0],
        down_bias_grad,
        pool_weight_grad,
        pool_bias_grad,
        class_weight_grad,
        class_bias_grad,
    )


def solution(mesh):
    return jax.shard_map(
        functools.partial(on_device, mesh),
        mesh=mesh,
        in_specs=(
            P(("dp", "head"), None),
            P(("dp", "head"), None),
            P(("dp", "head")),
            P(None, None, None, "head"),
            P(None, None, "head"),
            P(None, "head", None),
            P(None, "head"),
            P(None, None, "head"),
            P(None, None, "head"),
            P(None, "head", None),
            P(None, "head"),
            P(None, "head", None),
            P(None, "head"),
            P(None, "head", None),
            P(None, "head"),
            P(None, "head", None),
            P(),
        ),
        out_specs=(
            P(None, ("dp", "head"), None),
            P(None, ("dp", "head"), None),
            P(("dp", "head"), None),
            P(None, None, None, "head"),
            P(None, None, "head"),
            P(None, "head", None),
            P(None, "head"),
            P(None, None, "head"),
            P(None, None, "head"),
            P(None, "head", None),
            P(None, "head"),
            P(None, "head", None),
            P(None, "head"),
            P(None, "head", None),
            P(None, "head"),
            P(None, "head", None),
            P(),
        ),
        check_vma=False,
    )
```

```python
import functools

import jax
import jax.numpy as jnp
from jax import lax
from jax.experimental import pallas as pl
from jax.experimental.pallas import tpu as pltpu
from jax.sharding import PartitionSpec as P

D = 768
FF = 3072
HEAD_DIM = 64
SEQ = 128
LAYERS = 2
SHARDS = 4
PART = D // SHARDS
POOL_PART = PART // 4
CLASSES = 3
EPS = 1e-12
ROOT_HALF = 0.7071067811865476
DENSITY_SCALE = 0.3989422804014327
F32 = jnp.float32
BF16 = jnp.bfloat16
AXES = ("dp", "head")
VMEM_LIMIT = 58 * 1024 * 1024
TALL = PART + 16
FFN_ROWS = 2 * PART + POOL_PART
WIDE = 1024

QB, VB, OB, G0, G1, S0, S1, FB, PB, CW = 0, 1, 2, 3, 4, 5, 6, 11, 12, 13


def dot(left, right, dims):
    return lax.dot_general(left, right, ((dims[:1], dims[1:]), ((), ())), preferred_element_type=F32)


def nn(left, right):
    return dot(left, right, (1, 0))


def nt(left, right):
    return dot(left, right, (1, 1))


def tn(left, right):
    return dot(left, right, (0, 0))


def normalise(resid):
    centred = resid - jnp.mean(resid, -1, keepdims=True)
    rstd = lax.rsqrt(jnp.mean(centred * centred, -1, keepdims=True) + EPS)
    return centred * rstd, rstd


def norm_back(incoming, normed, rstd, gain):
    scaled = incoming * gain
    back = rstd * (
        scaled
        - jnp.mean(scaled, -1, keepdims=True)
        - normed * jnp.mean(scaled * normed, -1, keepdims=True)
    )
    gain_grad = jnp.sum(incoming * normed, 0, keepdims=True)
    shift_grad = jnp.sum(incoming, 0, keepdims=True)
    return back, gain_grad, shift_grad


def cost(micros):
    return pl.CostEstimate(flops=int(micros * 1e10), bytes_accessed=0, transcendentals=0)


def shard_index():
    return lax.axis_index("head")


def quarter_index():
    return lax.axis_index("dp") & 3


def rows_at(index, count):
    return pl.ds(pl.multiple_of(index * count, count), count)


def vmem():
    return pl.BlockSpec(memory_space=pltpu.VMEM)


def anywhere():
    return pl.BlockSpec(memory_space=pl.ANY)


ROOM = {
    "pack": 14, "arrange": 4, "attn_forward": 18, "ffn_forward": 30, "ffn_backward": 32,
    "attn_backward": 24, "ffn_weight": 20, "attn_weight": 16, "halve": 14, "unpack": 14,
}


def room(name):
    for start, size in ROOM.items():
        if name.startswith(start):
            return size << 20
    return 8 << 20


TOKEN = jax.ShapeDtypeStruct((8, 128), F32)


def main_memory():
    return pl.BlockSpec(memory_space=pltpu.HBM)


class Line:
    def __init__(self):
        self.waits = ()

    def call(self, name, micros, kernel, ins, outs, scratch=(), aliases=None):
        waits = tuple(self.waits)
        count, total = len(ins), len(ins) + len(waits) + len(outs)

        def body(*refs):
            kernel(*refs[:count], *refs[count + len(waits) : total], *refs[total + 1 :])

        *result, token = pl.pallas_call(
            body,
            out_shape=[jax.ShapeDtypeStruct(shape, dtype) for shape, dtype, _ in outs] + [TOKEN],
            in_specs=[spec for _, spec in ins] + [main_memory()] * len(waits),
            out_specs=[spec for _, _, spec in outs] + [main_memory()],
            scratch_shapes=list(scratch),
            input_output_aliases=aliases or {},
            compiler_params=pltpu.CompilerParams(vmem_limit_bytes=room(name)),
            cost_estimate=cost(micros),
            name=name,
        )(*[value for value, _ in ins], *waits)
        self.waits = (token,)
        return result

    def gate(self, *values):
        outs = [(value.shape, value.dtype, anywhere()) for value in values]
        aliases = {index: index for index in range(len(values))}
        return self.call("gate", 0.1, lambda *refs: None, away(*values), outs, aliases=aliases)


def near(*values):
    return [(value, vmem()) for value in values]


def fixed(*values):
    return [(value, main_memory()) for value in values]


def away(*values):
    return [(value, anywhere()) for value in values]


def made(*shapes):
    return [(shape, dtype, vmem()) for shape, dtype in shapes]


def sent(*shapes):
    return [(shape, dtype, anywhere()) for shape, dtype in shapes]


def run_copies(pairs, sems, start):
    copies = [
        pltpu.make_async_copy(src, dst, sems.at[start + index])
        for index, (src, dst) in enumerate(pairs)
    ]
    for item in copies:
        item.start()
    return copies


def wait_copies(copies):
    for item in copies:
        item.wait()


def flip(mesh, axis, bit):
    dp, head = mesh.shape["dp"], mesh.shape["head"]
    pairs = []
    for place in range(dp):
        for shard in range(head):
            to_place = place ^ bit if axis == "dp" else place
            to_shard = shard ^ bit if axis == "head" else shard
            pairs.append((place * head + shard, to_place * head + to_shard))
    return pairs


DIMS = {"c": ("head", 1), "y": ("head", 2), "d": ("head", 3), "x": ("dp", 1), "a": ("dp", 2), "b": ("dp", 4)}


class Moves:
    def __init__(self, mesh):
        self.mesh = mesh

    def __call__(self, dim, value):
        return lax.ppermute(value, AXES, flip(self.mesh, *DIMS[dim]))

    def more(self):
        bit = 8
        while bit < self.mesh.shape["dp"]:
            yield bit
            bit *= 2

    def place(self, bit, value):
        return lax.ppermute(value, AXES, flip(self.mesh, "dp", bit))


def stack_kernel(one, two, follow, follow_out, stack_ref, sems, *, order):
    refs = {"one": one, "two": two, "follow": follow}
    pairs = [(refs[name], stack_ref.at[index]) for index, name in enumerate(order)]
    wait_copies(run_copies(pairs, sems, 0))


class Spread:
    def __init__(self, line, moves, quarter, last):
        self.line, self.moves, self.last = line, moves, last
        self.far = [moves("y", quarter)]

    def second(self):
        self.far = list(self.line.gate(*self.far))
        self.far += [self.moves("x", self.far[0]), self.moves("a", self.far[0])]

    def third(self):
        follow = 2 if self.last == "x" else 1
        shape = self.far[0].shape
        order = ("one", "two", "follow") if follow == 2 else ("one", "follow", "two")
        operands = (self.far[0], self.far[3 - follow], self.far[follow])
        self.far[follow], stack = self.line.call(
            "stack",
            3,
            functools.partial(stack_kernel, order=order),
            fixed(*operands),
            [(shape, BF16, main_memory()), ((3, *shape), BF16, vmem())],
            [pltpu.SemaphoreType.DMA((3,))],
            {2: 0},
        )
        self.stack = self.moves("c", stack)
        self.far.append(self.moves(self.last, self.far[follow]))

    def fourth(self):
        self.far[3] = self.line.gate(self.far[3])[0]
        self.near = self.moves("c", self.far[3])

    def pieces(self):
        return [*self.far, self.stack, self.near]


def pack_attn_kernel(layer, qkv_ref, out_ref, own_ref, sems):
    pairs = [(qkv_ref.at[layer], own_ref.at[0:3]), (out_ref.at[layer], own_ref.at[3])]
    wait_copies(run_copies(pairs, sems, 0))


def pack_attn(line, layer, qkv, out):
    return line.call(
        "pack_attn%d" % layer,
        2,
        functools.partial(pack_attn_kernel, layer),
        away(qkv, out),
        made(((4, PART, D), BF16)),
        [pltpu.SemaphoreType.DMA((2,))],
    )[0]


def pack_ffn_kernel(layer, in_ref, down_ref, pool_ref, own_ref, quarter_ref, sems):
    pairs = []
    for index in range(4):
        target = own_ref.at[index]
        pairs += [
            (in_ref.at[layer, :, index * D : (index + 1) * D], target.at[0:PART]),
            (
                down_ref.at[layer, index * PART : (index + 1) * PART],
                target.at[PART : 2 * PART],
            ),
            (
                pool_ref.at[layer, index * POOL_PART : (index + 1) * POOL_PART],
                target.at[2 * PART : FFN_ROWS],
            ),
        ]
    wait_copies(run_copies(pairs, sems, 0))
    quarter_ref[...] = own_ref[quarter_index()]


def pack_ffn(line, layer, ffn_in, ffn_out, pool):
    return line.call(
        "pack_ffn%d" % layer,
        3,
        functools.partial(pack_ffn_kernel, layer),
        fixed(ffn_in, ffn_out, pool),
        made(((4, FFN_ROWS, D), BF16), ((FFN_ROWS, D), BF16)),
        [pltpu.SemaphoreType.DMA((12,))],
    )


def pack_small_kernel(
    qkv_bias, out_bias, gain, shift, in_bias, down_bias, pool_bias, class_weight, packed_ref
):
    for layer in range(LAYERS):
        packed_ref[layer, QB : VB + 1] = qkv_bias[layer].astype(F32)
        packed_ref[layer, OB : OB + 1] = out_bias[layer : layer + 1].astype(F32)
        packed_ref[layer, G0 : G1 + 1] = gain[layer].astype(F32)
        packed_ref[layer, S0 : S1 + 1] = shift[layer].astype(F32)
        for index in range(4):
            value = in_bias[layer : layer + 1, index * PART : (index + 1) * PART]
            packed_ref[layer, 7 + index : 8 + index] = value.astype(F32)
        packed_ref[layer, FB : FB + 1] = down_bias[layer : layer + 1].astype(F32)
        packed_ref[layer, PB : PB + 1] = pool_bias[layer : layer + 1].astype(F32)
        for cls in range(CLASSES):
            value = class_weight[cls, layer : layer + 1].astype(F32)
            packed_ref[layer, CW + cls : CW + cls + 1] = value


def arrange_kernel(own, core, row, both, shards_ref, small_ref, bias_ref):
    shard = shard_index()
    for slot, ref in enumerate((own, core, row, both)):
        shards_ref[shard ^ slot] = ref[...]
    for part in range(SHARDS):
        for layer in range(LAYERS):
            lanes = slice(part * PART, (part + 1) * PART)
            small_ref[layer, :, lanes] = shards_ref[part, layer]
            for index in range(4):
                target = slice(index * PART, (index + 1) * PART)
                value = shards_ref[part, layer, 7 + index : 8 + index]
                bias_ref[layer, part : part + 1, target] = value


def arrange(line, moves, packed):
    core, row = moves("c", packed), moves("y", packed)
    return line.call(
        "arrange",
        1,
        arrange_kernel,
        near(packed, core, row, moves("d", packed)),
        made(
            ((SHARDS, LAYERS, 16, PART), F32),
            ((LAYERS, 16, D), F32),
            ((LAYERS, SHARDS, D), F32),
        ),
    )


def load_attn_weights(refs, slots, sems, start=0):
    here = quarter_index()
    copies = []
    for slot in range(2):
        if len(refs) == 2:
            pairs = [(refs[slot], slots.at[slot])]
        else:
            pieces = refs[0:4] if slot == 0 else [refs[4].at[0], refs[4].at[1], refs[4].at[2], refs[5]]
            pairs = [(piece, slots.at[slot, here ^ index]) for index, piece in enumerate(pieces)]
        copies.append(run_copies(pairs, sems, start + len(pairs) * slot))
    return copies


def attn_forward_kernel(layer, half, x_ref, *refs):
    if half:
        (shard_small, small, total_in), refs = refs[:3], refs[3:]
        count = 2
        weights, refs = refs[:count], refs[count:]
        qkv_ref, probs_ref, context_ref, normed_ref, rstd_ref, low_ref, slots, sems = refs
    else:
        shard_small, weights, refs = refs[0], refs[1:3], refs[3:]
        qkv_ref, probs_ref, context_ref, total_ref, slots, sems = refs
    copies = load_attn_weights(weights, slots, sems)
    shard = shard_index()
    x = x_ref[...]
    if half:
        total = total_in[...] + small[layer, OB : OB + 1].astype(F32)
    else:
        total = x.astype(F32)
    for slot in range(2):
        wait_copies(copies[slot])
        biases = shard_small[shard ^ (2 * half + slot), layer]
        parts = []
        for part in range(3):
            value = nt(x, slots[slot, part])
            if part != 1:
                row = QB if part == 0 else VB
                value = value + biases[row : row + 1].astype(F32)
            value = value.astype(BF16)
            qkv_ref[slot, part] = value
            parts.append(value)
        query, key, val = parts
        places = [
            (
                slice(seq * SEQ, (seq + 1) * SEQ),
                slice(head * HEAD_DIM, (head + 1) * HEAD_DIM),
            )
            for seq in range(2)
            for head in range(PART // HEAD_DIM)
        ]
        scores = jnp.stack([nt(query[at], key[at]) for at in places]) * HEAD_DIM ** (-0.5)
        shifted = jnp.exp(scores - jnp.max(scores, -1, keepdims=True))
        probs = shifted * (1.0 / jnp.sum(shifted, -1, keepdims=True))
        probs_ref[slot] = probs
        low = probs.astype(BF16)
        heads = [nn(low[index], val[at]) for index, at in enumerate(places)]
        half_heads = len(heads) // 2
        context = jnp.concatenate(
            [
                jnp.concatenate(heads[:half_heads], -1),
                jnp.concatenate(heads[half_heads:], -1),
            ],
            0,
        ).astype(BF16)
        context_ref[slot] = context
        total = total + nn(context, slots[slot, 3])
    if half == 0:
        total_ref[...] = total
        return
    normed, rstd = normalise(total)
    normed_ref[...] = normed
    rstd_ref[...] = rstd
    middle = normed * small[layer, G0 : G0 + 1].astype(F32) + small[layer, S0 : S0 + 1].astype(F32)
    low_ref[...] = middle.astype(BF16)


def attn_forward(line, layer, half, x, inputs, weights):
    tokens = x.shape[0]
    outs = [
        ((2, 3, tokens, PART), BF16),
        ((2, 6, SEQ, SEQ), F32),
        ((2, tokens, PART), BF16),
        ((tokens, D), F32),
    ]
    if half:
        outs += [((tokens, 1), F32), ((tokens, D), BF16)]
    return line.call(
        "attn_forward%d%d" % (layer, half),
        7,
        functools.partial(attn_forward_kernel, layer, half),
        near(x, *inputs) + fixed(*weights),
        made(*outs),
        [pltpu.VMEM((2, 4, PART, D), BF16), pltpu.SemaphoreType.DMA((8,))],
    )


def load_ffn_weights(refs, up, down, pool, sems, down_first=False):
    here = quarter_index()
    shard = shard_index()
    ups, downs, pools = [], [], []

    def block_of(source, owner, block):
        ups.append((source.at[0:PART], up.at[block, rows_at(owner, PART)]))
        downs.append((source.at[PART : 2 * PART], down.at[owner, rows_at(block, PART)]))
        if pool is not None:
            target = pool.at[rows_at(owner * 4 + block, POOL_PART)]
            pools.append((source.at[2 * PART : FFN_ROWS], target))

    wholes = refs if len(refs) == 4 else refs[:2]
    for slot, whole in enumerate(wholes):
        for block in range(4):
            block_of(whole.at[block], shard ^ slot, block)
    if len(refs) == 8:
        pieces = [*refs[2:6], refs[6].at[0], refs[6].at[1], refs[6].at[2], refs[7]]
        for index, piece in enumerate(pieces):
            block_of(piece, shard ^ (2 + index // 4), here ^ (index % 4))
    order = (downs, ups, pools) if down_first else (ups, downs, pools)
    first = run_copies(order[0], sems, 0)
    second = run_copies(order[1], sems, len(ups))
    return first, second, run_copies(pools, sems, 2 * len(ups))


def ffn_forward_kernel(
    layer, labels_ref, class_bias_ref, x_ref, normed_ref, low_ref, small, in_bias, *refs
):
    count = 8
    weights, refs = refs[:count], refs[count:]
    if layer:
        (prior_out, prior_logits, prior_ramp), refs = refs[:3], refs[3:]
    act_ref, act_send_ref, slope_ref, normed_two_ref, rstd_two_ref, first_grad_ref = refs[:6]
    out_ref, logits_ref, ramp_ref, up, down, pool, acts, lows, slopes, sems, out_sems = refs[6:]
    ups, downs, pools = load_ffn_weights(weights, up, down, pool, sems)
    leaving = run_copies([(x_ref, act_send_ref.at[2, :, 0:D])], out_sems, 0)
    normed = normed_ref[...]
    low = low_ref[...]

    def row(index):
        return small[layer, index : index + 1].astype(F32)

    total = normed * row(G0) + row(S0) + row(FB)
    for part in range(4):
        lows[part, :, 0:PART] = low[:, part * PART : (part + 1) * PART]
        lows[part, :, PART:] = jnp.zeros((low.shape[0], WIDE - D - PART), BF16)
    wait_copies(ups)
    for block in range(4):
        pre_act = nn(low, up[block]) + in_bias[layer, block : block + 1].astype(F32)
        cumulative = 0.5 * (1.0 + lax.erf(pre_act * ROOT_HALF))
        act = (pre_act * cumulative).astype(BF16)
        density = jnp.exp(-0.5 * pre_act * pre_act) * DENSITY_SCALE
        acts[block] = act
        slopes[block] = (cumulative + pre_act * density).astype(BF16)
        leaving += run_copies([(slopes.at[block], slope_ref.at[block])], out_sems, 1 + block)
        if block == 0:
            wait_copies(downs)
        total = total + nn(act, down[block])
    shard = shard_index()
    pairs = []
    for slot in range(4):
        target = (act_send_ref if slot & 1 else act_ref).at[slot >> 1]
        pairs.append((acts.at[shard ^ slot], target.at[:, 0:D]))
        pairs.append((lows.at[shard ^ slot], target.at[:, D:WIDE]))
    leaving += run_copies(pairs, out_sems, 5)
    wait_copies(pools)
    normed_two, rstd_two = normalise(total)
    normed_two_ref[...] = normed_two
    rstd_two_ref[...] = rstd_two
    output = (normed_two * row(G1) + row(S1)).astype(BF16)

    first = jnp.concatenate([output[0:1], output[SEQ : SEQ + 1]], 0).astype(F32)
    first = jnp.concatenate([first, jnp.zeros((14, D), F32)], 0).astype(BF16)
    pool_weight = pool[...]
    pooled = jnp.tanh(nn(first, pool_weight) + row(PB))
    wide = pooled.astype(BF16).astype(F32)
    lanes = lax.broadcasted_iota(jnp.int32, (16, 128), 1)
    rows = lax.broadcasted_iota(jnp.int32, (16, 128), 0)
    logits = jnp.zeros((16, 128), F32)
    for cls in range(CLASSES):
        value = jnp.sum(wide * row(CW + cls), -1, keepdims=True)
        value = value + class_bias_ref[layer, cls]
        logits = jnp.where(lanes == cls, value, logits)
    valid = lanes < CLASSES
    peak = jnp.max(jnp.where(valid, logits, -jnp.inf), -1, keepdims=True)
    shifted = jnp.where(valid, jnp.exp(logits - peak), 0.0)
    soft = shifted / jnp.sum(shifted, -1, keepdims=True)
    label = jnp.where(rows == 0, labels_ref[0], labels_ref[1])
    logit_grad = (soft - (lanes == label).astype(F32)).astype(BF16)
    logit_wide = logit_grad.astype(F32)
    back = jnp.zeros((16, D), F32)
    for cls in range(CLASSES):
        picked = jnp.sum(jnp.where(lanes == cls, logit_wide, 0.0), -1, keepdims=True)
        back = back + picked * row(CW + cls)
    pool_grad = (back * (1.0 - pooled * pooled)).astype(BF16)
    first_grad_ref[...] = nt(pool_grad, pool_weight)[0:8]
    padded = jnp.concatenate([logit_wide[0:2], jnp.zeros((2, D - 128), F32)], -1)
    ramp = jnp.concatenate(
        [first.astype(F32)[0:2], pool_grad.astype(F32)[0:2], wide[0:2], padded], 0
    ).astype(BF16)
    if layer:
        out_ref[0] = prior_out[...]
        logits_ref[0] = prior_logits[...]
        ramp_ref[0] = prior_ramp[...]
        out_ref[1] = output
        logits_ref[1] = logits[0:8]
        ramp_ref[1] = ramp
    else:
        out_ref[...] = output
        logits_ref[...] = logits[0:8]
        ramp_ref[...] = ramp
    wait_copies(leaving)


def ffn_forward(line, layer, labels, class_bias, x, normed, low, small, in_bias, weights, prior):
    tokens = low.shape[0]
    smem = pl.BlockSpec(memory_space=pltpu.SMEM)
    stack = (2,) if layer else ()
    return line.call(
        "ffn_forward%d" % layer,
        12,
        functools.partial(ffn_forward_kernel, layer),
        [(labels, smem), (class_bias, smem)]
        + near(x, normed, low, small, in_bias)
        + fixed(*weights)
        + near(*prior),
        sent(
            ((2, tokens, WIDE), BF16),
            ((3, tokens, WIDE), BF16),
            ((4, tokens, D), BF16),
        )
        + made(
            ((tokens, D), F32),
            ((tokens, 1), F32),
            ((8, D), F32),
            ((*stack, tokens, D), BF16),
            ((*stack, 8, 128), F32),
            ((*stack, 8, D), BF16),
        ),
        [
            pltpu.VMEM((4, D, D), BF16),
            pltpu.VMEM((SHARDS, D, D), BF16),
            pltpu.VMEM((D, D), BF16),
            pltpu.VMEM((4, tokens, D), BF16),
            pltpu.VMEM((4, tokens, WIDE - D), BF16),
            pltpu.VMEM((4, tokens, D), BF16),
            pltpu.SemaphoreType.DMA((48,)),
            pltpu.SemaphoreType.DMA((13,)),
        ],
    )


def ffn_backward_kernel(
    layer, grad_ref, first_ref, normed_two_ref, rstd_two_ref, slope_ref, normed_ref, rstd_ref,
    small, *refs
):
    pairs_ref, rows_ref, low_ref, smalls_ref, up, down, pairs, sems, out_sems = refs[-9:]
    downs, ups, _ = load_ffn_weights(refs[:-9], up, down, None, sems, True)

    def row(index):
        return small[layer, index : index + 1].astype(F32)

    grad = grad_ref[...].astype(F32)
    index = lax.broadcasted_iota(jnp.int32, grad.shape, 0)
    grad = grad + jnp.where(index == 0, first_ref[0:1], 0.0)
    grad = grad + jnp.where(index == SEQ, first_ref[1:2], 0.0)
    res_two, gain_two, shift_two = norm_back(grad, normed_two_ref[...], rstd_two_ref[...], row(G1))
    ffn_grad = res_two.astype(BF16)
    pairs[4] = ffn_grad
    leaving = run_copies([(pairs.at[4], pairs_ref.at[4])], out_sems, 4)
    wait_copies(downs)
    middle_grad = res_two
    for block in range(4):
        act_grad = nt(ffn_grad, down[block])
        pre_grad = (act_grad * slope_ref[block].astype(F32)).astype(BF16)
        pairs[block] = pre_grad
        leaving += run_copies([(pairs.at[block], pairs_ref.at[block])], out_sems, block)
        if block == 0:
            wait_copies(ups)
        smalls_ref[block : block + 1] = jnp.sum(pre_grad.astype(F32), 0, keepdims=True)
        middle_grad = middle_grad + nt(pre_grad, up[block])
    res_one, gain_one, shift_one = norm_back(middle_grad, normed_ref[...], rstd_ref[...], row(G0))
    rows_ref[...] = res_one
    low = res_one.astype(BF16)
    low_ref[...] = low
    smalls_ref[4:5] = jnp.sum(ffn_grad.astype(F32), 0, keepdims=True)
    smalls_ref[5:6] = jnp.sum(low.astype(F32), 0, keepdims=True)
    smalls_ref[6:7] = gain_one
    smalls_ref[7:8] = gain_two
    smalls_ref[8:9] = shift_one
    smalls_ref[9:10] = shift_two
    wait_copies(leaving)


def ffn_backward(
    line, layer, grad, first_grad, normed_two, rstd_two, slope, normed, rstd, small, weights
):
    tokens = grad.shape[0]
    return line.call(
        "ffn_backward%d" % layer,
        11,
        functools.partial(ffn_backward_kernel, layer),
        near(grad, first_grad, normed_two, rstd_two, slope, normed, rstd, small)
        + away(*weights),
        sent(((5, tokens, D), BF16))
        + made(
            ((tokens, D), F32),
            ((tokens, D), BF16),
            ((10, D), F32),
        ),
        [
            pltpu.VMEM((4, D, D), BF16),
            pltpu.VMEM((SHARDS, D, D), BF16),
            pltpu.VMEM((5, tokens, D), BF16),
            pltpu.SemaphoreType.DMA((32,)),
            pltpu.SemaphoreType.DMA((5,)),
        ],
    )


def place_pieces(groups, natural, outs, y, sems):
    here = quarter_index()
    pairs = []
    for index, (order, first, count) in enumerate(groups):
        keep_ref, send_ref = outs[2 * index : 2 * index + 2]
        rows = slice(first, first + count)
        for x in range(2):
            for a in range(2):
                if not order:
                    target, unit, place = (send_ref if y else keep_ref), 2 * a + x, 2 * a + x
                else:
                    bits = {"y": y, "x": x, "a": a}
                    outer, middle, inner = (bits[dim] for dim in order)
                    target = send_ref if outer else keep_ref
                    unit, place = (2 * a + x) ^ here, 2 * middle + inner
                pairs.append((natural.at[y, unit, rows], target.at[place]))
    return run_copies(pairs, sems, y * len(pairs))


def piece_shapes(groups):
    shapes = []
    for _, _, count in groups:
        shapes += [((4, count, D), BF16)] * 2
    return shapes


def ffn_weights_kernel(groups, act_ref, act_near_ref, pairs_ref, pairs_near_ref, *refs):
    outs, (natural, sems) = refs[:-2], refs[-2:]
    leaving = []
    for slot in (1, 0):
        mine, other = act_ref[slot], act_near_ref[slot]
        down = tn(mine[:, 0:D], pairs_ref[4]) + tn(other[:, 0:D], pairs_near_ref[4])
        down = down.astype(BF16)
        for block in range(4):
            natural[slot, block, PART : 2 * PART] = down[block * PART : (block + 1) * PART]
            up = tn(mine[:, D : D + PART], pairs_ref[block])
            up = up + tn(other[:, D : D + PART], pairs_near_ref[block])
            natural[slot, block, 0:PART] = up.astype(BF16)
        leaving += place_pieces(groups, natural, outs, slot, sems)
    wait_copies(leaving)


def ffn_weight_grads(line, layer, groups, act, act_near, pairs, pairs_near):
    return line.call(
        "ffn_weight_grads%d" % layer,
        8,
        functools.partial(ffn_weights_kernel, groups),
        near(act, act_near, pairs, pairs_near),
        sent(*piece_shapes(groups)),
        [pltpu.VMEM((2, 4, 2 * PART, D), BF16), pltpu.SemaphoreType.DMA((8 * len(groups),))],
    )


def attn_weights_kernel(
    groups, x_ref, acts_near_ref, grad_ref, pairs_ref, near_ref, *refs
):
    outs, (natural, sems) = refs[-2 - 2 * len(groups) : -2], refs[-2:]
    leaving = []
    cut = 3 * PART
    tokens = x_ref.shape[0]
    x_near = acts_near_ref[2, :, 0:D]
    grad_near = near_ref[2 * tokens : 3 * tokens]
    if len(refs) > 2 + 2 * len(groups):
        smalls_ref, by_shard = refs[0], refs[-3]
        outs = refs[1:-3]
        smalls = []
        for layer in range(LAYERS):
            start = 3 * tokens + 32 * layer
            high = near_ref[start : start + 16].astype(F32)
            rest = near_ref[start + 16 : start + 32].astype(F32)
            smalls.append(smalls_ref[layer] + (high + rest)[0:12])
        for part in range(SHARDS):
            lanes = slice(part * PART, (part + 1) * PART)
            for layer in range(LAYERS):
                row = 3 * layer
                by_shard[part, row : row + 1] = smalls[layer][part : part + 1]
                for item in range(8):
                    target = slice((item % 4) * PART, (item % 4 + 1) * PART)
                    value = smalls[layer][4 + item : 5 + item, lanes]
                    by_shard[part, row + 1 + item // 4 : row + 2 + item // 4, target] = value
            by_shard[part, 6:16] = jnp.zeros((10, D), F32)
        shard = shard_index()
        for slot in range(2):
            natural[slot, 0, PART:TALL] = by_shard[shard ^ (2 * slot)].astype(BF16)
            for unit in range(1, 4):
                natural[slot, unit, PART:TALL] = jnp.zeros((TALL - PART, D), BF16)
    for slot in (1, 0):
        mine, other = pairs_ref[slot], near_ref[slot * tokens : (slot + 1) * tokens]
        value = tn(mine[:, 0:cut], x_ref[...]) + tn(other[:, 0:cut], x_near)
        value = value.astype(BF16)
        for unit in range(3):
            natural[slot, unit, 0:PART] = value[unit * PART : (unit + 1) * PART]
        value = tn(mine[:, cut:D], grad_ref[...]) + tn(other[:, cut:D], grad_near)
        natural[slot, 3, 0:PART] = value.astype(BF16)
        leaving += place_pieces(groups, natural, outs, slot, sems)
    wait_copies(leaving)


def attn_weight_grads(line, layer, groups, *operands):
    return line.call(
        "attn_weight_grads%d" % layer,
        5,
        functools.partial(attn_weights_kernel, groups),
        near(*operands),
        sent(*piece_shapes(groups)),
        ([pltpu.VMEM((SHARDS, 16, D), F32)] if len(operands) > 5 else [])
        + [
            pltpu.VMEM((2, 4, groups[0][2], D), BF16),
            pltpu.SemaphoreType.DMA((8 * len(groups),)),
        ],
    )


def attn_backward_kernel(
    layer, res_ref, grad_ref, smalls_in_ref, *refs
):
    count = 10
    kept, weights, refs = refs[:6], refs[6:count], refs[count:]
    if layer == 0:
        prior, refs = refs[0], refs[1:]
    pairs_ref, pairs_send_ref, rows_ref, smalls_ref, slots, sems, sums = refs
    tokens = grad_ref.shape[0]
    copies = load_attn_weights(weights[:2], slots.at[0:2], sems)
    copies += load_attn_weights(weights[2:], slots.at[2:4], sems, 2)
    shard = shard_index()
    grad = grad_ref[...]
    total = res_ref[...]
    for slot in range(4):
        wait_copies(copies[slot])
        half, index = slot >> 1, slot & 1
        qkv_ref, probs_ref, context_ref = kept[3 * half : 3 * half + 3]
        context_grad = nt(grad, slots[slot, 3]).astype(BF16)
        places = [
            (
                slice(seq * SEQ, (seq + 1) * SEQ),
                slice(head * HEAD_DIM, (head + 1) * HEAD_DIM),
            )
            for seq in range(2)
            for head in range(PART // HEAD_DIM)
        ]
        query, key, val = (qkv_ref[index, part] for part in range(3))
        probs = probs_ref[index]
        prob_grad = jnp.stack([nt(context_grad[at], val[at]) for at in places])
        mean = jnp.sum(prob_grad * probs, -1, keepdims=True)
        score_grad = (probs * (prob_grad - mean)).astype(BF16)
        probs_low = probs.astype(BF16)
        scale = HEAD_DIM ** (-0.5)
        heads = [
            [nn(score_grad[i], key[at]) * scale for i, at in enumerate(places)],
            [tn(score_grad[i], query[at]) * scale for i, at in enumerate(places)],
            [tn(probs_low[i], context_grad[at]) for i, at in enumerate(places)],
        ]
        half_heads = len(places) // 2
        seq_rows = [
            [jnp.concatenate(group[:half_heads], -1), jnp.concatenate(group[half_heads:], -1)]
            for group in heads
        ]
        for part in range(3):
            value = jnp.concatenate(seq_rows[part], 0).astype(BF16)
            if slot & 1:
                rows = slice(half * tokens, (half + 1) * tokens)
                pairs_send_ref[rows, part * PART : (part + 1) * PART] = value
            else:
                pairs_ref[half, :, part * PART : (part + 1) * PART] = value
            if part != 1:
                sums[shard ^ slot, part // 2] = jnp.sum(value.astype(F32), 0, keepdims=True)
            total = total + nn(value, slots[slot, part])
        if slot & 1:
            pairs_send_ref[half * tokens : (half + 1) * tokens, 3 * PART : D] = context_ref[index]
        else:
            pairs_ref[half, :, 3 * PART : D] = context_ref[index]
    pairs_send_ref[2 * tokens : 3 * tokens] = grad
    rows_ref[...] = total.astype(rows_ref.dtype)
    own = [
        jnp.concatenate([sums[part, index] for part in range(SHARDS)], -1) for index in range(2)
    ]
    if layer:
        smalls_ref[0:10] = smalls_in_ref[...]
        smalls_ref[10:11] = own[0]
        smalls_ref[11:12] = own[1]
    else:
        smalls_ref[1] = prior[...]
        smalls_ref[0, 0:10] = smalls_in_ref[...]
        smalls_ref[0, 10:11] = own[0]
        smalls_ref[0, 11:12] = own[1]
        for index in range(LAYERS):
            value = smalls_ref[index]
            high = value.astype(BF16)
            rest = (value - high.astype(F32)).astype(BF16)
            start = 3 * tokens + 32 * index
            pairs_send_ref[start : start + 16] = jnp.concatenate(
                [high, jnp.zeros((4, D), BF16)], 0
            )
            pairs_send_ref[start + 16 : start + 32] = jnp.concatenate(
                [rest, jnp.zeros((4, D), BF16)], 0
            )


def attn_backward(line, layer, res, grad, kept, smalls, weights, prior):
    tokens = grad.shape[0]
    return line.call(
        "attn_backward%d" % layer,
        15,
        functools.partial(attn_backward_kernel, layer),
        near(res, grad, smalls, *kept) + away(*weights) + near(*prior),
        made(
            ((2, tokens, D), BF16),
            ((3 * tokens + (0 if layer else 64), D), BF16),
            ((tokens, D), F32 if layer else BF16),
            ((12, D) if layer else (2, 12, D), F32),
        ),
        [
            pltpu.VMEM((4, 4, PART, D), BF16),
            pltpu.SemaphoreType.DMA((12,)),
            pltpu.VMEM((SHARDS, 2, 1, PART), F32),
        ],
    )


def halve_kernel(keep_ref, came_ref, low_ref, high_ref):
    half = low_ref.shape[0]
    low_ref[...] = keep_ref[0:half] + came_ref[0:half]
    high_ref[...] = keep_ref[half:] + came_ref[half:]


def add_kernel(keep_ref, came_ref, sum_ref):
    sum_ref[...] = keep_ref[...] + came_ref[...]


def reduction(line, moves, name, order, back, keep, send):
    shape = keep.shape
    micros = 1 + shape[1] / 192
    if not order:
        came = moves("y", send)
        yield
        total = line.call(
            "add_%s" % name, micros, add_kernel, near(keep, came), made((shape, BF16))
        )[0]
        yield (back, lax.psum(total, "dp"))
    came = moves(order[0], send)
    for step, dim in enumerate(order[1:]):
        yield
        half = (keep.shape[0] // 2, *shape[1:])
        keep, send = line.call(
            "halve_%s%d" % (name, step), micros, halve_kernel, near(keep, came),
            made((half, BF16), (half, BF16)),
        )
        came = moves(dim, send)
    yield
    keep, came = keep[0], came[0]
    total = line.call(
        "add_%s" % name, micros, add_kernel, near(keep, came), made((shape[1:], BF16))
    )[0]
    came = moves("b", total)
    for bit in moves.more():
        yield
        total = line.call(
            "more_%s%d" % (name, bit), micros, add_kernel, near(total, came),
            made((shape[1:], BF16)),
        )[0]
        came = moves.place(bit, total)
    yield
    total = line.call(
        "last_%s" % name, micros, add_kernel, near(total, came), made((shape[1:], BF16))
    )[0]
    came = moves(back[0], total)
    yield
    both = line.call(
        "both_%s" % name, micros, both_kernel, near(total, came), made(((2, *shape[1:]), BF16))
    )[0]
    yield (back, both, moves(back[1], both))


def join_kernel(one_ref, two_ref, joint_ref):
    count = one_ref.shape[0]
    joint_ref[0:count] = one_ref[...]
    joint_ref[count : 2 * count] = two_ref[...]


def join(line, one, two):
    shape = (2 * one.shape[0], *one.shape[1:])
    return line.call("join%d" % shape[0], 1, join_kernel, near(one, two), made((shape, BF16)))[0]


def both_kernel(one_ref, two_ref, both_ref):
    both_ref[0] = one_ref[...]
    both_ref[1] = two_ref[...]


def unpack_kernel(back, first, targets, prior, *refs):
    values = 2 if back else 1
    quarters = refs[:values]
    outs = refs[values + prior : -2]
    whole, sems = refs[-2:]
    here = quarter_index()
    count = whole.shape[1]
    for index in range(4):
        if not back:
            whole[index] = quarters[0][index, first : first + count].astype(F32)
            continue
        bits = {back[0]: index & 1, back[1]: index >> 1}
        relative = 2 * bits["a"] + bits["x"]
        quarter = quarters[index >> 1][index & 1, first : first + count]
        whole[relative ^ here] = quarter.astype(F32)
    if count == TALL:
        qkv_bias, out_bias, gain, shift, in_bias, down_bias = outs[len(targets) :]
        for layer in range(LAYERS):
            row = PART + 3 * layer

            def item(index):
                at = row + 1 + index // 4
                return whole[0, at : at + 1, (index % 4) * PART : (index % 4 + 1) * PART]

            in_bias[layer : layer + 1] = whole[0, row : row + 1]
            down_bias[layer : layer + 1] = item(0)
            out_bias[layer : layer + 1] = item(1)
            for index in range(2):
                gain[layer, index : index + 1] = item(2 + index)
                shift[layer, index : index + 1] = item(4 + index)
                qkv_bias[layer, index : index + 1] = item(6 + index)
    pairs = [
        (whole.at[unit, 0:PART], outs[which].at[where])
        for unit, which, where in targets_of(targets)
    ]
    wait_copies(run_copies(pairs, sems, 0))


def targets_of(targets):
    return [(unit, which, where) for which, places in enumerate(targets) for unit, where in places]


SMALL_SHAPES = (
    (LAYERS, 2, PART), (LAYERS, PART), (LAYERS, 2, PART), (LAYERS, 2, PART), (LAYERS, D), (LAYERS, PART)
)


def unpack(line, name, quarters, first, shapes, targets, prior):
    back, *values = quarters
    aliases = {len(values) + index: index for index in range(len(prior))}
    count = TALL if values[0].shape[1] == TALL else PART
    outs = [(shape, F32, anywhere()) for shape in shapes]
    if count == TALL:
        outs += made(*[(shape, F32) for shape in SMALL_SHAPES])
    return line.call(
        name,
        3,
        functools.partial(unpack_kernel, back, first, targets, len(prior)),
        near(*values) + away(*prior),
        outs,
        [pltpu.VMEM((4, count, D), F32), pltpu.SemaphoreType.DMA((4,))],
        aliases,
    )


def unpack_up(line, layer, quarters, first, prior):
    places = [(unit, (layer, slice(None), slice(unit * D, (unit + 1) * D))) for unit in range(4)]
    return unpack(
        line, "unpack_up%d" % layer, quarters, first, [(LAYERS, PART, FF)], [places], prior
    )


def unpack_down(line, layer, quarters, first, prior):
    places = [(unit, (layer, slice(unit * PART, (unit + 1) * PART))) for unit in range(4)]
    return unpack(
        line, "unpack_down%d" % layer, quarters, first, [(LAYERS, D, D)], [places], prior
    )


def unpack_attn(line, layer, quarters, first, prior):
    return unpack(
        line,
        "unpack_attn%d" % layer,
        quarters,
        first,
        [(LAYERS, 3, PART, D), (LAYERS, PART, D)],
        [[(unit, (layer, unit)) for unit in range(3)], [(3, (layer,))]],
        prior,
    )


def pool_grads(ramp, shard):
    ramp = ramp.reshape(ramp.shape[0], LAYERS, 4, 2, D)
    ramp = jnp.transpose(ramp, (1, 2, 0, 3, 4)).reshape(LAYERS, 4, -1, D)
    first, pool_grad, pooled, logit_grad = (ramp[:, part] for part in range(4))
    logit_grad = logit_grad[:, :, 0:CLASSES]
    own_first = lax.dynamic_slice_in_dim(first, shard * PART, PART, 2)
    own_pooled = lax.dynamic_slice_in_dim(pooled, shard * PART, PART, 2)
    pool_weight_grad = jnp.einsum("lnd,lne->lde", own_first, pool_grad, preferred_element_type=F32)
    class_weight_grad = jnp.einsum(
        "lnd,lnc->ldc", own_pooled, logit_grad, preferred_element_type=F32
    )
    class_bias_grad = jnp.sum(logit_grad.astype(F32), 1)
    own_pool = lax.dynamic_slice_in_dim(pool_grad, shard * PART, PART, 2)
    pool_bias_grad = jnp.sum(own_pool.astype(F32), 1)
    return pool_weight_grad, pool_bias_grad, class_weight_grad, class_bias_grad


ROUTES = {
    "f1": ("yxa", "ax"),
    "a1": ("axy", "ax"),
    "f0": ("axy", "ax"),
    "a0": ("yxa", "xa"),
}
SCHEDULE = (
    "F1", "A1", "FW1", "AW1", "F0", "a1", "A0", "FW0", "AW0", "f1", "a1", "a0", "f1", "a1",
    "f0", "a0", "f1", "a1", "f0", "a1", "f1", "f0", "a0", "Ua1", "a0", "R0", "R1", "f1", "R1",
    "a0", "f0", "R1", "Ua0", "f0", "R1", "Uf1", "R1", "P1", "Uf0",
)


def on_device(
    mesh,
    hidden_in,
    out_cotangent,
    labels,
    qkv_weight,
    qkv_bias,
    out_weight,
    out_bias,
    norm_gain,
    norm_shift,
    ffn_in,
    ffn_in_bias,
    ffn_out,
    ffn_out_bias,
    pool_weight,
    pool_bias,
    class_weight,
    class_bias,
):
    moves = Moves(mesh)
    line = Line()
    shard = shard_index()
    qkv_turned = jnp.swapaxes(qkv_weight, 2, 3)

    packed = line.call(
        "pack_small",
        1,
        pack_small_kernel,
        near(
            qkv_bias, out_bias, norm_gain, norm_shift, ffn_in_bias, ffn_out_bias, pool_bias,
            jnp.transpose(class_weight, (2, 0, 1)),
        ),
        made(((LAYERS, 16, PART), F32)),
    )[0]
    first_pack, ffn_quarter = pack_ffn(line, 0, ffn_in, ffn_out, pool_weight)
    ffn_far = [Spread(line, moves, ffn_quarter, "x")]
    own = pack_attn(line, 0, qkv_turned, out_weight)
    attn_own = [[own, moves("c", own)]]
    class_bias_wide = class_bias.astype(F32)
    shard_small, small, in_bias = arrange(line, moves, packed)

    far = moves("y", line.gate(attn_own[0][0])[0])

    x = hidden_in
    kept, nears = [], []
    prior = ()
    for layer in range(LAYERS):
        *attn_near, total = attn_forward(line, layer, 0, x, (shard_small,), attn_own[layer])
        if layer == 0:
            ffn_far[0].second()
            ffn_pack, ffn_quarter = pack_ffn(line, 1, ffn_in, ffn_out, pool_weight)
            ffn_far.append(Spread(line, moves, ffn_quarter, "a"))
            ffn_far[0].third()
            far, first_pack = line.gate(far, first_pack)
            ffn_own = [[first_pack, moves("c", first_pack)]]
            attn_far = [[far, moves("c", far)]]
        else:
            far, ffn_pack = line.gate(far, ffn_pack)
            ffn_own.append([ffn_pack, moves("c", ffn_pack)])
            attn_far.append([far, moves("c", far)])
        *attn_rest, normed, rstd, low = attn_forward(
            line, layer, 1, x, (shard_small, small, total), attn_far[layer]
        )
        if layer == 0:
            line.waits = (*line.waits, ffn_own[0][1], ffn_far[0].stack)
            own = pack_attn(line, 1, qkv_turned, out_weight)
            ffn_far[1].second()
            far = moves("y", line.gate(own)[0])
            ffn_far[0].fourth()
            attn_own.append([own, moves("c", own)])
            line.waits = (*line.waits, attn_own[1][1])
            ffn_weights = [ffn_own[0] + ffn_far[0].pieces()]
        else:
            line.waits = (*line.waits, nears[0])
            ffn_far[1].fourth()
            ffn_weights.append(ffn_own[1] + ffn_far[1].pieces())
        act, act_send, slope, normed_two, rstd_two, first_grad, *prior = ffn_forward(
            line, layer, labels, class_bias_wide, x, normed, low, small, in_bias,
            ffn_weights[layer], prior,
        )
        if layer == 0:
            ffn_far[1].third()
        act_near = moves("c", act_send)
        nears.append(act_near)
        kept.append(
            (
                x,
                (attn_near + attn_rest, normed, rstd),
                (act, act_near),
                (slope, normed_two, rstd_two, first_grad),
            )
        )
        x = prior[0]
    block_outputs, logits, ramp = prior

    chains, results, state = {}, {}, {"grad": out_cotangent, "prior": ()}
    ramp_value = [ramp[None]]
    ramp_steps = [("head", 1), ("head", 2)]
    bit = 1
    while bit < mesh.shape["dp"]:
        ramp_steps.append(("dp", bit))
        bit *= 2

    def begin(names, pieces):
        for index, name in enumerate(names):
            keep, send = pieces[2 * index : 2 * index + 2]
            chains[name] = reduction(line, moves, name, *ROUTES[name], keep, send)
            next(chains[name])

    def step(name):
        layer = int(name[-1])
        if name == "R0":
            ramp_value[0] = line.gate(ramp_value[0])[0]
        elif name[:-1] == "F":
            _, (_, normed, rstd), _, (slope, normed_two, rstd_two, first_grad) = kept[layer]
            pairs, res, low, rows = ffn_backward(
                line, layer, state["grad"], first_grad, normed_two, rstd_two, slope, normed, rstd,
                small, ffn_weights[layer],
            )
            state["ffn"] = (pairs, moves("c", pairs))
            state["low"] = low
            state["res"], state["rows"] = res, rows
            line.waits = (*line.waits, nears[layer])
        elif name[:-1] == "A":
            pairs, send, grad, smalls = attn_backward(
                line, layer, state["res"], state["low"], kept[layer][1][0], state["rows"],
                attn_own[layer] + attn_far[layer], state["prior"],
            )
            state["attn"] = (pairs, moves("c", send))
            state["grad"], state["prior"] = grad, (smalls,)
        elif name[:-1] == "FW":
            names = [key for key in ROUTES if key[-1] == name[-1] and key[0] != "a"]
            spans = {"f": (0, 2 * PART), "u": (0, PART), "d": (PART, PART)}
            groups = [(ROUTES[key][0], *spans[key[0]]) for key in names]
            begin(names, ffn_weight_grads(line, layer, groups, *kept[layer][2], *state["ffn"]))
        elif name[:-1] == "AW":
            key = "a" + name[-1]
            groups = [(ROUTES[key][0], 0, PART if layer else TALL)]
            operands = (kept[layer][0], kept[layer][2][1], state["low"], *state["attn"])
            if layer == 0:
                operands += state["prior"]
            begin([key], attn_weight_grads(line, layer, groups, *operands))
        elif name == "R1":
            for _ in range(max(1, len(ramp_steps) - 4)):
                axis, bit = ramp_steps.pop(0)
                came = lax.ppermute(ramp_value[0], AXES, flip(mesh, axis, bit))
                ramp_value[0] = join(line, ramp_value[0], came)
        elif name == "P1":
            state["pool"] = pool_grads(ramp_value[0], shard)
            line.waits = (*line.waits, *state["pool"])
        elif name[0] == "U":
            key = name[1:]
            while key not in results:
                results[key] = next(chains[key])
                if results[key] is None:
                    del results[key]
            if key[0] in "uf":
                state["up"] = unpack_up(line, layer, results[key], 0, state.get("up", ()))
            if key[0] in "df":
                first = PART if key[0] == "f" else 0
                state["down"] = unpack_down(line, layer, results[key], first, state.get("down", ()))
            if key[0] == "a":
                state["attn_out"] = unpack_attn(
                    line, layer, results[key], 0, state.get("attn_out", ())
                )
        else:
            result = next(chains[name], None)
            if result is not None:
                results[name] = result

    for name in SCHEDULE:
        step(name)
    qkv_grad, out_grad, qkv_bias_grad, out_bias_grad, *smalls = state["attn_out"]
    gain_grad, shift_grad, in_bias_grad, down_bias_grad = smalls
    pool_weight_grad, pool_bias_grad, class_weight_grad, class_bias_grad = state["pool"]
    return (
        block_outputs,
        logits[:, 0:2, 0:CLASSES],
        state["grad"],
        jnp.swapaxes(qkv_grad, 2, 3),
        qkv_bias_grad,
        out_grad,
        out_bias_grad,
        gain_grad,
        shift_grad,
        state["up"][0],
        in_bias_grad,
        state["down"][0],
        down_bias_grad,
        pool_weight_grad,
        pool_bias_grad,
        class_weight_grad,
        class_bias_grad,
    )


def solution(mesh):
    return jax.shard_map(
        functools.partial(on_device, mesh),
        mesh=mesh,
        in_specs=(
            P(("dp", "head"), None),
            P(("dp", "head"), None),
            P(("dp", "head")),
            P(None, None, None, "head"),
            P(None, None, "head"),
            P(None, "head", None),
            P(None, "head"),
            P(None, None, "head"),
            P(None, None, "head"),
            P(None, "head", None),
            P(None, "head"),
            P(None, "head", None),
            P(None, "head"),
            P(None, "head", None),
            P(None, "head"),
            P(None, "head", None),
            P(),
        ),
        out_specs=(
            P(None, ("dp", "head"), None),
            P(None, ("dp", "head"), None),
            P(("dp", "head"), None),
            P(None, None, None, "head"),
            P(None, None, "head"),
            P(None, "head", None),
            P(None, "head"),
            P(None, None, "head"),
            P(None, None, "head"),
            P(None, "head", None),
            P(None, "head"),
            P(None, "head", None),
            P(None, "head"),
            P(None, "head", None),
            P(None, "head"),
            P(None, "head", None),
            P(),
        ),
        check_vma=False,
    )
```

```python
import functools

import jax
import jax.numpy as jnp
from jax import lax
from jax.experimental import pallas as pl
from jax.experimental.pallas import tpu as pltpu
from jax.sharding import PartitionSpec as P

D = 768
FF = 3072
HEAD_DIM = 64
SEQ = 128
LAYERS = 2
SHARDS = 4
PART = D // SHARDS
POOL_PART = PART // 4
CLASSES = 3
EPS = 1e-12
ROOT_HALF = 0.7071067811865476
DENSITY_SCALE = 0.3989422804014327
F32 = jnp.float32
BF16 = jnp.bfloat16
AXES = ("dp", "head")
VMEM_LIMIT = 58 * 1024 * 1024
TALL = PART + 16
FFN_ROWS = 2 * PART + POOL_PART
WIDE = 1024

QB, VB, OB, G0, G1, S0, S1, FB, PB, CW = 0, 1, 2, 3, 4, 5, 6, 11, 12, 13


def dot(left, right, dims):
    return lax.dot_general(left, right, ((dims[:1], dims[1:]), ((), ())), preferred_element_type=F32)


def nn(left, right):
    return dot(left, right, (1, 0))


def nt(left, right):
    return dot(left, right, (1, 1))


def tn(left, right):
    return dot(left, right, (0, 0))


def normalise(resid):
    centred = resid - jnp.mean(resid, -1, keepdims=True)
    rstd = lax.rsqrt(jnp.mean(centred * centred, -1, keepdims=True) + EPS)
    return centred * rstd, rstd


def norm_back(incoming, normed, rstd, gain):
    scaled = incoming * gain
    back = rstd * (
        scaled
        - jnp.mean(scaled, -1, keepdims=True)
        - normed * jnp.mean(scaled * normed, -1, keepdims=True)
    )
    gain_grad = jnp.sum(incoming * normed, 0, keepdims=True)
    shift_grad = jnp.sum(incoming, 0, keepdims=True)
    return back, gain_grad, shift_grad


def cost(micros):
    return pl.CostEstimate(flops=int(micros * 1e10), bytes_accessed=0, transcendentals=0)


def shard_index():
    return lax.axis_index("head")


def quarter_index():
    return lax.axis_index("dp") & 3


def rows_at(index, count):
    return pl.ds(pl.multiple_of(index * count, count), count)


def vmem():
    return pl.BlockSpec(memory_space=pltpu.VMEM)


def anywhere():
    return pl.BlockSpec(memory_space=pl.ANY)


ROOM = {
    "pack": 14, "arrange": 4, "attn_forward": 18, "ffn_forward": 30, "ffn_backward": 32,
    "attn_backward": 24, "ffn_weight": 20, "attn_weight": 16, "halve": 14, "unpack": 14,
}


def room(name):
    for start, size in ROOM.items():
        if name.startswith(start):
            return size << 20
    return 8 << 20


TOKEN = jax.ShapeDtypeStruct((8, 128), F32)


def main_memory():
    return pl.BlockSpec(memory_space=pltpu.HBM)


class Line:
    def __init__(self):
        self.waits = ()

    def call(self, name, micros, kernel, ins, outs, scratch=(), aliases=None):
        waits = tuple(self.waits)
        count, total = len(ins), len(ins) + len(waits) + len(outs)

        def body(*refs):
            kernel(*refs[:count], *refs[count + len(waits) : total], *refs[total + 1 :])

        *result, token = pl.pallas_call(
            body,
            out_shape=[jax.ShapeDtypeStruct(shape, dtype) for shape, dtype, _ in outs] + [TOKEN],
            in_specs=[spec for _, spec in ins] + [main_memory()] * len(waits),
            out_specs=[spec for _, _, spec in outs] + [main_memory()],
            scratch_shapes=list(scratch),
            input_output_aliases=aliases or {},
            compiler_params=pltpu.CompilerParams(vmem_limit_bytes=room(name)),
            cost_estimate=cost(micros),
            name=name,
        )(*[value for value, _ in ins], *waits)
        self.waits = (token,)
        return result

    def gate(self, *values):
        outs = [(value.shape, value.dtype, anywhere()) for value in values]
        aliases = {index: index for index in range(len(values))}
        return self.call("gate", 0.1, lambda *refs: None, away(*values), outs, aliases=aliases)


def near(*values):
    return [(value, vmem()) for value in values]


def fixed(*values):
    return [(value, main_memory()) for value in values]


def away(*values):
    return [(value, anywhere()) for value in values]


def made(*shapes):
    return [(shape, dtype, vmem()) for shape, dtype in shapes]


def sent(*shapes):
    return [(shape, dtype, anywhere()) for shape, dtype in shapes]


def run_copies(pairs, sems, start):
    copies = [
        pltpu.make_async_copy(src, dst, sems.at[start + index])
        for index, (src, dst) in enumerate(pairs)
    ]
    for item in copies:
        item.start()
    return copies


def wait_copies(copies):
    for item in copies:
        item.wait()


def flip(mesh, axis, bit):
    dp, head = mesh.shape["dp"], mesh.shape["head"]
    pairs = []
    for place in range(dp):
        for shard in range(head):
            to_place = place ^ bit if axis == "dp" else place
            to_shard = shard ^ bit if axis == "head" else shard
            pairs.append((place * head + shard, to_place * head + to_shard))
    return pairs


DIMS = {"c": ("head", 1), "y": ("head", 2), "d": ("head", 3), "x": ("dp", 1), "a": ("dp", 2), "b": ("dp", 4)}


class Moves:
    def __init__(self, mesh):
        self.mesh = mesh

    def __call__(self, dim, value):
        return lax.ppermute(value, AXES, flip(self.mesh, *DIMS[dim]))

    def more(self):
        bit = 8
        while bit < self.mesh.shape["dp"]:
            yield bit
            bit *= 2

    def place(self, bit, value):
        return lax.ppermute(value, AXES, flip(self.mesh, "dp", bit))


def stack_kernel(one, two, follow, follow_out, stack_ref, sems, *, order):
    refs = {"one": one, "two": two, "follow": follow}
    pairs = [(refs[name], stack_ref.at[index]) for index, name in enumerate(order)]
    wait_copies(run_copies(pairs, sems, 0))


class Spread:
    def __init__(self, line, moves, quarter, last):
        self.line, self.moves, self.last = line, moves, last
        self.far = [moves("y", quarter)]

    def second(self):
        self.far = list(self.line.gate(*self.far))
        self.far += [self.moves("x", self.far[0]), self.moves("a", self.far[0])]

    def third(self):
        follow = 2 if self.last == "x" else 1
        shape = self.far[0].shape
        order = ("one", "two", "follow") if follow == 2 else ("one", "follow", "two")
        operands = (self.far[0], self.far[3 - follow], self.far[follow])
        self.far[follow], stack = self.line.call(
            "stack",
            3,
            functools.partial(stack_kernel, order=order),
            fixed(*operands),
            [(shape, BF16, main_memory()), ((3, *shape), BF16, vmem())],
            [pltpu.SemaphoreType.DMA((3,))],
            {2: 0},
        )
        self.stack = self.moves("c", stack)
        self.far.append(self.moves(self.last, self.far[follow]))

    def fourth(self):
        self.far[3] = self.line.gate(self.far[3])[0]
        self.near = self.moves("c", self.far[3])

    def pieces(self):
        return [*self.far, self.stack, self.near]


def pack_attn_kernel(layer, qkv_ref, out_ref, own_ref, sems):
    pairs = [(qkv_ref.at[layer], own_ref.at[0:3]), (out_ref.at[layer], own_ref.at[3])]
    wait_copies(run_copies(pairs, sems, 0))


def pack_attn(line, layer, qkv, out):
    return line.call(
        "pack_attn%d" % layer,
        2,
        functools.partial(pack_attn_kernel, layer),
        away(qkv, out),
        made(((4, PART, D), BF16)),
        [pltpu.SemaphoreType.DMA((2,))],
    )[0]


def pack_ffn_kernel(layer, in_ref, down_ref, pool_ref, own_ref, quarter_ref, sems):
    pairs = []
    for index in range(4):
        target = own_ref.at[index]
        pairs += [
            (in_ref.at[layer, :, index * D : (index + 1) * D], target.at[0:PART]),
            (
                down_ref.at[layer, index * PART : (index + 1) * PART],
                target.at[PART : 2 * PART],
            ),
            (
                pool_ref.at[layer, index * POOL_PART : (index + 1) * POOL_PART],
                target.at[2 * PART : FFN_ROWS],
            ),
        ]
    wait_copies(run_copies(pairs, sems, 0))
    quarter_ref[...] = own_ref[quarter_index()]


def pack_ffn(line, layer, ffn_in, ffn_out, pool):
    return line.call(
        "pack_ffn%d" % layer,
        3,
        functools.partial(pack_ffn_kernel, layer),
        fixed(ffn_in, ffn_out, pool),
        made(((4, FFN_ROWS, D), BF16), ((FFN_ROWS, D), BF16)),
        [pltpu.SemaphoreType.DMA((12,))],
    )


def pack_small_kernel(
    qkv_bias, out_bias, gain, shift, in_bias, down_bias, pool_bias, class_weight, packed_ref
):
    for layer in range(LAYERS):
        packed_ref[layer, QB : VB + 1] = qkv_bias[layer].astype(F32)
        packed_ref[layer, OB : OB + 1] = out_bias[layer : layer + 1].astype(F32)
        packed_ref[layer, G0 : G1 + 1] = gain[layer].astype(F32)
        packed_ref[layer, S0 : S1 + 1] = shift[layer].astype(F32)
        for index in range(4):
            value = in_bias[layer : layer + 1, index * PART : (index + 1) * PART]
            packed_ref[layer, 7 + index : 8 + index] = value.astype(F32)
        packed_ref[layer, FB : FB + 1] = down_bias[layer : layer + 1].astype(F32)
        packed_ref[layer, PB : PB + 1] = pool_bias[layer : layer + 1].astype(F32)
        for cls in range(CLASSES):
            value = class_weight[cls, layer : layer + 1].astype(F32)
            packed_ref[layer, CW + cls : CW + cls + 1] = value


def arrange_kernel(own, core, row, both, shards_ref, small_ref, bias_ref):
    shard = shard_index()
    for slot, ref in enumerate((own, core, row, both)):
        shards_ref[shard ^ slot] = ref[...]
    for part in range(SHARDS):
        for layer in range(LAYERS):
            lanes = slice(part * PART, (part + 1) * PART)
            small_ref[layer, :, lanes] = shards_ref[part, layer]
            for index in range(4):
                target = slice(index * PART, (index + 1) * PART)
                value = shards_ref[part, layer, 7 + index : 8 + index]
                bias_ref[layer, part : part + 1, target] = value


def arrange(line, moves, packed):
    core, row = moves("c", packed), moves("y", packed)
    return line.call(
        "arrange",
        1,
        arrange_kernel,
        near(packed, core, row, moves("d", packed)),
        made(
            ((SHARDS, LAYERS, 16, PART), F32),
            ((LAYERS, 16, D), F32),
            ((LAYERS, SHARDS, D), F32),
        ),
    )


def load_attn_weights(refs, slots, sems, start=0):
    here = quarter_index()
    copies = []
    for slot in range(2):
        if len(refs) == 2:
            pairs = [(refs[slot], slots.at[slot])]
        else:
            pieces = refs[0:4] if slot == 0 else [refs[4].at[0], refs[4].at[1], refs[4].at[2], refs[5]]
            pairs = [(piece, slots.at[slot, here ^ index]) for index, piece in enumerate(pieces)]
        copies.append(run_copies(pairs, sems, start + len(pairs) * slot))
    return copies


def attn_forward_kernel(layer, half, x_ref, *refs):
    if half:
        (shard_small, small, total_in), refs = refs[:3], refs[3:]
        count = 2
        weights, refs = refs[:count], refs[count:]
        qkv_ref, probs_ref, context_ref, normed_ref, rstd_ref, low_ref, slots, sems = refs
    else:
        shard_small, weights, refs = refs[0], refs[1:3], refs[3:]
        qkv_ref, probs_ref, context_ref, total_ref, slots, sems = refs
    copies = load_attn_weights(weights, slots, sems)
    shard = shard_index()
    x = x_ref[...]
    if half:
        total = total_in[...] + small[layer, OB : OB + 1].astype(F32)
    else:
        total = x.astype(F32)
    for slot in range(2):
        wait_copies(copies[slot])
        biases = shard_small[shard ^ (2 * half + slot), layer]
        parts = []
        for part in range(3):
            value = nt(x, slots[slot, part])
            if part != 1:
                row = QB if part == 0 else VB
                value = value + biases[row : row + 1].astype(F32)
            value = value.astype(BF16)
            qkv_ref[slot, part] = value
            parts.append(value)
        query, key, val = parts
        places = [
            (
                slice(seq * SEQ, (seq + 1) * SEQ),
                slice(head * HEAD_DIM, (head + 1) * HEAD_DIM),
            )
            for seq in range(2)
            for head in range(PART // HEAD_DIM)
        ]
        scores = jnp.stack([nt(query[at], key[at]) for at in places]) * HEAD_DIM ** (-0.5)
        shifted = jnp.exp(scores - jnp.max(scores, -1, keepdims=True))
        probs = shifted * (1.0 / jnp.sum(shifted, -1, keepdims=True))
        probs_ref[slot] = probs
        low = probs.astype(BF16)
        heads = [nn(low[index], val[at]) for index, at in enumerate(places)]
        half_heads = len(heads) // 2
        context = jnp.concatenate(
            [
                jnp.concatenate(heads[:half_heads], -1),
                jnp.concatenate(heads[half_heads:], -1),
            ],
            0,
        ).astype(BF16)
        context_ref[slot] = context
        total = total + nn(context, slots[slot, 3])
    if half == 0:
        total_ref[...] = total
        return
    normed, rstd = normalise(total)
    normed_ref[...] = normed
    rstd_ref[...] = rstd
    middle = normed * small[layer, G0 : G0 + 1].astype(F32) + small[layer, S0 : S0 + 1].astype(F32)
    low_ref[...] = middle.astype(BF16)


def attn_forward(line, layer, half, x, inputs, weights):
    tokens = x.shape[0]
    outs = [
        ((2, 3, tokens, PART), BF16),
        ((2, 6, SEQ, SEQ), F32),
        ((2, tokens, PART), BF16),
        ((tokens, D), F32),
    ]
    if half:
        outs += [((tokens, 1), F32), ((tokens, D), BF16)]
    return line.call(
        "attn_forward%d%d" % (layer, half),
        7,
        functools.partial(attn_forward_kernel, layer, half),
        near(x, *inputs) + fixed(*weights),
        made(*outs),
        [pltpu.VMEM((2, 4, PART, D), BF16), pltpu.SemaphoreType.DMA((8,))],
    )


def load_ffn_weights(refs, up, down, pool, sems, down_first=False):
    here = quarter_index()
    shard = shard_index()
    ups, downs, pools = [], [], []

    def block_of(source, owner, block):
        ups.append((source.at[0:PART], up.at[block, rows_at(owner, PART)]))
        downs.append((source.at[PART : 2 * PART], down.at[owner, rows_at(block, PART)]))
        if pool is not None:
            target = pool.at[rows_at(owner * 4 + block, POOL_PART)]
            pools.append((source.at[2 * PART : FFN_ROWS], target))

    wholes = refs if len(refs) == 4 else refs[:2]
    for slot, whole in enumerate(wholes):
        for block in range(4):
            block_of(whole.at[block], shard ^ slot, block)
    if len(refs) == 8:
        pieces = [*refs[2:6], refs[6].at[0], refs[6].at[1], refs[6].at[2], refs[7]]
        for index, piece in enumerate(pieces):
            block_of(piece, shard ^ (2 + index // 4), here ^ (index % 4))
    order = (downs, ups, pools) if down_first else (ups, downs, pools)
    first = run_copies(order[0], sems, 0)
    second = run_copies(order[1], sems, len(ups))
    return first, second, run_copies(pools, sems, 2 * len(ups))


def ffn_forward_kernel(
    layer, labels_ref, class_bias_ref, x_ref, normed_ref, low_ref, small, in_bias, *refs
):
    count = 8
    weights, refs = refs[:count], refs[count:]
    if layer:
        (prior_out, prior_logits, prior_ramp), refs = refs[:3], refs[3:]
    act_ref, act_send_ref, slope_ref, normed_two_ref, rstd_two_ref, first_grad_ref = refs[:6]
    out_ref, logits_ref, ramp_ref, up, down, pool, acts, lows, slopes, sems, out_sems = refs[6:]
    ups, downs, pools = load_ffn_weights(weights, up, down, pool, sems)
    leaving = run_copies([(x_ref, act_send_ref.at[2, :, 0:D])], out_sems, 0)
    normed = normed_ref[...]
    low = low_ref[...]

    def row(index):
        return small[layer, index : index + 1].astype(F32)

    total = normed * row(G0) + row(S0) + row(FB)
    for part in range(4):
        lows[part, :, 0:PART] = low[:, part * PART : (part + 1) * PART]
        lows[part, :, PART:] = jnp.zeros((low.shape[0], WIDE - D - PART), BF16)
    wait_copies(ups)
    for block in range(4):
        pre_act = nn(low, up[block]) + in_bias[layer, block : block + 1].astype(F32)
        cumulative = 0.5 * (1.0 + lax.erf(pre_act * ROOT_HALF))
        act = (pre_act * cumulative).astype(BF16)
        density = jnp.exp(-0.5 * pre_act * pre_act) * DENSITY_SCALE
        acts[block] = act
        slopes[block] = cumulative + pre_act * density
        leaving += run_copies([(slopes.at[block], slope_ref.at[block])], out_sems, 1 + block)
        if block == 0:
            wait_copies(downs)
        total = total + nn(act, down[block])
    shard = shard_index()
    pairs = []
    for slot in range(4):
        target = (act_send_ref if slot & 1 else act_ref).at[slot >> 1]
        pairs.append((acts.at[shard ^ slot], target.at[:, 0:D]))
        pairs.append((lows.at[shard ^ slot], target.at[:, D:WIDE]))
    leaving += run_copies(pairs, out_sems, 5)
    wait_copies(pools)
    normed_two, rstd_two = normalise(total)
    normed_two_ref[...] = normed_two
    rstd_two_ref[...] = rstd_two
    output = (normed_two * row(G1) + row(S1)).astype(BF16)

    first = jnp.concatenate([output[0:1], output[SEQ : SEQ + 1]], 0).astype(F32)
    first = jnp.concatenate([first, jnp.zeros((14, D), F32)], 0).astype(BF16)
    pool_weight = pool[...]
    pooled = jnp.tanh(nn(first, pool_weight) + row(PB))
    wide = pooled.astype(BF16).astype(F32)
    lanes = lax.broadcasted_iota(jnp.int32, (16, 128), 1)
    rows = lax.broadcasted_iota(jnp.int32, (16, 128), 0)
    logits = jnp.zeros((16, 128), F32)
    for cls in range(CLASSES):
        value = jnp.sum(wide * row(CW + cls), -1, keepdims=True)
        value = value + class_bias_ref[layer, cls]
        logits = jnp.where(lanes == cls, value, logits)
    valid = lanes < CLASSES
    peak = jnp.max(jnp.where(valid, logits, -jnp.inf), -1, keepdims=True)
    shifted = jnp.where(valid, jnp.exp(logits - peak), 0.0)
    soft = shifted / jnp.sum(shifted, -1, keepdims=True)
    label = jnp.where(rows == 0, labels_ref[0], labels_ref[1])
    logit_grad = (soft - (lanes == label).astype(F32)).astype(BF16)
    logit_wide = logit_grad.astype(F32)
    back = jnp.zeros((16, D), F32)
    for cls in range(CLASSES):
        picked = jnp.sum(jnp.where(lanes == cls, logit_wide, 0.0), -1, keepdims=True)
        back = back + picked * row(CW + cls)
    pool_grad = (back * (1.0 - pooled * pooled)).astype(BF16)
    first_grad_ref[...] = nt(pool_grad, pool_weight)[0:8]
    padded = jnp.concatenate([logit_wide[0:2], jnp.zeros((2, D - 128), F32)], -1)
    ramp = jnp.concatenate(
        [first.astype(F32)[0:2], pool_grad.astype(F32)[0:2], wide[0:2], padded], 0
    ).astype(BF16)
    if layer:
        out_ref[0] = prior_out[...]
        logits_ref[0] = prior_logits[...]
        ramp_ref[0] = prior_ramp[...]
        out_ref[1] = output
        logits_ref[1] = logits[0:8]
        ramp_ref[1] = ramp
    else:
        out_ref[...] = output
        logits_ref[...] = logits[0:8]
        ramp_ref[...] = ramp
    wait_copies(leaving)


def ffn_forward(line, layer, labels, class_bias, x, normed, low, small, in_bias, weights, prior):
    tokens = low.shape[0]
    smem = pl.BlockSpec(memory_space=pltpu.SMEM)
    stack = (2,) if layer else ()
    return line.call(
        "ffn_forward%d" % layer,
        12,
        functools.partial(ffn_forward_kernel, layer),
        [(labels, smem), (class_bias, smem)]
        + near(x, normed, low, small, in_bias)
        + fixed(*weights)
        + near(*prior),
        sent(
            ((2, tokens, WIDE), BF16),
            ((3, tokens, WIDE), BF16),
            ((4, tokens, D), F32),
        )
        + made(
            ((tokens, D), F32),
            ((tokens, 1), F32),
            ((8, D), F32),
            ((*stack, tokens, D), BF16),
            ((*stack, 8, 128), F32),
            ((*stack, 8, D), BF16),
        ),
        [
            pltpu.VMEM((4, D, D), BF16),
            pltpu.VMEM((SHARDS, D, D), BF16),
            pltpu.VMEM((D, D), BF16),
            pltpu.VMEM((4, tokens, D), BF16),
            pltpu.VMEM((4, tokens, WIDE - D), BF16),
            pltpu.VMEM((4, tokens, D), F32),
            pltpu.SemaphoreType.DMA((48,)),
            pltpu.SemaphoreType.DMA((13,)),
        ],
    )


def ffn_backward_kernel(
    layer, grad_ref, first_ref, normed_two_ref, rstd_two_ref, slope_ref, normed_ref, rstd_ref,
    small, *refs
):
    pairs_ref, rows_ref, low_ref, smalls_ref, up, down, pairs, sems, out_sems = refs[-9:]
    downs, ups, _ = load_ffn_weights(refs[:-9], up, down, None, sems, True)

    def row(index):
        return small[layer, index : index + 1].astype(F32)

    grad = grad_ref[...].astype(F32)
    index = lax.broadcasted_iota(jnp.int32, grad.shape, 0)
    grad = grad + jnp.where(index == 0, first_ref[0:1], 0.0)
    grad = grad + jnp.where(index == SEQ, first_ref[1:2], 0.0)
    res_two, gain_two, shift_two = norm_back(grad, normed_two_ref[...], rstd_two_ref[...], row(G1))
    ffn_grad = res_two.astype(BF16)
    pairs[4] = ffn_grad
    leaving = run_copies([(pairs.at[4], pairs_ref.at[4])], out_sems, 4)
    wait_copies(downs)
    middle_grad = res_two
    for block in range(4):
        act_grad = nt(ffn_grad, down[block])
        pre_grad = (act_grad * slope_ref[block]).astype(BF16)
        pairs[block] = pre_grad
        leaving += run_copies([(pairs.at[block], pairs_ref.at[block])], out_sems, block)
        if block == 0:
            wait_copies(ups)
        smalls_ref[block : block + 1] = jnp.sum(pre_grad.astype(F32), 0, keepdims=True)
        middle_grad = middle_grad + nt(pre_grad, up[block])
    res_one, gain_one, shift_one = norm_back(middle_grad, normed_ref[...], rstd_ref[...], row(G0))
    rows_ref[...] = res_one
    low = res_one.astype(BF16)
    low_ref[...] = low
    smalls_ref[4:5] = jnp.sum(ffn_grad.astype(F32), 0, keepdims=True)
    smalls_ref[5:6] = jnp.sum(low.astype(F32), 0, keepdims=True)
    smalls_ref[6:7] = gain_one
    smalls_ref[7:8] = gain_two
    smalls_ref[8:9] = shift_one
    smalls_ref[9:10] = shift_two
    wait_copies(leaving)


def ffn_backward(
    line, layer, grad, first_grad, normed_two, rstd_two, slope, normed, rstd, small, weights
):
    tokens = grad.shape[0]
    return line.call(
        "ffn_backward%d" % layer,
        11,
        functools.partial(ffn_backward_kernel, layer),
        near(grad, first_grad, normed_two, rstd_two, slope, normed, rstd, small)
        + away(*weights),
        sent(((5, tokens, D), BF16))
        + made(
            ((tokens, D), F32),
            ((tokens, D), BF16),
            ((10, D), F32),
        ),
        [
            pltpu.VMEM((4, D, D), BF16),
            pltpu.VMEM((SHARDS, D, D), BF16),
            pltpu.VMEM((5, tokens, D), BF16),
            pltpu.SemaphoreType.DMA((32,)),
            pltpu.SemaphoreType.DMA((5,)),
        ],
    )


def place_pieces(groups, natural, outs, y, sems):
    here = quarter_index()
    pairs = []
    for index, (order, first, count) in enumerate(groups):
        keep_ref, send_ref = outs[2 * index : 2 * index + 2]
        rows = slice(first, first + count)
        for x in range(2):
            for a in range(2):
                if not order:
                    target, unit, place = (send_ref if y else keep_ref), 2 * a + x, 2 * a + x
                else:
                    bits = {"y": y, "x": x, "a": a}
                    outer, middle, inner = (bits[dim] for dim in order)
                    target = send_ref if outer else keep_ref
                    unit, place = (2 * a + x) ^ here, 2 * middle + inner
                pairs.append((natural.at[y, unit, rows], target.at[place]))
    return run_copies(pairs, sems, y * len(pairs))


def piece_shapes(groups):
    shapes = []
    for _, _, count in groups:
        shapes += [((4, count, D), BF16)] * 2
    return shapes


def ffn_weights_kernel(groups, act_ref, act_near_ref, pairs_ref, pairs_near_ref, *refs):
    outs, (natural, sems) = refs[:-2], refs[-2:]
    leaving = []
    for slot in (1, 0):
        mine, other = act_ref[slot], act_near_ref[slot]
        down = tn(mine[:, 0:D], pairs_ref[4]) + tn(other[:, 0:D], pairs_near_ref[4])
        down = down.astype(BF16)
        for block in range(4):
            natural[slot, block, PART : 2 * PART] = down[block * PART : (block + 1) * PART]
            up = tn(mine[:, D : D + PART], pairs_ref[block])
            up = up + tn(other[:, D : D + PART], pairs_near_ref[block])
            natural[slot, block, 0:PART] = up.astype(BF16)
        leaving += place_pieces(groups, natural, outs, slot, sems)
    wait_copies(leaving)


def ffn_weight_grads(line, layer, groups, act, act_near, pairs, pairs_near):
    return line.call(
        "ffn_weight_grads%d" % layer,
        8,
        functools.partial(ffn_weights_kernel, groups),
        near(act, act_near, pairs, pairs_near),
        sent(*piece_shapes(groups)),
        [pltpu.VMEM((2, 4, 2 * PART, D), BF16), pltpu.SemaphoreType.DMA((8 * len(groups),))],
    )


def attn_weights_kernel(
    groups, x_ref, acts_near_ref, grad_ref, pairs_ref, near_ref, *refs
):
    outs, (natural, sems) = refs[-2 - 2 * len(groups) : -2], refs[-2:]
    leaving = []
    cut = 3 * PART
    tokens = x_ref.shape[0]
    x_near = acts_near_ref[2, :, 0:D]
    grad_near = near_ref[2 * tokens : 3 * tokens]
    if len(refs) > 2 + 2 * len(groups):
        smalls_ref, by_shard = refs[0], refs[-3]
        outs = refs[1:-3]
        smalls = []
        for layer in range(LAYERS):
            start = 3 * tokens + 32 * layer
            high = near_ref[start : start + 16].astype(F32)
            rest = near_ref[start + 16 : start + 32].astype(F32)
            smalls.append(smalls_ref[layer] + (high + rest)[0:12])
        for part in range(SHARDS):
            lanes = slice(part * PART, (part + 1) * PART)
            for layer in range(LAYERS):
                row = 3 * layer
                by_shard[part, row : row + 1] = smalls[layer][part : part + 1]
                for item in range(8):
                    target = slice((item % 4) * PART, (item % 4 + 1) * PART)
                    value = smalls[layer][4 + item : 5 + item, lanes]
                    by_shard[part, row + 1 + item // 4 : row + 2 + item // 4, target] = value
            by_shard[part, 6:16] = jnp.zeros((10, D), F32)
        shard = shard_index()
        for slot in range(2):
            natural[slot, 0, PART:TALL] = by_shard[shard ^ (2 * slot)].astype(BF16)
            for unit in range(1, 4):
                natural[slot, unit, PART:TALL] = jnp.zeros((TALL - PART, D), BF16)
    for slot in (1, 0):
        mine, other = pairs_ref[slot], near_ref[slot * tokens : (slot + 1) * tokens]
        value = tn(mine[:, 0:cut], x_ref[...]) + tn(other[:, 0:cut], x_near)
        value = value.astype(BF16)
        for unit in range(3):
            natural[slot, unit, 0:PART] = value[unit * PART : (unit + 1) * PART]
        value = tn(mine[:, cut:D], grad_ref[...]) + tn(other[:, cut:D], grad_near)
        natural[slot, 3, 0:PART] = value.astype(BF16)
        leaving += place_pieces(groups, natural, outs, slot, sems)
    wait_copies(leaving)


def attn_weight_grads(line, layer, groups, *operands):
    return line.call(
        "attn_weight_grads%d" % layer,
        5,
        functools.partial(attn_weights_kernel, groups),
        near(*operands),
        sent(*piece_shapes(groups)),
        ([pltpu.VMEM((SHARDS, 16, D), F32)] if len(operands) > 5 else [])
        + [
            pltpu.VMEM((2, 4, groups[0][2], D), BF16),
            pltpu.SemaphoreType.DMA((8 * len(groups),)),
        ],
    )


def attn_backward_kernel(
    layer, res_ref, grad_ref, smalls_in_ref, *refs
):
    count = 10
    kept, weights, refs = refs[:6], refs[6:count], refs[count:]
    if layer == 0:
        prior, refs = refs[0], refs[1:]
    pairs_ref, pairs_send_ref, rows_ref, smalls_ref, slots, sems, sums = refs
    tokens = grad_ref.shape[0]
    copies = load_attn_weights(weights[:2], slots.at[0:2], sems)
    copies += load_attn_weights(weights[2:], slots.at[2:4], sems, 2)
    shard = shard_index()
    grad = grad_ref[...]
    total = res_ref[...]
    for slot in range(4):
        wait_copies(copies[slot])
        half, index = slot >> 1, slot & 1
        qkv_ref, probs_ref, context_ref = kept[3 * half : 3 * half + 3]
        context_grad = nt(grad, slots[slot, 3]).astype(BF16)
        places = [
            (
                slice(seq * SEQ, (seq + 1) * SEQ),
                slice(head * HEAD_DIM, (head + 1) * HEAD_DIM),
            )
            for seq in range(2)
            for head in range(PART // HEAD_DIM)
        ]
        query, key, val = (qkv_ref[index, part] for part in range(3))
        probs = probs_ref[index]
        prob_grad = jnp.stack([nt(context_grad[at], val[at]) for at in places])
        mean = jnp.sum(prob_grad * probs, -1, keepdims=True)
        score_grad = (probs * (prob_grad - mean)).astype(BF16)
        probs_low = probs.astype(BF16)
        scale = HEAD_DIM ** (-0.5)
        heads = [
            [nn(score_grad[i], key[at]) * scale for i, at in enumerate(places)],
            [tn(score_grad[i], query[at]) * scale for i, at in enumerate(places)],
            [tn(probs_low[i], context_grad[at]) for i, at in enumerate(places)],
        ]
        half_heads = len(places) // 2
        seq_rows = [
            [jnp.concatenate(group[:half_heads], -1), jnp.concatenate(group[half_heads:], -1)]
            for group in heads
        ]
        for part in range(3):
            value = jnp.concatenate(seq_rows[part], 0).astype(BF16)
            if slot & 1:
                rows = slice(half * tokens, (half + 1) * tokens)
                pairs_send_ref[rows, part * PART : (part + 1) * PART] = value
            else:
                pairs_ref[half, :, part * PART : (part + 1) * PART] = value
            if part != 1:
                sums[shard ^ slot, part // 2] = jnp.sum(value.astype(F32), 0, keepdims=True)
            total = total + nn(value, slots[slot, part])
        if slot & 1:
            pairs_send_ref[half * tokens : (half + 1) * tokens, 3 * PART : D] = context_ref[index]
        else:
            pairs_ref[half, :, 3 * PART : D] = context_ref[index]
    pairs_send_ref[2 * tokens : 3 * tokens] = grad
    rows_ref[...] = total.astype(rows_ref.dtype)
    own = [
        jnp.concatenate([sums[part, index] for part in range(SHARDS)], -1) for index in range(2)
    ]
    if layer:
        smalls_ref[0:10] = smalls_in_ref[...]
        smalls_ref[10:11] = own[0]
        smalls_ref[11:12] = own[1]
    else:
        smalls_ref[1] = prior[...]
        smalls_ref[0, 0:10] = smalls_in_ref[...]
        smalls_ref[0, 10:11] = own[0]
        smalls_ref[0, 11:12] = own[1]
        for index in range(LAYERS):
            value = smalls_ref[index]
            high = value.astype(BF16)
            rest = (value - high.astype(F32)).astype(BF16)
            start = 3 * tokens + 32 * index
            pairs_send_ref[start : start + 16] = jnp.concatenate(
                [high, jnp.zeros((4, D), BF16)], 0
            )
            pairs_send_ref[start + 16 : start + 32] = jnp.concatenate(
                [rest, jnp.zeros((4, D), BF16)], 0
            )


def attn_backward(line, layer, res, grad, kept, smalls, weights, prior):
    tokens = grad.shape[0]
    return line.call(
        "attn_backward%d" % layer,
        15,
        functools.partial(attn_backward_kernel, layer),
        near(res, grad, smalls, *kept) + away(*weights) + near(*prior),
        made(
            ((2, tokens, D), BF16),
            ((3 * tokens + (0 if layer else 64), D), BF16),
            ((tokens, D), F32 if layer else BF16),
            ((12, D) if layer else (2, 12, D), F32),
        ),
        [
            pltpu.VMEM((4, 4, PART, D), BF16),
            pltpu.SemaphoreType.DMA((12,)),
            pltpu.VMEM((SHARDS, 2, 1, PART), F32),
        ],
    )


def halve_kernel(keep_ref, came_ref, low_ref, high_ref):
    half = low_ref.shape[0]
    low_ref[...] = keep_ref[0:half] + came_ref[0:half]
    high_ref[...] = keep_ref[half:] + came_ref[half:]


def add_kernel(keep_ref, came_ref, sum_ref):
    sum_ref[...] = keep_ref[...] + came_ref[...]


def reduction(line, moves, name, order, back, keep, send):
    shape = keep.shape
    micros = 1 + shape[1] / 192
    if not order:
        came = moves("y", send)
        yield
        total = line.call(
            "add_%s" % name, micros, add_kernel, near(keep, came), made((shape, BF16))
        )[0]
        yield (back, lax.psum(total, "dp"))
    came = moves(order[0], send)
    for step, dim in enumerate(order[1:]):
        yield
        half = (keep.shape[0] // 2, *shape[1:])
        keep, send = line.call(
            "halve_%s%d" % (name, step), micros, halve_kernel, near(keep, came),
            made((half, BF16), (half, BF16)),
        )
        came = moves(dim, send)
    yield
    keep, came = keep[0], came[0]
    total = line.call(
        "add_%s" % name, micros, add_kernel, near(keep, came), made((shape[1:], BF16))
    )[0]
    came = moves("b", total)
    for bit in moves.more():
        yield
        total = line.call(
            "more_%s%d" % (name, bit), micros, add_kernel, near(total, came),
            made((shape[1:], BF16)),
        )[0]
        came = moves.place(bit, total)
    yield
    total = line.call(
        "last_%s" % name, micros, add_kernel, near(total, came), made((shape[1:], BF16))
    )[0]
    came = moves(back[0], total)
    yield
    both = line.call(
        "both_%s" % name, micros, both_kernel, near(total, came), made(((2, *shape[1:]), BF16))
    )[0]
    yield (back, both, moves(back[1], both))


def join_kernel(one_ref, two_ref, joint_ref):
    count = one_ref.shape[0]
    joint_ref[0:count] = one_ref[...]
    joint_ref[count : 2 * count] = two_ref[...]


def join(line, one, two):
    shape = (2 * one.shape[0], *one.shape[1:])
    return line.call("join%d" % shape[0], 1, join_kernel, near(one, two), made((shape, BF16)))[0]


def both_kernel(one_ref, two_ref, both_ref):
    both_ref[0] = one_ref[...]
    both_ref[1] = two_ref[...]


def unpack_kernel(back, first, targets, prior, *refs):
    values = 2 if back else 1
    quarters = refs[:values]
    outs = refs[values + prior : -2]
    whole, sems = refs[-2:]
    here = quarter_index()
    count = whole.shape[1]
    for index in range(4):
        if not back:
            whole[index] = quarters[0][index, first : first + count].astype(F32)
            continue
        bits = {back[0]: index & 1, back[1]: index >> 1}
        relative = 2 * bits["a"] + bits["x"]
        quarter = quarters[index >> 1][index & 1, first : first + count]
        whole[relative ^ here] = quarter.astype(F32)
    if count == TALL:
        qkv_bias, out_bias, gain, shift, in_bias, down_bias = outs[len(targets) :]
        for layer in range(LAYERS):
            row = PART + 3 * layer

            def item(index):
                at = row + 1 + index // 4
                return whole[0, at : at + 1, (index % 4) * PART : (index % 4 + 1) * PART]

            in_bias[layer : layer + 1] = whole[0, row : row + 1]
            down_bias[layer : layer + 1] = item(0)
            out_bias[layer : layer + 1] = item(1)
            for index in range(2):
                gain[layer, index : index + 1] = item(2 + index)
                shift[layer, index : index + 1] = item(4 + index)
                qkv_bias[layer, index : index + 1] = item(6 + index)
    pairs = [
        (whole.at[unit, 0:PART], outs[which].at[where])
        for unit, which, where in targets_of(targets)
    ]
    wait_copies(run_copies(pairs, sems, 0))


def targets_of(targets):
    return [(unit, which, where) for which, places in enumerate(targets) for unit, where in places]


SMALL_SHAPES = (
    (LAYERS, 2, PART), (LAYERS, PART), (LAYERS, 2, PART), (LAYERS, 2, PART), (LAYERS, D), (LAYERS, PART)
)


def unpack(line, name, quarters, first, shapes, targets, prior):
    back, *values = quarters
    aliases = {len(values) + index: index for index in range(len(prior))}
    count = TALL if values[0].shape[1] == TALL else PART
    outs = [(shape, F32, anywhere()) for shape in shapes]
    if count == TALL:
        outs += made(*[(shape, F32) for shape in SMALL_SHAPES])
    return line.call(
        name,
        3,
        functools.partial(unpack_kernel, back, first, targets, len(prior)),
        near(*values) + away(*prior),
        outs,
        [pltpu.VMEM((4, count, D), F32), pltpu.SemaphoreType.DMA((4,))],
        aliases,
    )


def unpack_up(line, layer, quarters, first, prior):
    places = [(unit, (layer, slice(None), slice(unit * D, (unit + 1) * D))) for unit in range(4)]
    return unpack(
        line, "unpack_up%d" % layer, quarters, first, [(LAYERS, PART, FF)], [places], prior
    )


def unpack_down(line, layer, quarters, first, prior):
    places = [(unit, (layer, slice(unit * PART, (unit + 1) * PART))) for unit in range(4)]
    return unpack(
        line, "unpack_down%d" % layer, quarters, first, [(LAYERS, D, D)], [places], prior
    )


def unpack_attn(line, layer, quarters, first, prior):
    return unpack(
        line,
        "unpack_attn%d" % layer,
        quarters,
        first,
        [(LAYERS, 3, PART, D), (LAYERS, PART, D)],
        [[(unit, (layer, unit)) for unit in range(3)], [(3, (layer,))]],
        prior,
    )


def pool_grads(ramp, shard):
    ramp = ramp.reshape(ramp.shape[0], LAYERS, 4, 2, D)
    ramp = jnp.transpose(ramp, (1, 2, 0, 3, 4)).reshape(LAYERS, 4, -1, D)
    first, pool_grad, pooled, logit_grad = (ramp[:, part] for part in range(4))
    logit_grad = logit_grad[:, :, 0:CLASSES]
    own_first = lax.dynamic_slice_in_dim(first, shard * PART, PART, 2)
    own_pooled = lax.dynamic_slice_in_dim(pooled, shard * PART, PART, 2)
    pool_weight_grad = jnp.einsum("lnd,lne->lde", own_first, pool_grad, preferred_element_type=F32)
    class_weight_grad = jnp.einsum(
        "lnd,lnc->ldc", own_pooled, logit_grad, preferred_element_type=F32
    )
    class_bias_grad = jnp.sum(logit_grad.astype(F32), 1)
    own_pool = lax.dynamic_slice_in_dim(pool_grad, shard * PART, PART, 2)
    pool_bias_grad = jnp.sum(own_pool.astype(F32), 1)
    return pool_weight_grad, pool_bias_grad, class_weight_grad, class_bias_grad


ROUTES = {
    "f1": ("yxa", "ax"),
    "a1": ("axy", "ax"),
    "f0": ("axy", "xa"),
    "a0": ("xya", "xa"),
}
SCHEDULE = (
    "R0", "F1", "R1", "A1", "R1", "FW1", "R1", "AW1", "R1", "F0", "R1", "A0", "P1", "FW0",
    "AW0", "a1", "f1", "a0", "a1", "a0", "f0", "a1", "f1", "a1", "a0", "f1", "a0", "f0", "a1",
    "a0", "f0", "Ua1", "f1", "Ua0", "f0", "f1", "f0", "Uf1", "Uf0",
)


def on_device(
    mesh,
    hidden_in,
    out_cotangent,
    labels,
    qkv_weight,
    qkv_bias,
    out_weight,
    out_bias,
    norm_gain,
    norm_shift,
    ffn_in,
    ffn_in_bias,
    ffn_out,
    ffn_out_bias,
    pool_weight,
    pool_bias,
    class_weight,
    class_bias,
):
    moves = Moves(mesh)
    line = Line()
    shard = shard_index()
    qkv_turned = jnp.swapaxes(qkv_weight, 2, 3)

    packed = line.call(
        "pack_small",
        1,
        pack_small_kernel,
        near(
            qkv_bias, out_bias, norm_gain, norm_shift, ffn_in_bias, ffn_out_bias, pool_bias,
            jnp.transpose(class_weight, (2, 0, 1)),
        ),
        made(((LAYERS, 16, PART), F32)),
    )[0]
    first_pack, ffn_quarter = pack_ffn(line, 0, ffn_in, ffn_out, pool_weight)
    ffn_far = [Spread(line, moves, ffn_quarter, "x")]
    own = pack_attn(line, 0, qkv_turned, out_weight)
    attn_own = [[own, moves("c", own)]]
    class_bias_wide = class_bias.astype(F32)
    shard_small, small, in_bias = arrange(line, moves, packed)

    far = moves("y", line.gate(attn_own[0][0])[0])

    x = hidden_in
    kept, nears = [], []
    prior = ()
    for layer in range(LAYERS):
        *attn_near, total = attn_forward(line, layer, 0, x, (shard_small,), attn_own[layer])
        if layer == 0:
            ffn_far[0].second()
            ffn_pack, ffn_quarter = pack_ffn(line, 1, ffn_in, ffn_out, pool_weight)
            ffn_far.append(Spread(line, moves, ffn_quarter, "a"))
            ffn_far[0].third()
            far, first_pack = line.gate(far, first_pack)
            ffn_own = [[first_pack, moves("c", first_pack)]]
            attn_far = [[far, moves("c", far)]]
        else:
            far, ffn_pack = line.gate(far, ffn_pack)
            ffn_own.append([ffn_pack, moves("c", ffn_pack)])
            attn_far.append([far, moves("c", far)])
        *attn_rest, normed, rstd, low = attn_forward(
            line, layer, 1, x, (shard_small, small, total), attn_far[layer]
        )
        if layer == 0:
            line.waits = (*line.waits, ffn_own[0][1], ffn_far[0].stack)
            own = pack_attn(line, 1, qkv_turned, out_weight)
            ffn_far[1].second()
            far = moves("y", line.gate(own)[0])
            ffn_far[0].fourth()
            attn_own.append([own, moves("c", own)])
            line.waits = (*line.waits, attn_own[1][1])
            ffn_weights = [ffn_own[0] + ffn_far[0].pieces()]
        else:
            line.waits = (*line.waits, nears[0])
            ffn_far[1].fourth()
            ffn_weights.append(ffn_own[1] + ffn_far[1].pieces())
        act, act_send, slope, normed_two, rstd_two, first_grad, *prior = ffn_forward(
            line, layer, labels, class_bias_wide, x, normed, low, small, in_bias,
            ffn_weights[layer], prior,
        )
        if layer == 0:
            ffn_far[1].third()
        act_near = moves("c", act_send)
        nears.append(act_near)
        kept.append(
            (
                x,
                (attn_near + attn_rest, normed, rstd),
                (act, act_near),
                (slope, normed_two, rstd_two, first_grad),
            )
        )
        x = prior[0]
    block_outputs, logits, ramp = prior

    chains, results, state = {}, {}, {"grad": out_cotangent, "prior": ()}
    ramp_value = [ramp[None]]
    ramp_steps = [("head", 1), ("head", 2)]
    bit = 1
    while bit < mesh.shape["dp"]:
        ramp_steps.append(("dp", bit))
        bit *= 2

    def begin(names, pieces):
        for index, name in enumerate(names):
            keep, send = pieces[2 * index : 2 * index + 2]
            chains[name] = reduction(line, moves, name, *ROUTES[name], keep, send)
            next(chains[name])

    def step(name):
        layer = int(name[-1])
        if name == "R0":
            ramp_value[0] = line.gate(ramp_value[0])[0]
        elif name[:-1] == "F":
            _, (_, normed, rstd), _, (slope, normed_two, rstd_two, first_grad) = kept[layer]
            pairs, res, low, rows = ffn_backward(
                line, layer, state["grad"], first_grad, normed_two, rstd_two, slope, normed, rstd,
                small, ffn_weights[layer],
            )
            state["ffn"] = (pairs, moves("c", pairs))
            state["low"] = low
            state["res"], state["rows"] = res, rows
            line.waits = (*line.waits, nears[layer])
        elif name[:-1] == "A":
            pairs, send, grad, smalls = attn_backward(
                line, layer, state["res"], state["low"], kept[layer][1][0], state["rows"],
                attn_own[layer] + attn_far[layer], state["prior"],
            )
            state["attn"] = (pairs, moves("c", send))
            state["grad"], state["prior"] = grad, (smalls,)
        elif name[:-1] == "FW":
            names = [key for key in ROUTES if key[-1] == name[-1] and key[0] != "a"]
            spans = {"f": (0, 2 * PART), "u": (0, PART), "d": (PART, PART)}
            groups = [(ROUTES[key][0], *spans[key[0]]) for key in names]
            begin(names, ffn_weight_grads(line, layer, groups, *kept[layer][2], *state["ffn"]))
        elif name[:-1] == "AW":
            key = "a" + name[-1]
            groups = [(ROUTES[key][0], 0, PART if layer else TALL)]
            operands = (kept[layer][0], kept[layer][2][1], state["low"], *state["attn"])
            if layer == 0:
                operands += state["prior"]
            begin([key], attn_weight_grads(line, layer, groups, *operands))
        elif name == "R1":
            for _ in range(max(1, len(ramp_steps) - 4)):
                axis, bit = ramp_steps.pop(0)
                came = lax.ppermute(ramp_value[0], AXES, flip(mesh, axis, bit))
                ramp_value[0] = join(line, ramp_value[0], came)
        elif name == "P1":
            state["pool"] = pool_grads(ramp_value[0], shard)
            line.waits = (*line.waits, *state["pool"])
        elif name[0] == "U":
            key = name[1:]
            while key not in results:
                results[key] = next(chains[key])
                if results[key] is None:
                    del results[key]
            if key[0] in "uf":
                state["up"] = unpack_up(line, layer, results[key], 0, state.get("up", ()))
            if key[0] in "df":
                first = PART if key[0] == "f" else 0
                state["down"] = unpack_down(line, layer, results[key], first, state.get("down", ()))
            if key[0] == "a":
                state["attn_out"] = unpack_attn(
                    line, layer, results[key], 0, state.get("attn_out", ())
                )
        else:
            result = next(chains[name], None)
            if result is not None:
                results[name] = result

    for name in SCHEDULE:
        step(name)
    qkv_grad, out_grad, qkv_bias_grad, out_bias_grad, *smalls = state["attn_out"]
    gain_grad, shift_grad, in_bias_grad, down_bias_grad = smalls
    pool_weight_grad, pool_bias_grad, class_weight_grad, class_bias_grad = state["pool"]
    return (
        block_outputs,
        logits[:, 0:2, 0:CLASSES],
        state["grad"],
        jnp.swapaxes(qkv_grad, 2, 3),
        qkv_bias_grad,
        out_grad,
        out_bias_grad,
        gain_grad,
        shift_grad,
        state["up"][0],
        in_bias_grad,
        state["down"][0],
        down_bias_grad,
        pool_weight_grad,
        pool_bias_grad,
        class_weight_grad,
        class_bias_grad,
    )


def solution(mesh):
    return jax.shard_map(
        functools.partial(on_device, mesh),
        mesh=mesh,
        in_specs=(
            P(("dp", "head"), None),
            P(("dp", "head"), None),
            P(("dp", "head")),
            P(None, None, None, "head"),
            P(None, None, "head"),
            P(None, "head", None),
            P(None, "head"),
            P(None, None, "head"),
            P(None, None, "head"),
            P(None, "head", None),
            P(None, "head"),
            P(None, "head", None),
            P(None, "head"),
            P(None, "head", None),
            P(None, "head"),
            P(None, "head", None),
            P(),
        ),
        out_specs=(
            P(None, ("dp", "head"), None),
            P(None, ("dp", "head"), None),
            P(("dp", "head"), None),
            P(None, None, None, "head"),
            P(None, None, "head"),
            P(None, "head", None),
            P(None, "head"),
            P(None, None, "head"),
            P(None, None, "head"),
            P(None, "head", None),
            P(None, "head"),
            P(None, "head", None),
            P(None, "head"),
            P(None, "head", None),
            P(None, "head"),
            P(None, "head", None),
            P(),
        ),
        check_vma=False,
    )
```

```python
import functools

import jax
import jax.numpy as jnp
from jax import lax
from jax.experimental import pallas as pl
from jax.experimental.pallas import tpu as pltpu
from jax.sharding import PartitionSpec as P

D = 768
FF = 3072
HEAD_DIM = 64
SEQ = 128
LAYERS = 2
SHARDS = 4
PART = D // SHARDS
POOL_PART = PART // 4
CLASSES = 3
EPS = 1e-12
ROOT_HALF = 0.7071067811865476
DENSITY_SCALE = 0.3989422804014327
F32 = jnp.float32
BF16 = jnp.bfloat16
AXES = ("dp", "head")
VMEM_LIMIT = 58 * 1024 * 1024
TALL = PART + 16
FFN_ROWS = 2 * PART + POOL_PART
WIDE = 1024

QB, VB, OB, G0, G1, S0, S1, FB, PB, CW = 0, 1, 2, 3, 4, 5, 6, 11, 12, 13


def dot(left, right, dims):
    return lax.dot_general(left, right, ((dims[:1], dims[1:]), ((), ())), preferred_element_type=F32)


def nn(left, right):
    return dot(left, right, (1, 0))


def nt(left, right):
    return dot(left, right, (1, 1))


def tn(left, right):
    return dot(left, right, (0, 0))


def normalise(resid):
    centred = resid - jnp.mean(resid, -1, keepdims=True)
    rstd = lax.rsqrt(jnp.mean(centred * centred, -1, keepdims=True) + EPS)
    return centred * rstd, rstd


def norm_back(incoming, normed, rstd, gain):
    scaled = incoming * gain
    back = rstd * (
        scaled
        - jnp.mean(scaled, -1, keepdims=True)
        - normed * jnp.mean(scaled * normed, -1, keepdims=True)
    )
    gain_grad = jnp.sum(incoming * normed, 0, keepdims=True)
    shift_grad = jnp.sum(incoming, 0, keepdims=True)
    return back, gain_grad, shift_grad


def cost(micros):
    return pl.CostEstimate(flops=int(micros * 1e10), bytes_accessed=0, transcendentals=0)


def shard_index():
    return lax.axis_index("head")


def quarter_index():
    return lax.axis_index("dp") & 3


def rows_at(index, count):
    return pl.ds(pl.multiple_of(index * count, count), count)


def vmem():
    return pl.BlockSpec(memory_space=pltpu.VMEM)


def anywhere():
    return pl.BlockSpec(memory_space=pl.ANY)


ROOM = {
    "pack": 14, "arrange": 4, "attn_forward": 18, "ffn_forward": 30, "ffn_backward": 32,
    "attn_backward": 24, "ffn_weight": 20, "attn_weight": 16, "halve": 14, "unpack": 14,
}


def room(name):
    for start, size in ROOM.items():
        if name.startswith(start):
            return size << 20
    return 8 << 20


TOKEN = jax.ShapeDtypeStruct((8, 128), F32)


def main_memory():
    return pl.BlockSpec(memory_space=pltpu.HBM)


class Line:
    def __init__(self):
        self.waits = ()

    def call(self, name, micros, kernel, ins, outs, scratch=(), aliases=None):
        waits = tuple(self.waits)
        count, total = len(ins), len(ins) + len(waits) + len(outs)

        def body(*refs):
            kernel(*refs[:count], *refs[count + len(waits) : total], *refs[total + 1 :])

        *result, token = pl.pallas_call(
            body,
            out_shape=[jax.ShapeDtypeStruct(shape, dtype) for shape, dtype, _ in outs] + [TOKEN],
            in_specs=[spec for _, spec in ins] + [main_memory()] * len(waits),
            out_specs=[spec for _, _, spec in outs] + [main_memory()],
            scratch_shapes=list(scratch),
            input_output_aliases=aliases or {},
            compiler_params=pltpu.CompilerParams(vmem_limit_bytes=room(name)),
            cost_estimate=cost(micros),
            name=name,
        )(*[value for value, _ in ins], *waits)
        self.waits = (token,)
        return result

    def gate(self, *values):
        outs = [(value.shape, value.dtype, anywhere()) for value in values]
        aliases = {index: index for index in range(len(values))}
        return self.call("gate", 10, lambda *refs: None, away(*values), outs, aliases=aliases)


def near(*values):
    return [(value, vmem()) for value in values]


def fixed(*values):
    return [(value, main_memory()) for value in values]


def away(*values):
    return [(value, anywhere()) for value in values]


def made(*shapes):
    return [(shape, dtype, vmem()) for shape, dtype in shapes]


def sent(*shapes):
    return [(shape, dtype, anywhere()) for shape, dtype in shapes]


def run_copies(pairs, sems, start):
    copies = [
        pltpu.make_async_copy(src, dst, sems.at[start + index])
        for index, (src, dst) in enumerate(pairs)
    ]
    for item in copies:
        item.start()
    return copies


def wait_copies(copies):
    for item in copies:
        item.wait()


def flip(mesh, axis, bit):
    dp, head = mesh.shape["dp"], mesh.shape["head"]
    pairs = []
    for place in range(dp):
        for shard in range(head):
            to_place = place ^ bit if axis == "dp" else place
            to_shard = shard ^ bit if axis == "head" else shard
            pairs.append((place * head + shard, to_place * head + to_shard))
    return pairs


DIMS = {"c": ("head", 1), "y": ("head", 2), "d": ("head", 3), "x": ("dp", 1), "a": ("dp", 2), "b": ("dp", 4)}


class Moves:
    def __init__(self, mesh):
        self.mesh = mesh

    def __call__(self, dim, value):
        return lax.ppermute(value, AXES, flip(self.mesh, *DIMS[dim]))

    def more(self):
        bit = 8
        while bit < self.mesh.shape["dp"]:
            yield bit
            bit *= 2

    def place(self, bit, value):
        return lax.ppermute(value, AXES, flip(self.mesh, "dp", bit))


def stack_kernel(one, two, follow, follow_out, stack_ref, sems, *, order):
    refs = {"one": one, "two": two, "follow": follow}
    pairs = [(refs[name], stack_ref.at[index]) for index, name in enumerate(order)]
    wait_copies(run_copies(pairs, sems, 0))


class Spread:
    def __init__(self, line, moves, quarter, last):
        self.line, self.moves, self.last = line, moves, last
        self.far = [moves("y", quarter)]

    def second(self):
        self.far = list(self.line.gate(*self.far))
        self.far += [self.moves("x", self.far[0]), self.moves("a", self.far[0])]

    def third(self):
        follow = 2 if self.last == "x" else 1
        shape = self.far[0].shape
        order = ("one", "two", "follow") if follow == 2 else ("one", "follow", "two")
        operands = (self.far[0], self.far[3 - follow], self.far[follow])
        self.far[follow], stack = self.line.call(
            "stack",
            3,
            functools.partial(stack_kernel, order=order),
            fixed(*operands),
            [(shape, BF16, main_memory()), ((3, *shape), BF16, vmem())],
            [pltpu.SemaphoreType.DMA((3,))],
            {2: 0},
        )
        self.stack = self.moves("c", stack)
        self.far.append(self.moves(self.last, self.far[follow]))

    def fourth(self):
        self.far[3] = self.line.gate(self.far[3])[0]
        self.near = self.moves("c", self.far[3])

    def pieces(self):
        return [*self.far, self.stack, self.near]


def pack_attn_kernel(qkv_ref, out_ref, *refs):
    *whole_refs, quarter_ref, sems = refs
    pairs = []
    for index, own_ref in enumerate(whole_refs):
        layer = index % 2
        pairs += [(qkv_ref.at[layer], own_ref.at[0:3]), (out_ref.at[layer], own_ref.at[3])]
    copies = run_copies(pairs, sems, 0)
    wait_copies(copies[:2])
    quarter_ref[...] = whole_refs[0][quarter_index()]
    wait_copies(copies[2:])


def pack_attn(line, qkv, out):
    whole = ((4, PART, D), BF16)
    return line.call(
        "pack_attn",
        2,
        pack_attn_kernel,
        fixed(qkv, out),
        made(whole, whole, whole, whole, ((PART, D), BF16)),
        [pltpu.SemaphoreType.DMA((8,))],
    )


def pack_ffn_kernel(layer, in_ref, down_ref, pool_ref, own_ref, quarter_ref, sems):
    pairs = []
    for index in range(4):
        target = own_ref.at[index]
        pairs += [
            (in_ref.at[layer, :, index * D : (index + 1) * D], target.at[0:PART]),
            (
                down_ref.at[layer, index * PART : (index + 1) * PART],
                target.at[PART : 2 * PART],
            ),
            (
                pool_ref.at[layer, index * POOL_PART : (index + 1) * POOL_PART],
                target.at[2 * PART : FFN_ROWS],
            ),
        ]
    wait_copies(run_copies(pairs, sems, 0))
    quarter_ref[...] = own_ref[quarter_index()]


def pack_ffn(line, layer, ffn_in, ffn_out, pool):
    return line.call(
        "pack_ffn%d" % layer,
        3,
        functools.partial(pack_ffn_kernel, layer),
        fixed(ffn_in, ffn_out, pool),
        made(((4, FFN_ROWS, D), BF16), ((FFN_ROWS, D), BF16)),
        [pltpu.SemaphoreType.DMA((12,))],
    )


def pack_small_kernel(
    qkv_bias, out_bias, gain, shift, in_bias, down_bias, pool_bias, class_weight, packed_ref
):
    for layer in range(LAYERS):
        packed_ref[layer, QB : VB + 1] = qkv_bias[layer].astype(F32)
        packed_ref[layer, OB : OB + 1] = out_bias[layer : layer + 1].astype(F32)
        packed_ref[layer, G0 : G1 + 1] = gain[layer].astype(F32)
        packed_ref[layer, S0 : S1 + 1] = shift[layer].astype(F32)
        for index in range(4):
            value = in_bias[layer : layer + 1, index * PART : (index + 1) * PART]
            packed_ref[layer, 7 + index : 8 + index] = value.astype(F32)
        packed_ref[layer, FB : FB + 1] = down_bias[layer : layer + 1].astype(F32)
        packed_ref[layer, PB : PB + 1] = pool_bias[layer : layer + 1].astype(F32)
        for cls in range(CLASSES):
            value = class_weight[cls, layer : layer + 1].astype(F32)
            packed_ref[layer, CW + cls : CW + cls + 1] = value


def arrange_kernel(own, core, row, both, shards_ref, small_ref, bias_ref):
    shard = shard_index()
    for slot, ref in enumerate((own, core, row, both)):
        shards_ref[shard ^ slot] = ref[...]
    for part in range(SHARDS):
        for layer in range(LAYERS):
            lanes = slice(part * PART, (part + 1) * PART)
            small_ref[layer, :, lanes] = shards_ref[part, layer]
            for index in range(4):
                target = slice(index * PART, (index + 1) * PART)
                value = shards_ref[part, layer, 7 + index : 8 + index]
                bias_ref[layer, part : part + 1, target] = value


def arrange(line, moves, packed):
    core, row = moves("c", packed), moves("y", packed)
    return line.call(
        "arrange",
        1,
        arrange_kernel,
        near(packed, core, row, moves("d", packed)),
        made(
            ((SHARDS, LAYERS, 16, PART), F32),
            ((LAYERS, 16, D), F32),
            ((LAYERS, SHARDS, D), F32),
        ),
    )


def load_attn_weights(refs, slots, sems, start=0):
    here = quarter_index()
    copies = []
    for slot in range(2):
        if len(refs) == 2:
            pairs = [(refs[slot], slots.at[slot])]
        else:
            pieces = refs[0:4] if slot == 0 else [refs[4].at[0], refs[4].at[1], refs[4].at[2], refs[5]]
            pairs = [(piece, slots.at[slot, here ^ index]) for index, piece in enumerate(pieces)]
        copies.append(run_copies(pairs, sems, start + len(pairs) * slot))
    return copies


def attn_forward_kernel(layer, half, x_ref, *refs):
    if half:
        (shard_small, small, total_in), refs = refs[:3], refs[3:]
        count = 2 if layer or "pair0" not in FORWARD else 6
        weights, refs = refs[:count], refs[count:]
        qkv_ref, probs_ref, context_ref, normed_ref, rstd_ref, low_ref, slots, sems = refs
    else:
        shard_small, weights, refs = refs[0], refs[1:3], refs[3:]
        qkv_ref, probs_ref, context_ref, total_ref, slots, sems = refs
    copies = load_attn_weights(weights, slots, sems)
    shard = shard_index()
    x = x_ref[...]
    if half:
        total = total_in[...] + small[layer, OB : OB + 1].astype(F32)
    else:
        total = x.astype(F32)
    for slot in range(2):
        wait_copies(copies[slot])
        biases = shard_small[shard ^ (2 * half + slot), layer]
        parts = []
        for part in range(3):
            value = nt(x, slots[slot, part])
            if part != 1:
                row = QB if part == 0 else VB
                value = value + biases[row : row + 1].astype(F32)
            value = value.astype(BF16)
            qkv_ref[slot, part] = value
            parts.append(value)
        query, key, val = parts
        places = [
            (
                slice(seq * SEQ, (seq + 1) * SEQ),
                slice(head * HEAD_DIM, (head + 1) * HEAD_DIM),
            )
            for seq in range(2)
            for head in range(PART // HEAD_DIM)
        ]
        scores = jnp.stack([nt(query[at], key[at]) for at in places]) * HEAD_DIM ** (-0.5)
        shifted = jnp.exp(scores - jnp.max(scores, -1, keepdims=True))
        probs = shifted * (1.0 / jnp.sum(shifted, -1, keepdims=True))
        probs_ref[slot] = probs
        low = probs.astype(BF16)
        heads = [nn(low[index], val[at]) for index, at in enumerate(places)]
        half_heads = len(heads) // 2
        context = jnp.concatenate(
            [
                jnp.concatenate(heads[:half_heads], -1),
                jnp.concatenate(heads[half_heads:], -1),
            ],
            0,
        ).astype(BF16)
        context_ref[slot] = context
        total = total + nn(context, slots[slot, 3])
    if half == 0:
        total_ref[...] = total
        return
    normed, rstd = normalise(total)
    normed_ref[...] = normed
    rstd_ref[...] = rstd
    middle = normed * small[layer, G0 : G0 + 1].astype(F32) + small[layer, S0 : S0 + 1].astype(F32)
    low_ref[...] = middle.astype(BF16)


def attn_forward(line, layer, half, x, inputs, weights):
    tokens = x.shape[0]
    outs = [
        ((2, 3, tokens, PART), BF16),
        ((2, 6, SEQ, SEQ), F32),
        ((2, tokens, PART), BF16),
        ((tokens, D), F32),
    ]
    if half:
        outs += [((tokens, 1), F32), ((tokens, D), BF16)]
    return line.call(
        "attn_forward%d%d" % (layer, half),
        7,
        functools.partial(attn_forward_kernel, layer, half),
        near(x, *inputs) + fixed(*weights),
        made(*outs),
        [pltpu.VMEM((2, 4, PART, D), BF16), pltpu.SemaphoreType.DMA((8,))],
    )


def load_ffn_weights(refs, up, down, pool, sems, down_first=False):
    here = quarter_index()
    shard = shard_index()
    ups, downs, pools = [], [], []

    def block_of(source, owner, block):
        ups.append((source.at[0:PART], up.at[block, rows_at(owner, PART)]))
        downs.append((source.at[PART : 2 * PART], down.at[owner, rows_at(block, PART)]))
        if pool is not None:
            target = pool.at[rows_at(owner * 4 + block, POOL_PART)]
            pools.append((source.at[2 * PART : FFN_ROWS], target))

    wholes = refs if len(refs) == 4 else refs[:2]
    for slot, whole in enumerate(wholes):
        for block in range(4):
            block_of(whole.at[block], shard ^ slot, block)
    if len(refs) == 8:
        pieces = [*refs[2:6], refs[6].at[0], refs[6].at[1], refs[6].at[2], refs[7]]
        for index, piece in enumerate(pieces):
            block_of(piece, shard ^ (2 + index // 4), here ^ (index % 4))
    order = (downs, ups, pools) if down_first else (ups, downs, pools)
    first = run_copies(order[0], sems, 0)
    second = run_copies(order[1], sems, len(ups))
    return first, second, run_copies(pools, sems, 2 * len(ups))


def ffn_forward_kernel(
    layer, labels_ref, class_bias_ref, x_ref, normed_ref, low_ref, small, in_bias, *refs
):
    count = 8
    weights, refs = refs[:count], refs[count:]
    if layer:
        (prior_out, prior_logits, prior_ramp), refs = refs[:3], refs[3:]
    act_ref, act_send_ref, slope_ref, normed_two_ref, rstd_two_ref, first_grad_ref = refs[:6]
    out_ref, logits_ref, ramp_ref, up, down, pool, acts, lows, slopes, sems, out_sems = refs[6:]
    ups, downs, pools = load_ffn_weights(weights, up, down, pool, sems)
    leaving = run_copies([(x_ref, act_send_ref.at[2, :, 0:D])], out_sems, 0)
    normed = normed_ref[...]
    low = low_ref[...]

    def row(index):
        return small[layer, index : index + 1].astype(F32)

    total = normed * row(G0) + row(S0) + row(FB)
    for part in range(4):
        lows[part, :, 0:PART] = low[:, part * PART : (part + 1) * PART]
        lows[part, :, PART:] = jnp.zeros((low.shape[0], WIDE - D - PART), BF16)
    wait_copies(ups)
    for block in range(4):
        pre_act = nn(low, up[block]) + in_bias[layer, block : block + 1].astype(F32)
        cumulative = 0.5 * (1.0 + lax.erf(pre_act * ROOT_HALF))
        act = (pre_act * cumulative).astype(BF16)
        density = jnp.exp(-0.5 * pre_act * pre_act) * DENSITY_SCALE
        acts[block] = act
        slopes[block] = cumulative + pre_act * density
        leaving += run_copies([(slopes.at[block], slope_ref.at[block])], out_sems, 1 + block)
        if block == 0:
            wait_copies(downs)
        total = total + nn(act, down[block])
    shard = shard_index()
    pairs = []
    for slot in range(4):
        target = (act_send_ref if slot & 1 else act_ref).at[slot >> 1]
        pairs.append((acts.at[shard ^ slot], target.at[:, 0:D]))
        pairs.append((lows.at[shard ^ slot], target.at[:, D:WIDE]))
    leaving += run_copies(pairs, out_sems, 5)
    wait_copies(pools)
    normed_two, rstd_two = normalise(total)
    normed_two_ref[...] = normed_two
    rstd_two_ref[...] = rstd_two
    output = (normed_two * row(G1) + row(S1)).astype(BF16)

    first = jnp.concatenate([output[0:1], output[SEQ : SEQ + 1]], 0).astype(F32)
    first = jnp.concatenate([first, jnp.zeros((14, D), F32)], 0).astype(BF16)
    pool_weight = pool[...]
    pooled = jnp.tanh(nn(first, pool_weight) + row(PB))
    wide = pooled.astype(BF16).astype(F32)
    lanes = lax.broadcasted_iota(jnp.int32, (16, 128), 1)
    rows = lax.broadcasted_iota(jnp.int32, (16, 128), 0)
    logits = jnp.zeros((16, 128), F32)
    for cls in range(CLASSES):
        value = jnp.sum(wide * row(CW + cls), -1, keepdims=True)
        value = value + class_bias_ref[layer, cls]
        logits = jnp.where(lanes == cls, value, logits)
    valid = lanes < CLASSES
    peak = jnp.max(jnp.where(valid, logits, -jnp.inf), -1, keepdims=True)
    shifted = jnp.where(valid, jnp.exp(logits - peak), 0.0)
    soft = shifted / jnp.sum(shifted, -1, keepdims=True)
    label = jnp.where(rows == 0, labels_ref[0], labels_ref[1])
    logit_grad = (soft - (lanes == label).astype(F32)).astype(BF16)
    logit_wide = logit_grad.astype(F32)
    back = jnp.zeros((16, D), F32)
    for cls in range(CLASSES):
        picked = jnp.sum(jnp.where(lanes == cls, logit_wide, 0.0), -1, keepdims=True)
        back = back + picked * row(CW + cls)
    pool_grad = (back * (1.0 - pooled * pooled)).astype(BF16)
    first_grad_ref[...] = nt(pool_grad, pool_weight)[0:8]
    padded = jnp.concatenate([logit_wide[0:2], jnp.zeros((2, D - 128), F32)], -1)
    ramp = jnp.concatenate(
        [first.astype(F32)[0:2], pool_grad.astype(F32)[0:2], wide[0:2], padded], 0
    ).astype(BF16)
    if layer:
        out_ref[0] = prior_out[...]
        logits_ref[0] = prior_logits[...]
        ramp_ref[0] = prior_ramp[...]
        out_ref[1] = output
        logits_ref[1] = logits[0:8]
        ramp_ref[1] = ramp
    else:
        out_ref[...] = output
        logits_ref[...] = logits[0:8]
        ramp_ref[...] = ramp
    wait_copies(leaving)


def ffn_forward(line, layer, labels, class_bias, x, normed, low, small, in_bias, weights, prior):
    tokens = low.shape[0]
    smem = pl.BlockSpec(memory_space=pltpu.SMEM)
    stack = (2,) if layer else ()
    return line.call(
        "ffn_forward%d" % layer,
        12,
        functools.partial(ffn_forward_kernel, layer),
        [(labels, smem), (class_bias, smem)]
        + near(x, normed, low, small, in_bias)
        + fixed(*weights)
        + near(*prior),
        sent(
            ((2, tokens, WIDE), BF16),
            ((3, tokens, WIDE), BF16),
            ((4, tokens, D), F32),
        )
        + made(
            ((tokens, D), F32),
            ((tokens, 1), F32),
            ((8, D), F32),
            ((*stack, tokens, D), BF16),
            ((*stack, 8, 128), F32),
            ((*stack, 8, D), BF16),
        ),
        [
            pltpu.VMEM((4, D, D), BF16),
            pltpu.VMEM((SHARDS, D, D), BF16),
            pltpu.VMEM((D, D), BF16),
            pltpu.VMEM((4, tokens, D), BF16),
            pltpu.VMEM((4, tokens, WIDE - D), BF16),
            pltpu.VMEM((4, tokens, D), F32),
            pltpu.SemaphoreType.DMA((48,)),
            pltpu.SemaphoreType.DMA((13,)),
        ],
    )


def ffn_backward_kernel(
    layer, grad_ref, first_ref, normed_two_ref, rstd_two_ref, slope_ref, normed_ref, rstd_ref,
    small, *refs
):
    pairs_ref, rows_ref, low_ref, smalls_ref, up, down, pairs, sems, out_sems = refs[-9:]
    downs, ups, _ = load_ffn_weights(refs[:-9], up, down, None, sems, True)

    def row(index):
        return small[layer, index : index + 1].astype(F32)

    grad = grad_ref[...].astype(F32)
    index = lax.broadcasted_iota(jnp.int32, grad.shape, 0)
    grad = grad + jnp.where(index == 0, first_ref[0:1], 0.0)
    grad = grad + jnp.where(index == SEQ, first_ref[1:2], 0.0)
    res_two, gain_two, shift_two = norm_back(grad, normed_two_ref[...], rstd_two_ref[...], row(G1))
    ffn_grad = res_two.astype(BF16)
    pairs[4] = ffn_grad
    leaving = run_copies([(pairs.at[4], pairs_ref.at[4])], out_sems, 4)
    wait_copies(downs)
    middle_grad = res_two
    for block in range(4):
        act_grad = nt(ffn_grad, down[block])
        pre_grad = (act_grad * slope_ref[block]).astype(BF16)
        pairs[block] = pre_grad
        leaving += run_copies([(pairs.at[block], pairs_ref.at[block])], out_sems, block)
        if block == 0:
            wait_copies(ups)
        smalls_ref[block : block + 1] = jnp.sum(pre_grad.astype(F32), 0, keepdims=True)
        middle_grad = middle_grad + nt(pre_grad, up[block])
    res_one, gain_one, shift_one = norm_back(middle_grad, normed_ref[...], rstd_ref[...], row(G0))
    rows_ref[...] = res_one
    low = res_one.astype(BF16)
    low_ref[...] = low
    smalls_ref[4:5] = jnp.sum(ffn_grad.astype(F32), 0, keepdims=True)
    smalls_ref[5:6] = jnp.sum(low.astype(F32), 0, keepdims=True)
    smalls_ref[6:7] = gain_one
    smalls_ref[7:8] = gain_two
    smalls_ref[8:9] = shift_one
    smalls_ref[9:10] = shift_two
    wait_copies(leaving)


def ffn_backward(
    line, layer, grad, first_grad, normed_two, rstd_two, slope, normed, rstd, small, weights
):
    tokens = grad.shape[0]
    return line.call(
        "ffn_backward%d" % layer,
        11,
        functools.partial(ffn_backward_kernel, layer),
        near(grad, first_grad, normed_two, rstd_two, slope, normed, rstd, small)
        + away(*weights),
        sent(((5, tokens, D), BF16))
        + made(
            ((tokens, D), F32),
            ((tokens, D), BF16),
            ((10, D), F32),
        ),
        [
            pltpu.VMEM((4, D, D), BF16),
            pltpu.VMEM((SHARDS, D, D), BF16),
            pltpu.VMEM((5, tokens, D), BF16),
            pltpu.SemaphoreType.DMA((32,)),
            pltpu.SemaphoreType.DMA((5,)),
        ],
    )


def place_pieces(groups, natural, outs, y, sems):
    here = quarter_index()
    pairs = []
    for index, (order, first, count) in enumerate(groups):
        keep_ref, send_ref = outs[2 * index : 2 * index + 2]
        rows = slice(first, first + count)
        for x in range(2):
            for a in range(2):
                if not order:
                    target, unit, place = (send_ref if y else keep_ref), 2 * a + x, 2 * a + x
                else:
                    bits = {"y": y, "x": x, "a": a}
                    outer, middle, inner = (bits[dim] for dim in order)
                    target = send_ref if outer else keep_ref
                    unit, place = (2 * a + x) ^ here, 2 * middle + inner
                pairs.append((natural.at[y, unit, rows], target.at[place]))
    return run_copies(pairs, sems, y * len(pairs))


def piece_shapes(groups):
    shapes = []
    for _, _, count in groups:
        shapes += [((4, count, D), BF16)] * 2
    return shapes


def ffn_weights_kernel(groups, act_ref, act_near_ref, pairs_ref, pairs_near_ref, *refs):
    outs, (natural, sems) = refs[:-2], refs[-2:]
    leaving = []
    for slot in (1, 0):
        mine, other = act_ref[slot], act_near_ref[slot]
        down = tn(mine[:, 0:D], pairs_ref[4]) + tn(other[:, 0:D], pairs_near_ref[4])
        down = down.astype(BF16)
        for block in range(4):
            natural[slot, block, PART : 2 * PART] = down[block * PART : (block + 1) * PART]
            up = tn(mine[:, D : D + PART], pairs_ref[block])
            up = up + tn(other[:, D : D + PART], pairs_near_ref[block])
            natural[slot, block, 0:PART] = up.astype(BF16)
        leaving += place_pieces(groups, natural, outs, slot, sems)
    wait_copies(leaving)


def ffn_weight_grads(line, layer, groups, act, act_near, pairs, pairs_near):
    return line.call(
        "ffn_weight_grads%d" % layer,
        8,
        functools.partial(ffn_weights_kernel, groups),
        near(act, act_near, pairs, pairs_near),
        sent(*piece_shapes(groups)),
        [pltpu.VMEM((2, 4, 2 * PART, D), BF16), pltpu.SemaphoreType.DMA((8 * len(groups),))],
    )


def attn_weights_kernel(
    groups, x_ref, acts_near_ref, grad_ref, pairs_ref, near_ref, *refs
):
    outs, (natural, sems) = refs[-2 - 2 * len(groups) : -2], refs[-2:]
    leaving = []
    cut = 3 * PART
    tokens = x_ref.shape[0]
    x_near = acts_near_ref[2, :, 0:D]
    grad_near = near_ref[2 * tokens : 3 * tokens]
    if len(refs) > 2 + 2 * len(groups):
        smalls_ref, by_shard = refs[0], refs[-3]
        outs = refs[1:-3]
        smalls = []
        for layer in range(LAYERS):
            start = 3 * tokens + 32 * layer
            high = near_ref[start : start + 16].astype(F32)
            rest = near_ref[start + 16 : start + 32].astype(F32)
            smalls.append(smalls_ref[layer] + (high + rest)[0:12])
        for part in range(SHARDS):
            lanes = slice(part * PART, (part + 1) * PART)
            for layer in range(LAYERS):
                row = 3 * layer
                by_shard[part, row : row + 1] = smalls[layer][part : part + 1]
                for item in range(8):
                    target = slice((item % 4) * PART, (item % 4 + 1) * PART)
                    value = smalls[layer][4 + item : 5 + item, lanes]
                    by_shard[part, row + 1 + item // 4 : row + 2 + item // 4, target] = value
            by_shard[part, 6:16] = jnp.zeros((10, D), F32)
        shard = shard_index()
        for slot in range(2):
            natural[slot, 0, PART:TALL] = by_shard[shard ^ (2 * slot)].astype(BF16)
            for unit in range(1, 4):
                natural[slot, unit, PART:TALL] = jnp.zeros((TALL - PART, D), BF16)
    for slot in (1, 0):
        mine, other = pairs_ref[slot], near_ref[slot * tokens : (slot + 1) * tokens]
        value = tn(mine[:, 0:cut], x_ref[...]) + tn(other[:, 0:cut], x_near)
        value = value.astype(BF16)
        for unit in range(3):
            natural[slot, unit, 0:PART] = value[unit * PART : (unit + 1) * PART]
        value = tn(mine[:, cut:D], grad_ref[...]) + tn(other[:, cut:D], grad_near)
        natural[slot, 3, 0:PART] = value.astype(BF16)
        leaving += place_pieces(groups, natural, outs, slot, sems)
    wait_copies(leaving)


def attn_weight_grads(line, layer, groups, *operands):
    return line.call(
        "attn_weight_grads%d" % layer,
        5,
        functools.partial(attn_weights_kernel, groups),
        near(*operands),
        sent(*piece_shapes(groups)),
        ([pltpu.VMEM((SHARDS, 16, D), F32)] if len(operands) > 5 else [])
        + [
            pltpu.VMEM((2, 4, groups[0][2], D), BF16),
            pltpu.SemaphoreType.DMA((8 * len(groups),)),
        ],
    )


def attn_backward_kernel(
    layer, res_ref, grad_ref, smalls_in_ref, *refs
):
    count = 10 if layer or "pair0" not in FORWARD else 14
    kept, weights, refs = refs[:6], refs[6:count], refs[count:]
    if layer == 0:
        prior, refs = refs[0], refs[1:]
    pairs_ref, pairs_send_ref, rows_ref, smalls_ref, slots, sems, sums = refs
    tokens = grad_ref.shape[0]
    copies = load_attn_weights(weights[:2], slots.at[0:2], sems)
    copies += load_attn_weights(weights[2:], slots.at[2:4], sems, 2)
    shard = shard_index()
    grad = grad_ref[...]
    total = res_ref[...]
    for slot in range(4):
        wait_copies(copies[slot])
        half, index = slot >> 1, slot & 1
        qkv_ref, probs_ref, context_ref = kept[3 * half : 3 * half + 3]
        context_grad = nt(grad, slots[slot, 3]).astype(BF16)
        places = [
            (
                slice(seq * SEQ, (seq + 1) * SEQ),
                slice(head * HEAD_DIM, (head + 1) * HEAD_DIM),
            )
            for seq in range(2)
            for head in range(PART // HEAD_DIM)
        ]
        query, key, val = (qkv_ref[index, part] for part in range(3))
        probs = probs_ref[index]
        prob_grad = jnp.stack([nt(context_grad[at], val[at]) for at in places])
        mean = jnp.sum(prob_grad * probs, -1, keepdims=True)
        score_grad = (probs * (prob_grad - mean)).astype(BF16)
        probs_low = probs.astype(BF16)
        scale = HEAD_DIM ** (-0.5)
        heads = [
            [nn(score_grad[i], key[at]) * scale for i, at in enumerate(places)],
            [tn(score_grad[i], query[at]) * scale for i, at in enumerate(places)],
            [tn(probs_low[i], context_grad[at]) for i, at in enumerate(places)],
        ]
        half_heads = len(places) // 2
        seq_rows = [
            [jnp.concatenate(group[:half_heads], -1), jnp.concatenate(group[half_heads:], -1)]
            for group in heads
        ]
        for part in range(3):
            value = jnp.concatenate(seq_rows[part], 0).astype(BF16)
            if slot & 1:
                rows = slice(half * tokens, (half + 1) * tokens)
                pairs_send_ref[rows, part * PART : (part + 1) * PART] = value
            else:
                pairs_ref[half, :, part * PART : (part + 1) * PART] = value
            if part != 1:
                sums[shard ^ slot, part // 2] = jnp.sum(value.astype(F32), 0, keepdims=True)
            total = total + nn(value, slots[slot, part])
        if slot & 1:
            pairs_send_ref[half * tokens : (half + 1) * tokens, 3 * PART : D] = context_ref[index]
        else:
            pairs_ref[half, :, 3 * PART : D] = context_ref[index]
    pairs_send_ref[2 * tokens : 3 * tokens] = grad
    rows_ref[...] = total.astype(rows_ref.dtype)
    own = [
        jnp.concatenate([sums[part, index] for part in range(SHARDS)], -1) for index in range(2)
    ]
    if layer:
        smalls_ref[0:10] = smalls_in_ref[...]
        smalls_ref[10:11] = own[0]
        smalls_ref[11:12] = own[1]
    else:
        smalls_ref[1] = prior[...]
        smalls_ref[0, 0:10] = smalls_in_ref[...]
        smalls_ref[0, 10:11] = own[0]
        smalls_ref[0, 11:12] = own[1]
        for index in range(LAYERS):
            value = smalls_ref[index]
            high = value.astype(BF16)
            rest = (value - high.astype(F32)).astype(BF16)
            start = 3 * tokens + 32 * index
            pairs_send_ref[start : start + 16] = jnp.concatenate(
                [high, jnp.zeros((4, D), BF16)], 0
            )
            pairs_send_ref[start + 16 : start + 32] = jnp.concatenate(
                [rest, jnp.zeros((4, D), BF16)], 0
            )


def attn_backward(line, layer, res, grad, kept, smalls, weights, prior):
    tokens = grad.shape[0]
    return line.call(
        "attn_backward%d" % layer,
        15,
        functools.partial(attn_backward_kernel, layer),
        near(res, grad, smalls, *kept) + away(*weights) + near(*prior),
        made(
            ((2, tokens, D), BF16),
            ((3 * tokens + (0 if layer else 64), D), BF16),
            ((tokens, D), F32 if layer else BF16),
            ((12, D) if layer else (2, 12, D), F32),
        ),
        [
            pltpu.VMEM((4, 4, PART, D), BF16),
            pltpu.SemaphoreType.DMA((12,)),
            pltpu.VMEM((SHARDS, 2, 1, PART), F32),
        ],
    )


def halve_kernel(keep_ref, came_ref, low_ref, high_ref):
    half = low_ref.shape[0]
    low_ref[...] = keep_ref[0:half] + came_ref[0:half]
    high_ref[...] = keep_ref[half:] + came_ref[half:]


def add_kernel(keep_ref, came_ref, sum_ref):
    sum_ref[...] = keep_ref[...] + came_ref[...]


def reduction(line, moves, name, order, back, keep, send):
    shape = keep.shape
    micros = 1 + shape[1] / 192
    if not order:
        came = moves("y", send)
        yield
        total = line.call(
            "add_%s" % name, micros, add_kernel, near(keep, came), made((shape, BF16))
        )[0]
        yield (back, lax.psum(total, "dp"))
    came = moves(order[0], send)
    for step, dim in enumerate(order[1:]):
        yield
        half = (keep.shape[0] // 2, *shape[1:])
        keep, send = line.call(
            "halve_%s%d" % (name, step), micros, halve_kernel, near(keep, came),
            made((half, BF16), (half, BF16)),
        )
        came = moves(dim, send)
    yield
    keep, came = keep[0], came[0]
    total = line.call(
        "add_%s" % name, micros, add_kernel, near(keep, came), made((shape[1:], BF16))
    )[0]
    came = moves("b", total)
    for bit in moves.more():
        yield
        total = line.call(
            "more_%s%d" % (name, bit), micros, add_kernel, near(total, came),
            made((shape[1:], BF16)),
        )[0]
        came = moves.place(bit, total)
    yield
    total = line.call(
        "last_%s" % name, micros, add_kernel, near(total, came), made((shape[1:], BF16))
    )[0]
    came = moves(back[0], total)
    yield
    both = line.call(
        "both_%s" % name, micros, both_kernel, near(total, came), made(((2, *shape[1:]), BF16))
    )[0]
    yield (back, both, moves(back[1], both))


def join_kernel(one_ref, two_ref, joint_ref):
    count = one_ref.shape[0]
    joint_ref[0:count] = one_ref[...]
    joint_ref[count : 2 * count] = two_ref[...]


def join(line, one, two):
    shape = (2 * one.shape[0], *one.shape[1:])
    return line.call("join%d" % shape[0], 1, join_kernel, near(one, two), made((shape, BF16)))[0]


def both_kernel(one_ref, two_ref, both_ref):
    both_ref[0] = one_ref[...]
    both_ref[1] = two_ref[...]


def unpack_kernel(back, first, targets, prior, *refs):
    values = 2 if back else 1
    quarters = refs[:values]
    outs = refs[values + prior : -2]
    whole, sems = refs[-2:]
    here = quarter_index()
    count = whole.shape[1]
    for index in range(4):
        if not back:
            whole[index] = quarters[0][index, first : first + count].astype(F32)
            continue
        bits = {back[0]: index & 1, back[1]: index >> 1}
        relative = 2 * bits["a"] + bits["x"]
        quarter = quarters[index >> 1][index & 1, first : first + count]
        whole[relative ^ here] = quarter.astype(F32)
    if count == TALL:
        qkv_bias, out_bias, gain, shift, in_bias, down_bias = outs[len(targets) :]
        for layer in range(LAYERS):
            row = PART + 3 * layer

            def item(index):
                at = row + 1 + index // 4
                return whole[0, at : at + 1, (index % 4) * PART : (index % 4 + 1) * PART]

            in_bias[layer : layer + 1] = whole[0, row : row + 1]
            down_bias[layer : layer + 1] = item(0)
            out_bias[layer : layer + 1] = item(1)
            for index in range(2):
                gain[layer, index : index + 1] = item(2 + index)
                shift[layer, index : index + 1] = item(4 + index)
                qkv_bias[layer, index : index + 1] = item(6 + index)
    pairs = [
        (whole.at[unit, 0:PART], outs[which].at[where])
        for unit, which, where in targets_of(targets)
    ]
    wait_copies(run_copies(pairs, sems, 0))


def targets_of(targets):
    return [(unit, which, where) for which, places in enumerate(targets) for unit, where in places]


SMALL_SHAPES = (
    (LAYERS, 2, PART), (LAYERS, PART), (LAYERS, 2, PART), (LAYERS, 2, PART), (LAYERS, D), (LAYERS, PART)
)


def unpack(line, name, quarters, first, shapes, targets, prior):
    back, *values = quarters
    aliases = {len(values) + index: index for index in range(len(prior))}
    count = TALL if values[0].shape[1] == TALL else PART
    outs = [(shape, F32, anywhere()) for shape in shapes]
    if count == TALL:
        outs += made(*[(shape, F32) for shape in SMALL_SHAPES])
    return line.call(
        name,
        3,
        functools.partial(unpack_kernel, back, first, targets, len(prior)),
        near(*values) + away(*prior),
        outs,
        [pltpu.VMEM((4, count, D), F32), pltpu.SemaphoreType.DMA((4,))],
        aliases,
    )


def unpack_up(line, layer, quarters, first, prior):
    places = [(unit, (layer, slice(None), slice(unit * D, (unit + 1) * D))) for unit in range(4)]
    return unpack(
        line, "unpack_up%d" % layer, quarters, first, [(LAYERS, PART, FF)], [places], prior
    )


def unpack_down(line, layer, quarters, first, prior):
    places = [(unit, (layer, slice(unit * PART, (unit + 1) * PART))) for unit in range(4)]
    return unpack(
        line, "unpack_down%d" % layer, quarters, first, [(LAYERS, D, D)], [places], prior
    )


def unpack_attn(line, layer, quarters, first, prior):
    return unpack(
        line,
        "unpack_attn%d" % layer,
        quarters,
        first,
        [(LAYERS, 3, PART, D), (LAYERS, PART, D)],
        [[(unit, (layer, unit)) for unit in range(3)], [(3, (layer,))]],
        prior,
    )


def pool_grads(ramp, shard):
    ramp = ramp.reshape(ramp.shape[0], LAYERS, 4, 2, D)
    ramp = jnp.transpose(ramp, (1, 2, 0, 3, 4)).reshape(LAYERS, 4, -1, D)
    first, pool_grad, pooled, logit_grad = (ramp[:, part] for part in range(4))
    logit_grad = logit_grad[:, :, 0:CLASSES]
    own_first = lax.dynamic_slice_in_dim(first, shard * PART, PART, 2)
    own_pooled = lax.dynamic_slice_in_dim(pooled, shard * PART, PART, 2)
    pool_weight_grad = jnp.einsum("lnd,lne->lde", own_first, pool_grad, preferred_element_type=F32)
    class_weight_grad = jnp.einsum(
        "lnd,lnc->ldc", own_pooled, logit_grad, preferred_element_type=F32
    )
    class_bias_grad = jnp.sum(logit_grad.astype(F32), 1)
    own_pool = lax.dynamic_slice_in_dim(pool_grad, shard * PART, PART, 2)
    pool_bias_grad = jnp.sum(own_pool.astype(F32), 1)
    return pool_weight_grad, pool_bias_grad, class_weight_grad, class_bias_grad


ROUTES = {
    "f1": ("yxa", "ax"),
    "a1": ("axy", "ax"),
    "f0": ("axy", "xa"),
    "a0": ("xya", "xa"),
}
FORWARD = (
    "small0", "ffn0", "attn0", "arrange0", "row0", "near0", "second0", "ffn1", "third0",
    "cross0", "swap0", "far0", "meet0", "second1", "row1", "fourth0", "block0", "third1",
    "near1", "cross1", "swap1", "far1", "fourth1", "block1",
)
SCHEDULE = (
    "R0", "F1", "R1", "A1", "R1", "FW1", "R1", "AW1", "R1", "F0", "R1", "A0", "P1", "FW0",
    "AW0", "a1", "f1", "a0", "a1", "a0", "f0", "a1", "f1", "a1", "a0", "f1", "a0", "f0", "a1",
    "a0", "f0", "Ua1", "f1", "Ua0", "f0", "f1", "f0", "Uf1", "Uf0",
)


def on_device(
    mesh,
    hidden_in,
    out_cotangent,
    labels,
    qkv_weight,
    qkv_bias,
    out_weight,
    out_bias,
    norm_gain,
    norm_shift,
    ffn_in,
    ffn_in_bias,
    ffn_out,
    ffn_out_bias,
    pool_weight,
    pool_bias,
    class_weight,
    class_bias,
):
    moves = Moves(mesh)
    line = Line()
    shard = shard_index()
    qkv_turned = jnp.swapaxes(qkv_weight, 2, 3)

    class_bias_wide = class_bias.astype(F32)
    ffn_own, ffn_far, attn_own, attn_far = [None] * 2, [None] * 2, [None] * 2, [None] * 2
    kept, held = [None] * 2, {"x0": hidden_in}

    def go(name):
        layer = int(name[-1])
        part = name[:-1]
        if part == "small":
            held["packed"] = line.call(
                "pack_small",
                1,
                pack_small_kernel,
                near(
                    qkv_bias, out_bias, norm_gain, norm_shift, ffn_in_bias, ffn_out_bias, pool_bias,
                    jnp.transpose(class_weight, (2, 0, 1)),
                ),
                made(((LAYERS, 16, PART), F32)),
            )[0]
        elif part == "arrange":
            held["small"] = arrange(line, moves, held["packed"])
        elif part == "ffn":
            pack, quarter = pack_ffn(line, layer, ffn_in, ffn_out, pool_weight)
            ffn_own[layer] = [pack]
            ffn_far[layer] = Spread(line, moves, quarter, "a" if layer else "x")
        elif part == "attn":
            *own, quarter = pack_attn(line, qkv_turned, out_weight)
            held["leaving"] = own[2:]
            if "pair0" in FORWARD:
                attn_far[0] = Spread(line, moves, quarter, "a")
            for index, value in enumerate(own[:2]):
                attn_own[index] = [value, moves("c", value)]
        elif part == "second":
            ffn_far[layer].second()
        elif part == "third":
            ffn_far[layer].third()
        elif part == "fourth":
            ffn_far[layer].fourth()
        elif part == "pair":
            attn_far[0].second()
        elif part == "last":
            attn_far[0].third()
        elif part == "end":
            attn_far[0].fourth()
            attn_far[0] = attn_far[0].pieces()
        elif part == "row":
            held["far%d" % layer] = moves("y", line.gate(held["leaving"][layer])[0])
        elif part == "cross":
            far = line.gate(held["far%d" % layer])[0]
            attn_far[layer] = [far, moves("c", far)]
        elif part == "swap":
            pack = line.gate(ffn_own[layer][0])[0]
            ffn_own[layer] = [pack, moves("c", pack)]
        elif part == "meet":
            line.waits = (*line.waits, ffn_own[layer][1], ffn_far[layer].stack)
        elif part == "near":
            shard_small, small, in_bias = held["small"]
            *attn_near, total = attn_forward(
                line, layer, 0, held["x%d" % layer], (shard_small,), attn_own[layer]
            )
            kept[layer] = [attn_near, total]
        elif part == "far":
            shard_small, small, in_bias = held["small"]
            attn_near, total = kept[layer]
            *attn_rest, normed, rstd, low = attn_forward(
                line, layer, 1, held["x%d" % layer], (shard_small, small, total), attn_far[layer]
            )
            kept[layer] = [(attn_near + attn_rest, normed, rstd), low]
        elif part == "block":
            shard_small, small, in_bias = held["small"]
            attention, low = kept[layer]
            x = held["x%d" % layer]
            if layer:
                line.waits = (*line.waits, kept[0][2][1])
            act, act_send, slope, normed_two, rstd_two, first_grad, *prior = ffn_forward(
                line, layer, labels, class_bias_wide, x, attention[1], low, small, in_bias,
                ffn_own[layer] + ffn_far[layer].pieces(), held.get("prior", ()),
            )
            act_near = moves("c", act_send)
            kept[layer] = (
                x, attention, (act, act_near), (slope, normed_two, rstd_two, first_grad)
            )
            held["prior"] = prior
            held["x1"] = prior[0]

    for name in FORWARD:
        go(name)
    ffn_weights = [ffn_own[layer] + ffn_far[layer].pieces() for layer in range(LAYERS)]
    nears = [kept[layer][2][1] for layer in range(LAYERS)]
    small = held["small"][1]
    block_outputs, logits, ramp = held["prior"]

    chains, results, state = {}, {}, {"grad": out_cotangent, "prior": ()}
    ramp_value = [ramp[None]]
    ramp_steps = [("head", 1), ("head", 2)]
    bit = 1
    while bit < mesh.shape["dp"]:
        ramp_steps.append(("dp", bit))
        bit *= 2

    def begin(names, pieces):
        for index, name in enumerate(names):
            keep, send = pieces[2 * index : 2 * index + 2]
            chains[name] = reduction(line, moves, name, *ROUTES[name], keep, send)
            next(chains[name])

    def step(name):
        layer = int(name[-1])
        if name == "R0":
            ramp_value[0] = line.gate(ramp_value[0])[0]
        elif name[:-1] == "F":
            _, (_, normed, rstd), _, (slope, normed_two, rstd_two, first_grad) = kept[layer]
            pairs, res, low, rows = ffn_backward(
                line, layer, state["grad"], first_grad, normed_two, rstd_two, slope, normed, rstd,
                small, ffn_weights[layer],
            )
            state["ffn"] = (pairs, moves("c", pairs))
            state["low"] = low
            state["res"], state["rows"] = res, rows
            line.waits = (*line.waits, nears[layer])
        elif name[:-1] == "A":
            pairs, send, grad, smalls = attn_backward(
                line, layer, state["res"], state["low"], kept[layer][1][0], state["rows"],
                attn_own[layer] + attn_far[layer], state["prior"],
            )
            state["attn"] = (pairs, moves("c", send))
            state["grad"], state["prior"] = grad, (smalls,)
        elif name[:-1] == "FW":
            names = [key for key in ROUTES if key[-1] == name[-1] and key[0] != "a"]
            spans = {"f": (0, 2 * PART), "u": (0, PART), "d": (PART, PART)}
            groups = [(ROUTES[key][0], *spans[key[0]]) for key in names]
            begin(names, ffn_weight_grads(line, layer, groups, *kept[layer][2], *state["ffn"]))
        elif name[:-1] == "AW":
            key = "a" + name[-1]
            groups = [(ROUTES[key][0], 0, PART if layer else TALL)]
            operands = (kept[layer][0], kept[layer][2][1], state["low"], *state["attn"])
            if layer == 0:
                operands += state["prior"]
            begin([key], attn_weight_grads(line, layer, groups, *operands))
        elif name == "R1":
            for _ in range(max(1, len(ramp_steps) - 4)):
                axis, bit = ramp_steps.pop(0)
                came = lax.ppermute(ramp_value[0], AXES, flip(mesh, axis, bit))
                ramp_value[0] = join(line, ramp_value[0], came)
        elif name == "P1":
            state["pool"] = pool_grads(ramp_value[0], shard)
            line.waits = (*line.waits, *state["pool"])
        elif name[0] == "U":
            key = name[1:]
            while key not in results:
                results[key] = next(chains[key])
                if results[key] is None:
                    del results[key]
            if key[0] in "uf":
                state["up"] = unpack_up(line, layer, results[key], 0, state.get("up", ()))
            if key[0] in "df":
                first = PART if key[0] == "f" else 0
                state["down"] = unpack_down(line, layer, results[key], first, state.get("down", ()))
            if key[0] == "a":
                state["attn_out"] = unpack_attn(
                    line, layer, results[key], 0, state.get("attn_out", ())
                )
        else:
            result = next(chains[name], None)
            if result is not None:
                results[name] = result

    for name in SCHEDULE:
        step(name)
    qkv_grad, out_grad, qkv_bias_grad, out_bias_grad, *smalls = state["attn_out"]
    gain_grad, shift_grad, in_bias_grad, down_bias_grad = smalls
    pool_weight_grad, pool_bias_grad, class_weight_grad, class_bias_grad = state["pool"]
    return (
        block_outputs,
        logits[:, 0:2, 0:CLASSES],
        state["grad"],
        jnp.swapaxes(qkv_grad, 2, 3),
        qkv_bias_grad,
        out_grad,
        out_bias_grad,
        gain_grad,
        shift_grad,
        state["up"][0],
        in_bias_grad,
        state["down"][0],
        down_bias_grad,
        pool_weight_grad,
        pool_bias_grad,
        class_weight_grad,
        class_bias_grad,
    )


def solution(mesh):
    return jax.shard_map(
        functools.partial(on_device, mesh),
        mesh=mesh,
        in_specs=(
            P(("dp", "head"), None),
            P(("dp", "head"), None),
            P(("dp", "head")),
            P(None, None, None, "head"),
            P(None, None, "head"),
            P(None, "head", None),
            P(None, "head"),
            P(None, None, "head"),
            P(None, None, "head"),
            P(None, "head", None),
            P(None, "head"),
            P(None, "head", None),
            P(None, "head"),
            P(None, "head", None),
            P(None, "head"),
            P(None, "head", None),
            P(),
        ),
        out_specs=(
            P(None, ("dp", "head"), None),
            P(None, ("dp", "head"), None),
            P(("dp", "head"), None),
            P(None, None, None, "head"),
            P(None, None, "head"),
            P(None, "head", None),
            P(None, "head"),
            P(None, None, "head"),
            P(None, None, "head"),
            P(None, "head", None),
            P(None, "head"),
            P(None, "head", None),
            P(None, "head"),
            P(None, "head", None),
            P(None, "head"),
            P(None, "head", None),
            P(),
        ),
        check_vma=False,
    )
```

```python
import functools

import jax
import jax.numpy as jnp
from jax import lax
from jax.experimental import pallas as pl
from jax.experimental.pallas import tpu as pltpu
from jax.sharding import PartitionSpec as P

D = 768
FF = 3072
HEAD_DIM = 64
SEQ = 128
LAYERS = 2
SHARDS = 4
PART = D // SHARDS
POOL_PART = PART // 4
CLASSES = 3
EPS = 1e-12
ROOT_HALF = 0.7071067811865476
DENSITY_SCALE = 0.3989422804014327
F32 = jnp.float32
BF16 = jnp.bfloat16
HEAD = "head"
DP = "dp"
AXES = (DP, HEAD)
VMEM_LIMIT = 58 * 1024 * 1024
TALL = PART + 16
FFN_ROWS = 2 * PART + POOL_PART
WIDE = 1024

QB, VB, OB, G0, G1, S0, S1, FB, PB, CW = 0, 1, 2, 3, 4, 5, 6, 11, 12, 13


def dot(left, right, dims):
    return lax.dot_general(left, right, ((dims[:1], dims[1:]), ((), ())), preferred_element_type=F32)


def nn(left, right):
    return dot(left, right, (1, 0))


def nt(left, right):
    return dot(left, right, (1, 1))


def tn(left, right):
    return dot(left, right, (0, 0))


def normalise(resid):
    centred = resid - jnp.mean(resid, -1, keepdims=True)
    rstd = lax.rsqrt(jnp.mean(centred * centred, -1, keepdims=True) + EPS)
    return centred * rstd, rstd


def norm_back(incoming, normed, rstd, gain):
    scaled = incoming * gain
    back = rstd * (
        scaled
        - jnp.mean(scaled, -1, keepdims=True)
        - normed * jnp.mean(scaled * normed, -1, keepdims=True)
    )
    gain_grad = jnp.sum(incoming * normed, 0, keepdims=True)
    shift_grad = jnp.sum(incoming, 0, keepdims=True)
    return back, gain_grad, shift_grad


def cost(micros):
    return pl.CostEstimate(flops=int(micros * 1e10), bytes_accessed=0, transcendentals=0)


def shard_index():
    return lax.axis_index(HEAD)


def quarter_index():
    return lax.axis_index(DP) & 3


def rows_at(index, count):
    return pl.ds(pl.multiple_of(index * count, count), count)


def vmem():
    return pl.BlockSpec(memory_space=pltpu.VMEM)


def anywhere():
    return pl.BlockSpec(memory_space=pl.ANY)


ROOM = {
    "pack": 14, "arrange": 4, "attn_forward": 18, "ffn_forward": 30, "ffn_backward": 32,
    "attn_backward": 24, "ffn_weight": 20, "attn_weight": 16, "halve": 14, "unpack": 14,
}


def room(name):
    for start, size in ROOM.items():
        if name.startswith(start):
            return size << 20
    return 8 << 20


TOKEN = jax.ShapeDtypeStruct((8, 128), F32)


def main_memory():
    return pl.BlockSpec(memory_space=pltpu.HBM)


class Line:
    def __init__(self):
        self.waits = ()

    def call(self, name, micros, kernel, ins, outs, scratch=(), aliases=None):
        waits = tuple(self.waits)
        count, total = len(ins), len(ins) + len(waits) + len(outs)

        def body(*refs):
            kernel(*refs[:count], *refs[count + len(waits) : total], *refs[total + 1 :])

        *result, token = pl.pallas_call(
            body,
            out_shape=[jax.ShapeDtypeStruct(shape, dtype) for shape, dtype, _ in outs] + [TOKEN],
            in_specs=[spec for _, spec in ins] + [main_memory()] * len(waits),
            out_specs=[spec for _, _, spec in outs] + [main_memory()],
            scratch_shapes=list(scratch),
            input_output_aliases=aliases or {},
            compiler_params=pltpu.CompilerParams(vmem_limit_bytes=room(name)),
            cost_estimate=cost(micros),
            name=name,
        )(*[value for value, _ in ins], *waits)
        self.waits = (token,)
        return result

    def gate(self, *values):
        outs = [(value.shape, value.dtype, anywhere()) for value in values]
        aliases = {index: index for index in range(len(values))}
        return self.call("gate", 10, lambda *refs: None, away(*values), outs, aliases=aliases)


def near(*values):
    return [(value, vmem()) for value in values]


def fixed(*values):
    return [(value, main_memory()) for value in values]


def away(*values):
    return [(value, anywhere()) for value in values]


def made(*shapes):
    return [(shape, dtype, vmem()) for shape, dtype in shapes]


def sent(*shapes):
    return [(shape, dtype, anywhere()) for shape, dtype in shapes]


def run_copies(pairs, sems, start):
    copies = [
        pltpu.make_async_copy(src, dst, sems.at[start + index])
        for index, (src, dst) in enumerate(pairs)
    ]
    for item in copies:
        item.start()
    return copies


def wait_copies(copies):
    for item in copies:
        item.wait()


def flip(mesh, axis, bit):
    dp, head = mesh.shape[DP], mesh.shape[HEAD]
    pairs = []
    for place in range(dp):
        for shard in range(head):
            to_place = place ^ bit if axis == DP else place
            to_shard = shard ^ bit if axis == HEAD else shard
            pairs.append((place * head + shard, to_place * head + to_shard))
    return pairs


DIMS = {"c": (HEAD, 1), "y": (HEAD, 2), "d": (HEAD, 3), "x": (DP, 1), "a": (DP, 2), "b": (DP, 4)}


class Moves:
    def __init__(self, mesh):
        self.mesh = mesh

    def __call__(self, dim, value):
        return lax.ppermute(value, AXES, flip(self.mesh, *DIMS[dim]))

    def more(self):
        bit = 8
        while bit < self.mesh.shape[DP]:
            yield bit
            bit *= 2

    def place(self, bit, value):
        return lax.ppermute(value, AXES, flip(self.mesh, DP, bit))


def stack_kernel(one, two, follow, follow_out, stack_ref, sems, *, order):
    refs = {"one": one, "two": two, "follow": follow}
    pairs = [(refs[name], stack_ref.at[index]) for index, name in enumerate(order)]
    wait_copies(run_copies(pairs, sems, 0))


class Spread:
    def __init__(self, line, moves, quarter, last):
        self.line, self.moves, self.last = line, moves, last
        self.far = [moves("y", quarter)]

    def second(self):
        self.far = list(self.line.gate(*self.far))
        self.far += [self.moves("x", self.far[0]), self.moves("a", self.far[0])]

    def third(self):
        follow = 2 if self.last == "x" else 1
        shape = self.far[0].shape
        order = ("one", "two", "follow") if follow == 2 else ("one", "follow", "two")
        operands = (self.far[0], self.far[3 - follow], self.far[follow])
        self.far[follow], stack = self.line.call(
            "stack",
            3,
            functools.partial(stack_kernel, order=order),
            fixed(*operands),
            [(shape, BF16, main_memory()), ((3, *shape), BF16, vmem())],
            [pltpu.SemaphoreType.DMA((3,))],
            {2: 0},
        )
        self.stack = self.moves("c", stack)
        self.far.append(self.moves(self.last, self.far[follow]))

    def fourth(self):
        self.far[3] = self.line.gate(self.far[3])[0]
        self.near = self.moves("c", self.far[3])

    def pieces(self):
        return [*self.far, self.stack, self.near]


def pack_attn_kernel(qkv_ref, out_ref, *refs):
    *whole_refs, quarter_ref, sems = refs
    pairs = []
    for index, own_ref in enumerate(whole_refs):
        layer = index % 2
        pairs += [(qkv_ref.at[layer], own_ref.at[0:3]), (out_ref.at[layer], own_ref.at[3])]
    copies = run_copies(pairs, sems, 0)
    wait_copies(copies[:2])
    quarter_ref[...] = whole_refs[0][quarter_index()]
    wait_copies(copies[2:])


def pack_attn(line, qkv, out):
    whole = ((4, PART, D), BF16)
    return line.call(
        "pack_attn",
        2,
        pack_attn_kernel,
        fixed(qkv, out),
        made(whole, whole, whole, whole, ((PART, D), BF16)),
        [pltpu.SemaphoreType.DMA((8,))],
    )


def pack_ffn_kernel(layer, in_ref, down_ref, pool_ref, own_ref, quarter_ref, sems):
    pairs = []
    for index in range(4):
        target = own_ref.at[index]
        pairs += [
            (in_ref.at[layer, :, index * D : (index + 1) * D], target.at[0:PART]),
            (
                down_ref.at[layer, index * PART : (index + 1) * PART],
                target.at[PART : 2 * PART],
            ),
            (
                pool_ref.at[layer, index * POOL_PART : (index + 1) * POOL_PART],
                target.at[2 * PART : FFN_ROWS],
            ),
        ]
    wait_copies(run_copies(pairs, sems, 0))
    quarter_ref[...] = own_ref[quarter_index()]


def pack_ffn(line, layer, ffn_in, ffn_out, pool):
    return line.call(
        "pack_ffn%d" % layer,
        3,
        functools.partial(pack_ffn_kernel, layer),
        fixed(ffn_in, ffn_out, pool),
        made(((4, FFN_ROWS, D), BF16), ((FFN_ROWS, D), BF16)),
        [pltpu.SemaphoreType.DMA((12,))],
    )


def pack_small_kernel(
    qkv_bias, out_bias, gain, shift, in_bias, down_bias, pool_bias, class_weight, packed_ref
):
    for layer in range(LAYERS):
        packed_ref[layer, QB : VB + 1] = qkv_bias[layer].astype(F32)
        packed_ref[layer, OB : OB + 1] = out_bias[layer : layer + 1].astype(F32)
        packed_ref[layer, G0 : G1 + 1] = gain[layer].astype(F32)
        packed_ref[layer, S0 : S1 + 1] = shift[layer].astype(F32)
        for index in range(4):
            value = in_bias[layer : layer + 1, index * PART : (index + 1) * PART]
            packed_ref[layer, 7 + index : 8 + index] = value.astype(F32)
        packed_ref[layer, FB : FB + 1] = down_bias[layer : layer + 1].astype(F32)
        packed_ref[layer, PB : PB + 1] = pool_bias[layer : layer + 1].astype(F32)
        for cls in range(CLASSES):
            value = class_weight[cls, layer : layer + 1].astype(F32)
            packed_ref[layer, CW + cls : CW + cls + 1] = value


def arrange_kernel(own, core, row, both, shards_ref, small_ref, bias_ref):
    shard = shard_index()
    for slot, ref in enumerate((own, core, row, both)):
        shards_ref[shard ^ slot] = ref[...]
    for part in range(SHARDS):
        for layer in range(LAYERS):
            lanes = slice(part * PART, (part + 1) * PART)
            small_ref[layer, :, lanes] = shards_ref[part, layer]
            for index in range(4):
                target = slice(index * PART, (index + 1) * PART)
                value = shards_ref[part, layer, 7 + index : 8 + index]
                bias_ref[layer, part : part + 1, target] = value


def arrange(line, moves, packed):
    core, row = moves("c", packed), moves("y", packed)
    return line.call(
        "arrange",
        1,
        arrange_kernel,
        near(packed, core, row, moves("d", packed)),
        made(
            ((SHARDS, LAYERS, 16, PART), F32),
            ((LAYERS, 16, D), F32),
            ((LAYERS, SHARDS, D), F32),
        ),
    )


def load_attn_weights(refs, slots, sems, start=0):
    here = quarter_index()
    copies = []
    for slot in range(2):
        if len(refs) == 2:
            pairs = [(refs[slot], slots.at[slot])]
        else:
            pieces = refs[0:4] if slot == 0 else [refs[4].at[0], refs[4].at[1], refs[4].at[2], refs[5]]
            pairs = [(piece, slots.at[slot, here ^ index]) for index, piece in enumerate(pieces)]
        copies.append(run_copies(pairs, sems, start + len(pairs) * slot))
    return copies


def attn_forward_kernel(layer, half, x_ref, *refs):
    if half:
        (shard_small, small, total_in), refs = refs[:3], refs[3:]
        count = 2 if layer or "pair0" not in FORWARD else 6
        weights, refs = refs[:count], refs[count:]
        qkv_ref, probs_ref, context_ref, normed_ref, rstd_ref, low_ref, slots, sems = refs
    else:
        shard_small, weights, refs = refs[0], refs[1:3], refs[3:]
        qkv_ref, probs_ref, context_ref, total_ref, slots, sems = refs
    copies = load_attn_weights(weights, slots, sems)
    shard = shard_index()
    x = x_ref[...]
    if half:
        total = total_in[...] + small[layer, OB : OB + 1].astype(F32)
    else:
        total = x.astype(F32)
    for slot in range(2):
        wait_copies(copies[slot])
        biases = shard_small[shard ^ (2 * half + slot), layer]
        parts = []
        for part in range(3):
            value = nt(x, slots[slot, part])
            if part != 1:
                row = QB if part == 0 else VB
                value = value + biases[row : row + 1].astype(F32)
            value = value.astype(BF16)
            qkv_ref[slot, part] = value
            parts.append(value)
        query, key, val = parts
        places = [
            (
                slice(seq * SEQ, (seq + 1) * SEQ),
                slice(head * HEAD_DIM, (head + 1) * HEAD_DIM),
            )
            for seq in range(2)
            for head in range(PART // HEAD_DIM)
        ]
        scores = jnp.stack([nt(query[at], key[at]) for at in places]) * HEAD_DIM ** (-0.5)
        shifted = jnp.exp(scores - jnp.max(scores, -1, keepdims=True))
        probs = shifted * (1.0 / jnp.sum(shifted, -1, keepdims=True))
        probs_ref[slot] = probs
        low = probs.astype(BF16)
        heads = [nn(low[index], val[at]) for index, at in enumerate(places)]
        half_heads = len(heads) // 2
        context = jnp.concatenate(
            [
                jnp.concatenate(heads[:half_heads], -1),
                jnp.concatenate(heads[half_heads:], -1),
            ],
            0,
        ).astype(BF16)
        context_ref[slot] = context
        total = total + nn(context, slots[slot, 3])
    if half == 0:
        total_ref[...] = total
        return
    normed, rstd = normalise(total)
    normed_ref[...] = normed
    rstd_ref[...] = rstd
    middle = normed * small[layer, G0 : G0 + 1].astype(F32) + small[layer, S0 : S0 + 1].astype(F32)
    low_ref[...] = middle.astype(BF16)


def attn_forward(line, layer, half, x, inputs, weights):
    tokens = x.shape[0]
    outs = [
        ((2, 3, tokens, PART), BF16),
        ((2, 6, SEQ, SEQ), F32),
        ((2, tokens, PART), BF16),
        ((tokens, D), F32),
    ]
    if half:
        outs += [((tokens, 1), F32), ((tokens, D), BF16)]
    return line.call(
        "attn_forward%d%d" % (layer, half),
        7,
        functools.partial(attn_forward_kernel, layer, half),
        near(x, *inputs) + fixed(*weights),
        made(*outs),
        [pltpu.VMEM((2, 4, PART, D), BF16), pltpu.SemaphoreType.DMA((8,))],
    )


def load_ffn_weights(refs, up, down, pool, sems, down_first=False):
    here = quarter_index()
    shard = shard_index()
    ups, downs, pools = [], [], []

    def block_of(source, owner, block):
        ups.append((source.at[0:PART], up.at[block, rows_at(owner, PART)]))
        downs.append((source.at[PART : 2 * PART], down.at[owner, rows_at(block, PART)]))
        if pool is not None:
            target = pool.at[rows_at(owner * 4 + block, POOL_PART)]
            pools.append((source.at[2 * PART : FFN_ROWS], target))

    wholes = refs if len(refs) == 4 else refs[:2]
    for slot, whole in enumerate(wholes):
        for block in range(4):
            block_of(whole.at[block], shard ^ slot, block)
    if len(refs) == 8:
        pieces = [*refs[2:6], refs[6].at[0], refs[6].at[1], refs[6].at[2], refs[7]]
        for index, piece in enumerate(pieces):
            block_of(piece, shard ^ (2 + index // 4), here ^ (index % 4))
    order = (downs, ups, pools) if down_first else (ups, downs, pools)
    first = run_copies(order[0], sems, 0)
    second = run_copies(order[1], sems, len(ups))
    return first, second, run_copies(pools, sems, 2 * len(ups))


def ffn_forward_kernel(
    layer, labels_ref, class_bias_ref, x_ref, normed_ref, low_ref, small, in_bias, *refs
):
    count = 8
    weights, refs = refs[:count], refs[count:]
    if layer:
        (prior_out, prior_logits, prior_ramp), refs = refs[:3], refs[3:]
    act_ref, act_send_ref, slope_ref, normed_two_ref, rstd_two_ref, first_grad_ref = refs[:6]
    out_ref, logits_ref, ramp_ref, up, down, pool, acts, lows, slopes, sems, out_sems = refs[6:]
    ups, downs, pools = load_ffn_weights(weights, up, down, pool, sems)
    leaving = run_copies([(x_ref, act_send_ref.at[2, :, 0:D])], out_sems, 0)
    normed = normed_ref[...]
    low = low_ref[...]

    def row(index):
        return small[layer, index : index + 1].astype(F32)

    total = normed * row(G0) + row(S0) + row(FB)
    for part in range(4):
        lows[part, :, 0:PART] = low[:, part * PART : (part + 1) * PART]
        lows[part, :, PART:] = jnp.zeros((low.shape[0], WIDE - D - PART), BF16)
    wait_copies(ups)
    for block in range(4):
        pre_act = nn(low, up[block]) + in_bias[layer, block : block + 1].astype(F32)
        cumulative = 0.5 * (1.0 + lax.erf(pre_act * ROOT_HALF))
        act = (pre_act * cumulative).astype(BF16)
        density = jnp.exp(-0.5 * pre_act * pre_act) * DENSITY_SCALE
        acts[block] = act
        slopes[block] = cumulative + pre_act * density
        leaving += run_copies([(slopes.at[block], slope_ref.at[block])], out_sems, 1 + block)
        if block == 0:
            wait_copies(downs)
        total = total + nn(act, down[block])
    shard = shard_index()
    pairs = []
    for slot in range(4):
        target = (act_send_ref if slot & 1 else act_ref).at[slot >> 1]
        pairs.append((acts.at[shard ^ slot], target.at[:, 0:D]))
        pairs.append((lows.at[shard ^ slot], target.at[:, D:WIDE]))
    leaving += run_copies(pairs, out_sems, 5)
    wait_copies(pools)
    normed_two, rstd_two = normalise(total)
    normed_two_ref[...] = normed_two
    rstd_two_ref[...] = rstd_two
    output = (normed_two * row(G1) + row(S1)).astype(BF16)

    first = jnp.concatenate([output[0:1], output[SEQ : SEQ + 1]], 0).astype(F32)
    first = jnp.concatenate([first, jnp.zeros((14, D), F32)], 0).astype(BF16)
    pool_weight = pool[...]
    pooled = jnp.tanh(nn(first, pool_weight) + row(PB))
    wide = pooled.astype(BF16).astype(F32)
    lanes = lax.broadcasted_iota(jnp.int32, (16, 128), 1)
    rows = lax.broadcasted_iota(jnp.int32, (16, 128), 0)
    logits = jnp.zeros((16, 128), F32)
    for cls in range(CLASSES):
        value = jnp.sum(wide * row(CW + cls), -1, keepdims=True)
        value = value + class_bias_ref[layer, cls]
        logits = jnp.where(lanes == cls, value, logits)
    valid = lanes < CLASSES
    peak = jnp.max(jnp.where(valid, logits, -jnp.inf), -1, keepdims=True)
    shifted = jnp.where(valid, jnp.exp(logits - peak), 0.0)
    soft = shifted / jnp.sum(shifted, -1, keepdims=True)
    label = jnp.where(rows == 0, labels_ref[0], labels_ref[1])
    logit_grad = (soft - (lanes == label).astype(F32)).astype(BF16)
    logit_wide = logit_grad.astype(F32)
    back = jnp.zeros((16, D), F32)
    for cls in range(CLASSES):
        picked = jnp.sum(jnp.where(lanes == cls, logit_wide, 0.0), -1, keepdims=True)
        back = back + picked * row(CW + cls)
    pool_grad = (back * (1.0 - pooled * pooled)).astype(BF16)
    first_grad_ref[...] = nt(pool_grad, pool_weight)[0:8]
    padded = jnp.concatenate([logit_wide[0:2], jnp.zeros((2, D - 128), F32)], -1)
    ramp = jnp.concatenate(
        [first.astype(F32)[0:2], pool_grad.astype(F32)[0:2], wide[0:2], padded], 0
    ).astype(BF16)
    if layer:
        out_ref[0] = prior_out[...]
        logits_ref[0] = prior_logits[...]
        ramp_ref[0] = prior_ramp[...]
        out_ref[1] = output
        logits_ref[1] = logits[0:8]
        ramp_ref[1] = ramp
    else:
        out_ref[...] = output
        logits_ref[...] = logits[0:8]
        ramp_ref[...] = ramp
    wait_copies(leaving)


def ffn_forward(line, layer, labels, class_bias, x, normed, low, small, in_bias, weights, prior):
    tokens = low.shape[0]
    smem = pl.BlockSpec(memory_space=pltpu.SMEM)
    stack = (2,) if layer else ()
    return line.call(
        "ffn_forward%d" % layer,
        12,
        functools.partial(ffn_forward_kernel, layer),
        [(labels, smem), (class_bias, smem)]
        + near(x, normed, low, small, in_bias)
        + fixed(*weights)
        + near(*prior),
        sent(
            ((2, tokens, WIDE), BF16),
            ((3, tokens, WIDE), BF16),
            ((4, tokens, D), F32),
        )
        + made(
            ((tokens, D), F32),
            ((tokens, 1), F32),
            ((8, D), F32),
            ((*stack, tokens, D), BF16),
            ((*stack, 8, 128), F32),
            ((*stack, 8, D), BF16),
        ),
        [
            pltpu.VMEM((4, D, D), BF16),
            pltpu.VMEM((SHARDS, D, D), BF16),
            pltpu.VMEM((D, D), BF16),
            pltpu.VMEM((4, tokens, D), BF16),
            pltpu.VMEM((4, tokens, WIDE - D), BF16),
            pltpu.VMEM((4, tokens, D), F32),
            pltpu.SemaphoreType.DMA((48,)),
            pltpu.SemaphoreType.DMA((13,)),
        ],
    )


def ffn_backward_kernel(
    layer, grad_ref, first_ref, normed_two_ref, rstd_two_ref, slope_ref, normed_ref, rstd_ref,
    small, *refs
):
    pairs_ref, rows_ref, low_ref, smalls_ref, up, down, pairs, sems, out_sems = refs[-9:]
    downs, ups, _ = load_ffn_weights(refs[:-9], up, down, None, sems, True)

    def row(index):
        return small[layer, index : index + 1].astype(F32)

    grad = grad_ref[...].astype(F32)
    index = lax.broadcasted_iota(jnp.int32, grad.shape, 0)
    grad = grad + jnp.where(index == 0, first_ref[0:1], 0.0)
    grad = grad + jnp.where(index == SEQ, first_ref[1:2], 0.0)
    res_two, gain_two, shift_two = norm_back(grad, normed_two_ref[...], rstd_two_ref[...], row(G1))
    ffn_grad = res_two.astype(BF16)
    pairs[4] = ffn_grad
    leaving = run_copies([(pairs.at[4], pairs_ref.at[4])], out_sems, 4)
    wait_copies(downs)
    middle_grad = res_two
    for block in range(4):
        act_grad = nt(ffn_grad, down[block])
        pre_grad = (act_grad * slope_ref[block]).astype(BF16)
        pairs[block] = pre_grad
        leaving += run_copies([(pairs.at[block], pairs_ref.at[block])], out_sems, block)
        if block == 0:
            wait_copies(ups)
        smalls_ref[block : block + 1] = jnp.sum(pre_grad.astype(F32), 0, keepdims=True)
        middle_grad = middle_grad + nt(pre_grad, up[block])
    res_one, gain_one, shift_one = norm_back(middle_grad, normed_ref[...], rstd_ref[...], row(G0))
    rows_ref[...] = res_one
    low = res_one.astype(BF16)
    low_ref[...] = low
    smalls_ref[4:5] = jnp.sum(ffn_grad.astype(F32), 0, keepdims=True)
    smalls_ref[5:6] = jnp.sum(low.astype(F32), 0, keepdims=True)
    smalls_ref[6:7] = gain_one
    smalls_ref[7:8] = gain_two
    smalls_ref[8:9] = shift_one
    smalls_ref[9:10] = shift_two
    wait_copies(leaving)


def ffn_backward(
    line, layer, grad, first_grad, normed_two, rstd_two, slope, normed, rstd, small, weights
):
    tokens = grad.shape[0]
    return line.call(
        "ffn_backward%d" % layer,
        11,
        functools.partial(ffn_backward_kernel, layer),
        near(grad, first_grad, normed_two, rstd_two, slope, normed, rstd, small)
        + away(*weights),
        sent(((5, tokens, D), BF16))
        + made(
            ((tokens, D), F32),
            ((tokens, D), BF16),
            ((10, D), F32),
        ),
        [
            pltpu.VMEM((4, D, D), BF16),
            pltpu.VMEM((SHARDS, D, D), BF16),
            pltpu.VMEM((5, tokens, D), BF16),
            pltpu.SemaphoreType.DMA((32,)),
            pltpu.SemaphoreType.DMA((5,)),
        ],
    )


def place_pieces(groups, natural, outs, y, sems):
    here = quarter_index()
    pairs = []
    for index, (order, first, count) in enumerate(groups):
        keep_ref, send_ref = outs[2 * index : 2 * index + 2]
        rows = slice(first, first + count)
        for x in range(2):
            for a in range(2):
                if not order:
                    target, unit, place = (send_ref if y else keep_ref), 2 * a + x, 2 * a + x
                else:
                    bits = {"y": y, "x": x, "a": a}
                    outer, middle, inner = (bits[dim] for dim in order)
                    target = send_ref if outer else keep_ref
                    unit, place = (2 * a + x) ^ here, 2 * middle + inner
                pairs.append((natural.at[y, unit, rows], target.at[place]))
    return run_copies(pairs, sems, y * len(pairs))


def piece_shapes(groups):
    shapes = []
    for _, _, count in groups:
        shapes += [((4, count, D), BF16)] * 2
    return shapes


def ffn_weights_kernel(groups, act_ref, act_near_ref, pairs_ref, pairs_near_ref, *refs):
    outs, (natural, sems) = refs[:-2], refs[-2:]
    leaving = []
    for slot in (1, 0):
        mine, other = act_ref[slot], act_near_ref[slot]
        down = tn(mine[:, 0:D], pairs_ref[4]) + tn(other[:, 0:D], pairs_near_ref[4])
        down = down.astype(BF16)
        for block in range(4):
            natural[slot, block, PART : 2 * PART] = down[block * PART : (block + 1) * PART]
            up = tn(mine[:, D : D + PART], pairs_ref[block])
            up = up + tn(other[:, D : D + PART], pairs_near_ref[block])
            natural[slot, block, 0:PART] = up.astype(BF16)
        leaving += place_pieces(groups, natural, outs, slot, sems)
    wait_copies(leaving)


def ffn_weight_grads(line, layer, groups, act, act_near, pairs, pairs_near):
    return line.call(
        "ffn_weight_grads%d" % layer,
        8,
        functools.partial(ffn_weights_kernel, groups),
        near(act, act_near, pairs, pairs_near),
        sent(*piece_shapes(groups)),
        [pltpu.VMEM((2, 4, 2 * PART, D), BF16), pltpu.SemaphoreType.DMA((8 * len(groups),))],
    )


def attn_weights_kernel(
    groups, x_ref, acts_near_ref, grad_ref, pairs_ref, near_ref, *refs
):
    outs, (natural, sems) = refs[-2 - 2 * len(groups) : -2], refs[-2:]
    leaving = []
    cut = 3 * PART
    tokens = x_ref.shape[0]
    x_near = acts_near_ref[2, :, 0:D]
    grad_near = near_ref[2 * tokens : 3 * tokens]
    if len(refs) > 2 + 2 * len(groups):
        smalls_ref, by_shard = refs[0], refs[-3]
        outs = refs[1:-3]
        smalls = []
        for layer in range(LAYERS):
            start = 3 * tokens + 32 * layer
            high = near_ref[start : start + 16].astype(F32)
            rest = near_ref[start + 16 : start + 32].astype(F32)
            smalls.append(smalls_ref[layer] + (high + rest)[0:12])
        for part in range(SHARDS):
            lanes = slice(part * PART, (part + 1) * PART)
            for layer in range(LAYERS):
                row = 3 * layer
                by_shard[part, row : row + 1] = smalls[layer][part : part + 1]
                for item in range(8):
                    target = slice((item % 4) * PART, (item % 4 + 1) * PART)
                    value = smalls[layer][4 + item : 5 + item, lanes]
                    by_shard[part, row + 1 + item // 4 : row + 2 + item // 4, target] = value
            by_shard[part, 6:16] = jnp.zeros((10, D), F32)
        shard = shard_index()
        for slot in range(2):
            natural[slot, 0, PART:TALL] = by_shard[shard ^ (2 * slot)].astype(BF16)
            for unit in range(1, 4):
                natural[slot, unit, PART:TALL] = jnp.zeros((TALL - PART, D), BF16)
    for slot in (1, 0):
        mine, other = pairs_ref[slot], near_ref[slot * tokens : (slot + 1) * tokens]
        value = tn(mine[:, 0:cut], x_ref[...]) + tn(other[:, 0:cut], x_near)
        value = value.astype(BF16)
        for unit in range(3):
            natural[slot, unit, 0:PART] = value[unit * PART : (unit + 1) * PART]
        value = tn(mine[:, cut:D], grad_ref[...]) + tn(other[:, cut:D], grad_near)
        natural[slot, 3, 0:PART] = value.astype(BF16)
        leaving += place_pieces(groups, natural, outs, slot, sems)
    wait_copies(leaving)


def attn_weight_grads(line, layer, groups, *operands):
    return line.call(
        "attn_weight_grads%d" % layer,
        5,
        functools.partial(attn_weights_kernel, groups),
        near(*operands),
        sent(*piece_shapes(groups)),
        ([pltpu.VMEM((SHARDS, 16, D), F32)] if len(operands) > 5 else [])
        + [
            pltpu.VMEM((2, 4, groups[0][2], D), BF16),
            pltpu.SemaphoreType.DMA((8 * len(groups),)),
        ],
    )


def attn_backward_kernel(
    layer, res_ref, grad_ref, smalls_in_ref, *refs
):
    count = 10 if layer or "pair0" not in FORWARD else 14
    kept, weights, refs = refs[:6], refs[6:count], refs[count:]
    if layer == 0:
        prior, refs = refs[0], refs[1:]
    pairs_ref, pairs_send_ref, rows_ref, smalls_ref, slots, sems, sums = refs
    tokens = grad_ref.shape[0]
    copies = load_attn_weights(weights[:2], slots.at[0:2], sems)
    copies += load_attn_weights(weights[2:], slots.at[2:4], sems, 2)
    shard = shard_index()
    grad = grad_ref[...]
    total = res_ref[...]
    for slot in range(4):
        wait_copies(copies[slot])
        half, index = slot >> 1, slot & 1
        qkv_ref, probs_ref, context_ref = kept[3 * half : 3 * half + 3]
        context_grad = nt(grad, slots[slot, 3]).astype(BF16)
        places = [
            (
                slice(seq * SEQ, (seq + 1) * SEQ),
                slice(head * HEAD_DIM, (head + 1) * HEAD_DIM),
            )
            for seq in range(2)
            for head in range(PART // HEAD_DIM)
        ]
        query, key, val = (qkv_ref[index, part] for part in range(3))
        probs = probs_ref[index]
        prob_grad = jnp.stack([nt(context_grad[at], val[at]) for at in places])
        mean = jnp.sum(prob_grad * probs, -1, keepdims=True)
        score_grad = (probs * (prob_grad - mean)).astype(BF16)
        probs_low = probs.astype(BF16)
        scale = HEAD_DIM ** (-0.5)
        heads = [
            [nn(score_grad[i], key[at]) * scale for i, at in enumerate(places)],
            [tn(score_grad[i], query[at]) * scale for i, at in enumerate(places)],
            [tn(probs_low[i], context_grad[at]) for i, at in enumerate(places)],
        ]
        half_heads = len(places) // 2
        seq_rows = [
            [jnp.concatenate(group[:half_heads], -1), jnp.concatenate(group[half_heads:], -1)]
            for group in heads
        ]
        for part in range(3):
            value = jnp.concatenate(seq_rows[part], 0).astype(BF16)
            if slot & 1:
                rows = slice(half * tokens, (half + 1) * tokens)
                pairs_send_ref[rows, part * PART : (part + 1) * PART] = value
            else:
                pairs_ref[half, :, part * PART : (part + 1) * PART] = value
            if part != 1:
                sums[shard ^ slot, part // 2] = jnp.sum(value.astype(F32), 0, keepdims=True)
            total = total + nn(value, slots[slot, part])
        if slot & 1:
            pairs_send_ref[half * tokens : (half + 1) * tokens, 3 * PART : D] = context_ref[index]
        else:
            pairs_ref[half, :, 3 * PART : D] = context_ref[index]
    pairs_send_ref[2 * tokens : 3 * tokens] = grad
    rows_ref[...] = total.astype(rows_ref.dtype)
    own = [
        jnp.concatenate([sums[part, index] for part in range(SHARDS)], -1) for index in range(2)
    ]
    if layer:
        smalls_ref[0:10] = smalls_in_ref[...]
        smalls_ref[10:11] = own[0]
        smalls_ref[11:12] = own[1]
    else:
        smalls_ref[1] = prior[...]
        smalls_ref[0, 0:10] = smalls_in_ref[...]
        smalls_ref[0, 10:11] = own[0]
        smalls_ref[0, 11:12] = own[1]
        for index in range(LAYERS):
            value = smalls_ref[index]
            high = value.astype(BF16)
            rest = (value - high.astype(F32)).astype(BF16)
            start = 3 * tokens + 32 * index
            pairs_send_ref[start : start + 16] = jnp.concatenate(
                [high, jnp.zeros((4, D), BF16)], 0
            )
            pairs_send_ref[start + 16 : start + 32] = jnp.concatenate(
                [rest, jnp.zeros((4, D), BF16)], 0
            )


def attn_backward(line, layer, res, grad, kept, smalls, weights, prior):
    tokens = grad.shape[0]
    return line.call(
        "attn_backward%d" % layer,
        15,
        functools.partial(attn_backward_kernel, layer),
        near(res, grad, smalls, *kept) + away(*weights) + near(*prior),
        made(
            ((2, tokens, D), BF16),
            ((3 * tokens + (0 if layer else 64), D), BF16),
            ((tokens, D), F32 if layer else BF16),
            ((12, D) if layer else (2, 12, D), F32),
        ),
        [
            pltpu.VMEM((4, 4, PART, D), BF16),
            pltpu.SemaphoreType.DMA((12,)),
            pltpu.VMEM((SHARDS, 2, 1, PART), F32),
        ],
    )


def halve_kernel(keep_ref, came_ref, low_ref, high_ref):
    half = low_ref.shape[0]
    low_ref[...] = keep_ref[0:half] + came_ref[0:half]
    high_ref[...] = keep_ref[half:] + came_ref[half:]


def add_kernel(keep_ref, came_ref, sum_ref):
    sum_ref[...] = keep_ref[...] + came_ref[...]


def reduction(line, moves, name, order, back, keep, send):
    shape = keep.shape
    micros = 1 + shape[1] / 192
    if not order:
        came = moves("y", send)
        yield
        total = line.call(
            "add_%s" % name, micros, add_kernel, near(keep, came), made((shape, BF16))
        )[0]
        yield (back, lax.psum(total, DP))
    came = moves(order[0], send)
    for step, dim in enumerate(order[1:]):
        yield
        half = (keep.shape[0] // 2, *shape[1:])
        keep, send = line.call(
            "halve_%s%d" % (name, step), micros, halve_kernel, near(keep, came),
            made((half, BF16), (half, BF16)),
        )
        came = moves(dim, send)
    yield
    keep, came = keep[0], came[0]
    total = line.call(
        "add_%s" % name, micros, add_kernel, near(keep, came), made((shape[1:], BF16))
    )[0]
    came = moves("b", total)
    for bit in moves.more():
        yield
        total = line.call(
            "more_%s%d" % (name, bit), micros, add_kernel, near(total, came),
            made((shape[1:], BF16)),
        )[0]
        came = moves.place(bit, total)
    yield
    total = line.call(
        "last_%s" % name, micros, add_kernel, near(total, came), made((shape[1:], BF16))
    )[0]
    came = moves(back[0], total)
    yield
    both = line.call(
        "both_%s" % name, micros, both_kernel, near(total, came), made(((2, *shape[1:]), BF16))
    )[0]
    yield (back, both, moves(back[1], both))


def join_kernel(one_ref, two_ref, joint_ref):
    count = one_ref.shape[0]
    joint_ref[0:count] = one_ref[...]
    joint_ref[count : 2 * count] = two_ref[...]


def join(line, one, two):
    shape = (2 * one.shape[0], *one.shape[1:])
    return line.call("join%d" % shape[0], 1, join_kernel, near(one, two), made((shape, BF16)))[0]


def both_kernel(one_ref, two_ref, both_ref):
    both_ref[0] = one_ref[...]
    both_ref[1] = two_ref[...]


def unpack_kernel(back, first, targets, prior, *refs):
    values = 2 if back else 1
    quarters = refs[:values]
    outs = refs[values + prior : -2]
    whole, sems = refs[-2:]
    here = quarter_index()
    count = whole.shape[1]
    for index in range(4):
        if not back:
            whole[index] = quarters[0][index, first : first + count].astype(F32)
            continue
        bits = {back[0]: index & 1, back[1]: index >> 1}
        relative = 2 * bits["a"] + bits["x"]
        quarter = quarters[index >> 1][index & 1, first : first + count]
        whole[relative ^ here] = quarter.astype(F32)
    if count == TALL:
        qkv_bias, out_bias, gain, shift, in_bias, down_bias = outs[len(targets) :]
        for layer in range(LAYERS):
            row = PART + 3 * layer

            def item(index):
                at = row + 1 + index // 4
                return whole[0, at : at + 1, (index % 4) * PART : (index % 4 + 1) * PART]

            in_bias[layer : layer + 1] = whole[0, row : row + 1]
            down_bias[layer : layer + 1] = item(0)
            out_bias[layer : layer + 1] = item(1)
            for index in range(2):
                gain[layer, index : index + 1] = item(2 + index)
                shift[layer, index : index + 1] = item(4 + index)
                qkv_bias[layer, index : index + 1] = item(6 + index)
    pairs = [
        (whole.at[unit, 0:PART], outs[which].at[where])
        for unit, which, where in targets_of(targets)
    ]
    wait_copies(run_copies(pairs, sems, 0))


def targets_of(targets):
    return [(unit, which, where) for which, places in enumerate(targets) for unit, where in places]


SMALL_SHAPES = (
    (LAYERS, 2, PART), (LAYERS, PART), (LAYERS, 2, PART), (LAYERS, 2, PART), (LAYERS, D), (LAYERS, PART)
)


def unpack(line, name, quarters, first, shapes, targets, prior):
    back, *values = quarters
    aliases = {len(values) + index: index for index in range(len(prior))}
    count = TALL if values[0].shape[1] == TALL else PART
    outs = [(shape, F32, anywhere()) for shape in shapes]
    if count == TALL:
        outs += made(*[(shape, F32) for shape in SMALL_SHAPES])
    return line.call(
        name,
        3,
        functools.partial(unpack_kernel, back, first, targets, len(prior)),
        near(*values) + away(*prior),
        outs,
        [pltpu.VMEM((4, count, D), F32), pltpu.SemaphoreType.DMA((4,))],
        aliases,
    )


def unpack_up(line, layer, quarters, first, prior):
    places = [(unit, (layer, slice(None), slice(unit * D, (unit + 1) * D))) for unit in range(4)]
    return unpack(
        line, "unpack_up%d" % layer, quarters, first, [(LAYERS, PART, FF)], [places], prior
    )


def unpack_down(line, layer, quarters, first, prior):
    places = [(unit, (layer, slice(unit * PART, (unit + 1) * PART))) for unit in range(4)]
    return unpack(
        line, "unpack_down%d" % layer, quarters, first, [(LAYERS, D, D)], [places], prior
    )


def unpack_attn(line, layer, quarters, first, prior):
    return unpack(
        line,
        "unpack_attn%d" % layer,
        quarters,
        first,
        [(LAYERS, 3, PART, D), (LAYERS, PART, D)],
        [[(unit, (layer, unit)) for unit in range(3)], [(3, (layer,))]],
        prior,
    )


def pool_grads(ramp, shard):
    ramp = ramp.reshape(ramp.shape[0], LAYERS, 4, 2, D)
    ramp = jnp.transpose(ramp, (1, 2, 0, 3, 4)).reshape(LAYERS, 4, -1, D)
    first, pool_grad, pooled, logit_grad = (ramp[:, part] for part in range(4))
    logit_grad = logit_grad[:, :, 0:CLASSES]
    own_first = lax.dynamic_slice_in_dim(first, shard * PART, PART, 2)
    own_pooled = lax.dynamic_slice_in_dim(pooled, shard * PART, PART, 2)
    pool_weight_grad = jnp.einsum("lnd,lne->lde", own_first, pool_grad, preferred_element_type=F32)
    class_weight_grad = jnp.einsum(
        "lnd,lnc->ldc", own_pooled, logit_grad, preferred_element_type=F32
    )
    class_bias_grad = jnp.sum(logit_grad.astype(F32), 1)
    own_pool = lax.dynamic_slice_in_dim(pool_grad, shard * PART, PART, 2)
    pool_bias_grad = jnp.sum(own_pool.astype(F32), 1)
    return pool_weight_grad, pool_bias_grad, class_weight_grad, class_bias_grad


ROUTES = {
    "f1": ("yxa", "ax"),
    "a1": ("axy", "ax"),
    "f0": ("axy", "xa"),
    "a0": ("xya", "xa"),
}
FORWARD_NAMES = (
    "ffn0", "small0", "arrange0", "attn0", "row0", "near0", "second0", "ffn1", "third0",
    "cross0", "swap0", "far0", "meet0", "second1", "fourth0", "row1", "block0", "third1",
    "near1", "cross1", "swap1", "far1", "fourth1", "block1",
)
FORWARD = [FORWARD_NAMES[index] for index in (
    0, 1, 2, 3, 4, 5, 6, 7, 8, 9, 10, 11, 12, 13, 14, 15, 16, 17, 18, 19, 20, 21, 22, 23,
)]
SCHEDULE_NAMES = (
    "R0", "F1", "R1", "A1", "FW1", "AW1", "F0", "A0", "FW0", "AW0", "a1", "f1", "a0", "f0",
    "Ua1", "Ua0", "P1", "Uf1", "Uf0",
)
SCHEDULE = [SCHEDULE_NAMES[index] for index in (
    0, 1, 2, 3, 2, 4, 2, 5, 2, 6, 2, 7, 8, 9, 10, 11, 12, 10, 12, 13, 10, 11, 10, 12, 11, 12,
    13, 10, 12, 13, 14, 11, 15, 13, 11, 16, 13, 17, 18,
)]


def on_device(
    mesh,
    hidden_in,
    out_cotangent,
    labels,
    qkv_weight,
    qkv_bias,
    out_weight,
    out_bias,
    norm_gain,
    norm_shift,
    ffn_in,
    ffn_in_bias,
    ffn_out,
    ffn_out_bias,
    pool_weight,
    pool_bias,
    class_weight,
    class_bias,
):
    moves = Moves(mesh)
    line = Line()
    shard = shard_index()
    qkv_turned = jnp.swapaxes(qkv_weight, 2, 3)

    class_bias_wide = class_bias.astype(F32)
    ffn_own, ffn_far, attn_own, attn_far = [None] * 2, [None] * 2, [None] * 2, [None] * 2
    kept, held = [None] * 2, {"x0": hidden_in}

    def go(name):
        layer = int(name[-1])
        part = name[:-1]
        if part == "small":
            held["packed"] = line.call(
                "pack_small",
                1,
                pack_small_kernel,
                near(
                    qkv_bias, out_bias, norm_gain, norm_shift, ffn_in_bias, ffn_out_bias, pool_bias,
                    jnp.transpose(class_weight, (2, 0, 1)),
                ),
                made(((LAYERS, 16, PART), F32)),
            )[0]
        elif part == "arrange":
            held["small"] = arrange(line, moves, held["packed"])
        elif part == "ffn":
            pack, quarter = pack_ffn(line, layer, ffn_in, ffn_out, pool_weight)
            ffn_own[layer] = [pack]
            ffn_far[layer] = Spread(line, moves, quarter, "a" if layer else "x")
        elif part == "attn":
            *own, quarter = pack_attn(line, qkv_turned, out_weight)
            held["leaving"] = own[2:]
            if "pair0" in FORWARD:
                attn_far[0] = Spread(line, moves, quarter, "a")
            for index, value in enumerate(own[:2]):
                attn_own[index] = [value, moves("c", value)]
        elif part == "second":
            ffn_far[layer].second()
        elif part == "third":
            ffn_far[layer].third()
        elif part == "fourth":
            ffn_far[layer].fourth()
        elif part == "pair":
            attn_far[0].second()
        elif part == "last":
            attn_far[0].third()
        elif part == "end":
            attn_far[0].fourth()
            attn_far[0] = attn_far[0].pieces()
        elif part == "row":
            held["far%d" % layer] = moves("y", line.gate(held["leaving"][layer])[0])
        elif part == "cross":
            far = line.gate(held["far%d" % layer])[0]
            attn_far[layer] = [far, moves("c", far)]
        elif part == "swap":
            pack = line.gate(ffn_own[layer][0])[0]
            ffn_own[layer] = [pack, moves("c", pack)]
        elif part == "meet":
            line.waits = (*line.waits, ffn_own[layer][1], ffn_far[layer].stack)
        elif part == "near":
            shard_small, small, in_bias = held["small"]
            *attn_near, total = attn_forward(
                line, layer, 0, held["x%d" % layer], (shard_small,), attn_own[layer]
            )
            kept[layer] = [attn_near, total]
        elif part == "far":
            shard_small, small, in_bias = held["small"]
            attn_near, total = kept[layer]
            *attn_rest, normed, rstd, low = attn_forward(
                line, layer, 1, held["x%d" % layer], (shard_small, small, total), attn_far[layer]
            )
            kept[layer] = [(attn_near + attn_rest, normed, rstd), low]
        elif part == "block":
            shard_small, small, in_bias = held["small"]
            attention, low = kept[layer]
            x = held["x%d" % layer]
            if layer:
                line.waits = (*line.waits, kept[0][2][1])
            act, act_send, slope, normed_two, rstd_two, first_grad, *prior = ffn_forward(
                line, layer, labels, class_bias_wide, x, attention[1], low, small, in_bias,
                ffn_own[layer] + ffn_far[layer].pieces(), held.get("prior", ()),
            )
            act_near = moves("c", act_send)
            kept[layer] = (
                x, attention, (act, act_near), (slope, normed_two, rstd_two, first_grad)
            )
            held["prior"] = prior
            held["x1"] = prior[0]

    for name in FORWARD:
        go(name)
    ffn_weights = [ffn_own[layer] + ffn_far[layer].pieces() for layer in range(LAYERS)]
    nears = [kept[layer][2][1] for layer in range(LAYERS)]
    small = held["small"][1]
    block_outputs, logits, ramp = held["prior"]

    chains, results, state = {}, {}, {"grad": out_cotangent, "prior": ()}
    ramp_value = [ramp[None]]
    ramp_steps = [(HEAD, 1), (HEAD, 2)]
    bit = 1
    while bit < mesh.shape[DP]:
        ramp_steps.append((DP, bit))
        bit *= 2

    def begin(names, pieces):
        for index, name in enumerate(names):
            keep, send = pieces[2 * index : 2 * index + 2]
            chains[name] = reduction(line, moves, name, *ROUTES[name], keep, send)
            next(chains[name])

    def step(name):
        layer = int(name[-1])
        if name == "R0":
            ramp_value[0] = line.gate(ramp_value[0])[0]
        elif name[:-1] == "F":
            _, (_, normed, rstd), _, (slope, normed_two, rstd_two, first_grad) = kept[layer]
            pairs, res, low, rows = ffn_backward(
                line, layer, state["grad"], first_grad, normed_two, rstd_two, slope, normed, rstd,
                small, ffn_weights[layer],
            )
            state["ffn"] = (pairs, moves("c", pairs))
            state["low"] = low
            state["res"], state["rows"] = res, rows
            line.waits = (*line.waits, nears[layer])
        elif name[:-1] == "A":
            pairs, send, grad, smalls = attn_backward(
                line, layer, state["res"], state["low"], kept[layer][1][0], state["rows"],
                attn_own[layer] + attn_far[layer], state["prior"],
            )
            state["attn"] = (pairs, moves("c", send))
            state["grad"], state["prior"] = grad, (smalls,)
        elif name[:-1] == "FW":
            names = [key for key in ROUTES if key[-1] == name[-1] and key[0] != "a"]
            spans = {"f": (0, 2 * PART), "u": (0, PART), "d": (PART, PART)}
            groups = [(ROUTES[key][0], *spans[key[0]]) for key in names]
            begin(names, ffn_weight_grads(line, layer, groups, *kept[layer][2], *state["ffn"]))
        elif name[:-1] == "AW":
            key = "a" + name[-1]
            groups = [(ROUTES[key][0], 0, PART if layer else TALL)]
            operands = (kept[layer][0], kept[layer][2][1], state["low"], *state["attn"])
            if layer == 0:
                operands += state["prior"]
            begin([key], attn_weight_grads(line, layer, groups, *operands))
        elif name == "R1":
            for _ in range(max(1, len(ramp_steps) - 4)):
                axis, bit = ramp_steps.pop(0)
                came = lax.ppermute(ramp_value[0], AXES, flip(mesh, axis, bit))
                ramp_value[0] = join(line, ramp_value[0], came)
        elif name == "P1":
            state["pool"] = pool_grads(line.gate(ramp_value[0])[0], shard)
            line.waits = (*line.waits, *state["pool"])
        elif name[0] == "U":
            key = name[1:]
            while key not in results:
                results[key] = next(chains[key])
                if results[key] is None:
                    del results[key]
            if key[0] in "uf":
                state["up"] = unpack_up(line, layer, results[key], 0, state.get("up", ()))
            if key[0] in "df":
                first = PART if key[0] == "f" else 0
                state["down"] = unpack_down(line, layer, results[key], first, state.get("down", ()))
            if key[0] == "a":
                state["attn_out"] = unpack_attn(
                    line, layer, results[key], 0, state.get("attn_out", ())
                )
        else:
            result = next(chains[name], None)
            if result is not None:
                results[name] = result

    for name in SCHEDULE:
        step(name)
    qkv_grad, out_grad, qkv_bias_grad, out_bias_grad, *smalls = state["attn_out"]
    gain_grad, shift_grad, in_bias_grad, down_bias_grad = smalls
    pool_weight_grad, pool_bias_grad, class_weight_grad, class_bias_grad = state["pool"]
    return (
        block_outputs,
        logits[:, 0:2, 0:CLASSES],
        state["grad"],
        jnp.swapaxes(qkv_grad, 2, 3),
        qkv_bias_grad,
        out_grad,
        out_bias_grad,
        gain_grad,
        shift_grad,
        state["up"][0],
        in_bias_grad,
        state["down"][0],
        down_bias_grad,
        pool_weight_grad,
        pool_bias_grad,
        class_weight_grad,
        class_bias_grad,
    )


def solution(mesh):
    return jax.shard_map(
        functools.partial(on_device, mesh),
        mesh=mesh,
        in_specs=(
            P((DP, HEAD), None),
            P((DP, HEAD), None),
            P((DP, HEAD)),
            P(None, None, None, HEAD),
            P(None, None, HEAD),
            P(None, HEAD, None),
            P(None, HEAD),
            P(None, None, HEAD),
            P(None, None, HEAD),
            P(None, HEAD, None),
            P(None, HEAD),
            P(None, HEAD, None),
            P(None, HEAD),
            P(None, HEAD, None),
            P(None, HEAD),
            P(None, HEAD, None),
            P(),
        ),
        out_specs=(
            P(None, (DP, HEAD), None),
            P(None, (DP, HEAD), None),
            P((DP, HEAD), None),
            P(None, None, None, HEAD),
            P(None, None, HEAD),
            P(None, HEAD, None),
            P(None, HEAD),
            P(None, None, HEAD),
            P(None, None, HEAD),
            P(None, HEAD, None),
            P(None, HEAD),
            P(None, HEAD, None),
            P(None, HEAD),
            P(None, HEAD, None),
            P(None, HEAD),
            P(None, HEAD, None),
            P(),
        ),
        check_vma=False,
    )
```

```python
import functools

import jax
import jax.numpy as jnp
from jax import lax
from jax.experimental import pallas as pl
from jax.experimental.pallas import tpu as pltpu
from jax.sharding import PartitionSpec as P

D = 768
FF = 3072
HEAD_DIM = 64
SEQ = 128
LAYERS = 2
SHARDS = 4
PART = D // SHARDS
POOL_PART = PART // 4
CLASSES = 3
EPS = 1e-12
ROOT_HALF = 0.7071067811865476
DENSITY_SCALE = 0.3989422804014327
F32 = jnp.float32
BF16 = jnp.bfloat16
HEAD = "head"
DP = "dp"
AXES = (DP, HEAD)
VMEM_LIMIT = 58 * 1024 * 1024
TALL = PART + 16
FFN_ROWS = 2 * PART + POOL_PART
WIDE = 1024

QB, VB, OB, G0, G1, S0, S1, FB, PB, CW = 0, 1, 2, 3, 4, 5, 6, 11, 12, 13


def dot(left, right, dims):
    return lax.dot_general(left, right, ((dims[:1], dims[1:]), ((), ())), preferred_element_type=F32)


def nn(left, right):
    return dot(left, right, (1, 0))


def nt(left, right):
    return dot(left, right, (1, 1))


def tn(left, right):
    return dot(left, right, (0, 0))


def normalise(resid):
    centred = resid - jnp.mean(resid, -1, keepdims=True)
    rstd = lax.rsqrt(jnp.mean(centred * centred, -1, keepdims=True) + EPS)
    return centred * rstd, rstd


def norm_back(incoming, normed, rstd, gain):
    scaled = incoming * gain
    back = rstd * (
        scaled
        - jnp.mean(scaled, -1, keepdims=True)
        - normed * jnp.mean(scaled * normed, -1, keepdims=True)
    )
    gain_grad = jnp.sum(incoming * normed, 0, keepdims=True)
    shift_grad = jnp.sum(incoming, 0, keepdims=True)
    return back, gain_grad, shift_grad


def cost(micros):
    return pl.CostEstimate(flops=int(micros * 1e10), bytes_accessed=0, transcendentals=0)


def shard_index():
    return lax.axis_index(HEAD)


def quarter_index():
    return lax.axis_index(DP) & 3


def rows_at(index, count):
    return pl.ds(pl.multiple_of(index * count, count), count)


def vmem():
    return pl.BlockSpec(memory_space=pltpu.VMEM)


def anywhere():
    return pl.BlockSpec(memory_space=pl.ANY)


ROOM = {
    "pack": 12, "arrange": 4, "attn_forward": 14, "ffn_forward": 27, "ffn_backward": 26,
    "attn_backward": 18, "ffn_weight": 18, "attn_weight": 12, "halve": 10, "unpack": 10,
}


def room(name):
    for start, size in ROOM.items():
        if name.startswith(start):
            return size << 20
    return 8 << 20


TOKEN = jax.ShapeDtypeStruct((8, 128), F32)


def main_memory():
    return pl.BlockSpec(memory_space=pltpu.HBM)


class Line:
    def __init__(self):
        self.waits = ()

    def call(self, name, micros, kernel, ins, outs, scratch=(), aliases=None):
        waits = tuple(self.waits)
        count, total = len(ins), len(ins) + len(waits) + len(outs)

        def body(*refs):
            kernel(*refs[:count], *refs[count + len(waits) : total], *refs[total + 1 :])

        *result, token = pl.pallas_call(
            body,
            out_shape=[jax.ShapeDtypeStruct(shape, dtype) for shape, dtype, _ in outs] + [TOKEN],
            in_specs=[spec for _, spec in ins] + [main_memory()] * len(waits),
            out_specs=[spec for _, _, spec in outs] + [main_memory()],
            scratch_shapes=list(scratch),
            input_output_aliases=aliases or {},
            compiler_params=pltpu.CompilerParams(vmem_limit_bytes=room(name)),
            cost_estimate=cost(micros),
            name=name,
        )(*[value for value, _ in ins], *waits)
        self.waits = (token,)
        return result

    def gate(self, *values):
        outs = [(value.shape, value.dtype, anywhere()) for value in values]
        aliases = {index: index for index in range(len(values))}
        return self.call("gate", 4, lambda *refs: None, away(*values), outs, aliases=aliases)


def near(*values):
    return [(value, vmem()) for value in values]


def fixed(*values):
    return [(value, main_memory()) for value in values]


def away(*values):
    return [(value, anywhere()) for value in values]


def made(*shapes):
    return [(shape, dtype, vmem()) for shape, dtype in shapes]


def sent(*shapes):
    return [(shape, dtype, anywhere()) for shape, dtype in shapes]


def run_copies(pairs, sems, start):
    copies = [
        pltpu.make_async_copy(src, dst, sems.at[start + index])
        for index, (src, dst) in enumerate(pairs)
    ]
    for item in copies:
        item.start()
    return copies


def wait_copies(copies):
    for item in copies:
        item.wait()


def flip(mesh, axis, bit):
    dp, head = mesh.shape[DP], mesh.shape[HEAD]
    pairs = []
    for place in range(dp):
        for shard in range(head):
            to_place = place ^ bit if axis == DP else place
            to_shard = shard ^ bit if axis == HEAD else shard
            pairs.append((place * head + shard, to_place * head + to_shard))
    return pairs


DIMS = {"c": (HEAD, 1), "y": (HEAD, 2), "d": (HEAD, 3), "x": (DP, 1), "a": (DP, 2), "b": (DP, 4)}


class Moves:
    def __init__(self, mesh):
        self.mesh = mesh

    def __call__(self, dim, value):
        return lax.ppermute(value, AXES, flip(self.mesh, *DIMS[dim]))

    def more(self):
        bit = 8
        while bit < self.mesh.shape[DP]:
            yield bit
            bit *= 2

    def place(self, bit, value):
        return lax.ppermute(value, AXES, flip(self.mesh, DP, bit))


def stack_kernel(one, two, follow, follow_out, stack_ref, sems, *, order):
    refs = {"one": one, "two": two, "follow": follow}
    pairs = [(refs[name], stack_ref.at[index]) for index, name in enumerate(order)]
    wait_copies(run_copies(pairs, sems, 0))


class Spread:
    def __init__(self, line, moves, quarter, last):
        self.line, self.moves, self.last = line, moves, last
        self.far = [moves("y", quarter)]

    def second(self):
        self.far = list(self.line.gate(*self.far))
        self.far += [self.moves("x", self.far[0]), self.moves("a", self.far[0])]

    def third(self):
        follow = 2 if self.last == "x" else 1
        shape = self.far[0].shape
        order = ("one", "two", "follow") if follow == 2 else ("one", "follow", "two")
        operands = (self.far[0], self.far[3 - follow], self.far[follow])
        self.far[follow], stack = self.line.call(
            "stack",
            3,
            functools.partial(stack_kernel, order=order),
            fixed(*operands),
            [(shape, BF16, main_memory()), ((3, *shape), BF16, vmem())],
            [pltpu.SemaphoreType.DMA((3,))],
            {2: 0},
        )
        self.stack = self.moves("c", stack)
        self.far.append(self.moves(self.last, self.far[follow]))

    def fourth(self):
        self.far[3] = self.line.gate(self.far[3])[0]
        self.near = self.moves("c", self.far[3])

    def pieces(self):
        return [*self.far, self.stack, self.near]


def pack_attn_kernel(qkv_ref, out_ref, *refs):
    *whole_refs, quarter_ref, sems = refs
    pairs = []
    for index, own_ref in enumerate(whole_refs):
        layer = index % 2
        pairs += [(qkv_ref.at[layer], own_ref.at[0:3]), (out_ref.at[layer], own_ref.at[3])]
    copies = run_copies(pairs, sems, 0)
    wait_copies(copies[:2])
    quarter_ref[...] = whole_refs[0][quarter_index()]
    wait_copies(copies[2:])


def pack_attn(line, qkv, out):
    whole = ((4, PART, D), BF16)
    return line.call(
        "pack_attn",
        2,
        pack_attn_kernel,
        fixed(qkv, out),
        made(whole, whole, whole, whole, ((PART, D), BF16)),
        [pltpu.SemaphoreType.DMA((8,))],
    )


def pack_ffn_kernel(layer, in_ref, down_ref, pool_ref, own_ref, quarter_ref, sems):
    pairs = []
    for index in range(4):
        target = own_ref.at[index]
        pairs += [
            (in_ref.at[layer, :, index * D : (index + 1) * D], target.at[0:PART]),
            (
                down_ref.at[layer, index * PART : (index + 1) * PART],
                target.at[PART : 2 * PART],
            ),
            (
                pool_ref.at[layer, index * POOL_PART : (index + 1) * POOL_PART],
                target.at[2 * PART : FFN_ROWS],
            ),
        ]
    wait_copies(run_copies(pairs, sems, 0))
    quarter_ref[...] = own_ref[quarter_index()]


def pack_ffn(line, layer, ffn_in, ffn_out, pool):
    return line.call(
        "pack_ffn%d" % layer,
        3,
        functools.partial(pack_ffn_kernel, layer),
        fixed(ffn_in, ffn_out, pool),
        made(((4, FFN_ROWS, D), BF16), ((FFN_ROWS, D), BF16)),
        [pltpu.SemaphoreType.DMA((12,))],
    )


def pack_small_kernel(
    qkv_bias, out_bias, gain, shift, in_bias, down_bias, pool_bias, class_weight, packed_ref
):
    for layer in range(LAYERS):
        packed_ref[layer, QB : VB + 1] = qkv_bias[layer].astype(F32)
        packed_ref[layer, OB : OB + 1] = out_bias[layer : layer + 1].astype(F32)
        packed_ref[layer, G0 : G1 + 1] = gain[layer].astype(F32)
        packed_ref[layer, S0 : S1 + 1] = shift[layer].astype(F32)
        for index in range(4):
            value = in_bias[layer : layer + 1, index * PART : (index + 1) * PART]
            packed_ref[layer, 7 + index : 8 + index] = value.astype(F32)
        packed_ref[layer, FB : FB + 1] = down_bias[layer : layer + 1].astype(F32)
        packed_ref[layer, PB : PB + 1] = pool_bias[layer : layer + 1].astype(F32)
        for cls in range(CLASSES):
            value = class_weight[cls, layer : layer + 1].astype(F32)
            packed_ref[layer, CW + cls : CW + cls + 1] = value


def arrange_kernel(own, core, row, both, shards_ref, small_ref, bias_ref):
    shard = shard_index()
    for slot, ref in enumerate((own, core, row, both)):
        shards_ref[shard ^ slot] = ref[...]
    for part in range(SHARDS):
        for layer in range(LAYERS):
            lanes = slice(part * PART, (part + 1) * PART)
            small_ref[layer, :, lanes] = shards_ref[part, layer]
            for index in range(4):
                target = slice(index * PART, (index + 1) * PART)
                value = shards_ref[part, layer, 7 + index : 8 + index]
                bias_ref[layer, part : part + 1, target] = value


def arrange(line, moves, packed):
    core, row = moves("c", packed), moves("y", packed)
    return line.call(
        "arrange",
        1,
        arrange_kernel,
        near(packed, core, row, moves("d", packed)),
        made(
            ((SHARDS, LAYERS, 16, PART), F32),
            ((LAYERS, 16, D), F32),
            ((LAYERS, SHARDS, D), F32),
        ),
    )


def load_attn_weights(refs, slots, sems, start=0):
    here = quarter_index()
    copies = []
    for slot in range(2):
        if len(refs) == 2:
            pairs = [(refs[slot], slots.at[slot])]
        else:
            pieces = refs[0:4] if slot == 0 else [refs[4].at[0], refs[4].at[1], refs[4].at[2], refs[5]]
            pairs = [(piece, slots.at[slot, here ^ index]) for index, piece in enumerate(pieces)]
        copies.append(run_copies(pairs, sems, start + len(pairs) * slot))
    return copies


def attn_forward_kernel(layer, half, x_ref, *refs):
    if half:
        (shard_small, small, total_in), refs = refs[:3], refs[3:]
        count = 2 if layer or "pair0" not in FORWARD else 6
        weights, refs = refs[:count], refs[count:]
        qkv_ref, probs_ref, context_ref, normed_ref, rstd_ref, low_ref, slots, sems = refs
    else:
        shard_small, weights, refs = refs[0], refs[1:3], refs[3:]
        qkv_ref, probs_ref, context_ref, total_ref, slots, sems = refs
    copies = load_attn_weights(weights, slots, sems)
    shard = shard_index()
    x = x_ref[...]
    if half:
        total = total_in[...] + small[layer, OB : OB + 1].astype(F32)
    else:
        total = x.astype(F32)
    for slot in range(2):
        wait_copies(copies[slot])
        biases = shard_small[shard ^ (2 * half + slot), layer]
        parts = []
        for part in range(3):
            value = nt(x, slots[slot, part])
            if part != 1:
                row = QB if part == 0 else VB
                value = value + biases[row : row + 1].astype(F32)
            value = value.astype(BF16)
            qkv_ref[slot, part] = value
            parts.append(value)
        query, key, val = parts
        places = [
            (
                slice(seq * SEQ, (seq + 1) * SEQ),
                slice(head * HEAD_DIM, (head + 1) * HEAD_DIM),
            )
            for seq in range(2)
            for head in range(PART // HEAD_DIM)
        ]
        scores = jnp.stack([nt(query[at], key[at]) for at in places]) * HEAD_DIM ** (-0.5)
        shifted = jnp.exp(scores - jnp.max(scores, -1, keepdims=True))
        probs = shifted * (1.0 / jnp.sum(shifted, -1, keepdims=True))
        probs_ref[slot] = probs
        low = probs.astype(BF16)
        heads = [nn(low[index], val[at]) for index, at in enumerate(places)]
        half_heads = len(heads) // 2
        context = jnp.concatenate(
            [
                jnp.concatenate(heads[:half_heads], -1),
                jnp.concatenate(heads[half_heads:], -1),
            ],
            0,
        ).astype(BF16)
        context_ref[slot] = context
        total = total + nn(context, slots[slot, 3])
    if half == 0:
        total_ref[...] = total
        return
    normed, rstd = normalise(total)
    normed_ref[...] = normed
    rstd_ref[...] = rstd
    middle = normed * small[layer, G0 : G0 + 1].astype(F32) + small[layer, S0 : S0 + 1].astype(F32)
    low_ref[...] = middle.astype(BF16)


def attn_forward(line, layer, half, x, inputs, weights):
    tokens = x.shape[0]
    outs = [
        ((2, 3, tokens, PART), BF16),
        ((2, 6, SEQ, SEQ), F32),
        ((2, tokens, PART), BF16),
        ((tokens, D), F32),
    ]
    if half:
        outs += [((tokens, 1), F32), ((tokens, D), BF16)]
    return line.call(
        "attn_forward%d%d" % (layer, half),
        7,
        functools.partial(attn_forward_kernel, layer, half),
        near(x, *inputs) + fixed(*weights),
        made(*outs),
        [pltpu.VMEM((2, 4, PART, D), BF16), pltpu.SemaphoreType.DMA((8,))],
    )


def load_ffn_weights(refs, up, down, pool, sems, down_first=False):
    here = quarter_index()
    shard = shard_index()
    ups, downs, pools = [], [], []

    def block_of(source, owner, block):
        ups.append((source.at[0:PART], up.at[block, rows_at(owner, PART)]))
        downs.append((source.at[PART : 2 * PART], down.at[owner, rows_at(block, PART)]))
        if pool is not None:
            target = pool.at[rows_at(owner * 4 + block, POOL_PART)]
            pools.append((source.at[2 * PART : FFN_ROWS], target))

    wholes = refs if len(refs) == 4 else refs[:2]
    for slot, whole in enumerate(wholes):
        for block in range(4):
            block_of(whole.at[block], shard ^ slot, block)
    if len(refs) == 8:
        pieces = [*refs[2:6], refs[6].at[0], refs[6].at[1], refs[6].at[2], refs[7]]
        for index, piece in enumerate(pieces):
            block_of(piece, shard ^ (2 + index // 4), here ^ (index % 4))
    order = (downs, ups, pools) if down_first else (ups, downs, pools)
    first = run_copies(order[0], sems, 0)
    second = run_copies(order[1], sems, len(ups))
    return first, second, run_copies(pools, sems, 2 * len(ups))


def ffn_forward_kernel(
    layer, labels_ref, class_bias_ref, x_ref, normed_ref, low_ref, small, in_bias, *refs
):
    count = 8
    weights, refs = refs[:count], refs[count:]
    if layer:
        (prior_out, prior_logits, prior_ramp), refs = refs[:3], refs[3:]
    act_ref, act_send_ref, slope_ref, normed_two_ref, rstd_two_ref, first_grad_ref = refs[:6]
    out_ref, logits_ref, ramp_ref, up, down, pool, acts, lows, slopes, sems, out_sems = refs[6:]
    ups, downs, pools = load_ffn_weights(weights, up, down, pool, sems)
    leaving = run_copies([(x_ref, act_send_ref.at[2, :, 0:D])], out_sems, 0)
    normed = normed_ref[...]
    low = low_ref[...]

    def row(index):
        return small[layer, index : index + 1].astype(F32)

    total = normed * row(G0) + row(S0) + row(FB)
    for part in range(4):
        lows[part, :, 0:PART] = low[:, part * PART : (part + 1) * PART]
        lows[part, :, PART:] = jnp.zeros((low.shape[0], WIDE - D - PART), BF16)
    wait_copies(ups)
    for block in range(4):
        pre_act = nn(low, up[block]) + in_bias[layer, block : block + 1].astype(F32)
        cumulative = 0.5 * (1.0 + lax.erf(pre_act * ROOT_HALF))
        act = (pre_act * cumulative).astype(BF16)
        density = jnp.exp(-0.5 * pre_act * pre_act) * DENSITY_SCALE
        acts[block] = act
        slopes[block] = cumulative + pre_act * density
        leaving += run_copies([(slopes.at[block], slope_ref.at[block])], out_sems, 1 + block)
        if block == 0:
            wait_copies(downs)
        total = total + nn(act, down[block])
    shard = shard_index()
    pairs = []
    for slot in range(4):
        target = (act_send_ref if slot & 1 else act_ref).at[slot >> 1]
        pairs.append((acts.at[shard ^ slot], target.at[:, 0:D]))
        pairs.append((lows.at[shard ^ slot], target.at[:, D:WIDE]))
    leaving += run_copies(pairs, out_sems, 5)
    wait_copies(pools)
    normed_two, rstd_two = normalise(total)
    normed_two_ref[...] = normed_two
    rstd_two_ref[...] = rstd_two
    output = (normed_two * row(G1) + row(S1)).astype(BF16)

    first = jnp.concatenate([output[0:1], output[SEQ : SEQ + 1]], 0).astype(F32)
    first = jnp.concatenate([first, jnp.zeros((14, D), F32)], 0).astype(BF16)
    pool_weight = pool[...]
    pooled = jnp.tanh(nn(first, pool_weight) + row(PB))
    wide = pooled.astype(BF16).astype(F32)
    lanes = lax.broadcasted_iota(jnp.int32, (16, 128), 1)
    rows = lax.broadcasted_iota(jnp.int32, (16, 128), 0)
    logits = jnp.zeros((16, 128), F32)
    for cls in range(CLASSES):
        value = jnp.sum(wide * row(CW + cls), -1, keepdims=True)
        value = value + class_bias_ref[layer, cls]
        logits = jnp.where(lanes == cls, value, logits)
    valid = lanes < CLASSES
    peak = jnp.max(jnp.where(valid, logits, -jnp.inf), -1, keepdims=True)
    shifted = jnp.where(valid, jnp.exp(logits - peak), 0.0)
    soft = shifted / jnp.sum(shifted, -1, keepdims=True)
    label = jnp.where(rows == 0, labels_ref[0], labels_ref[1])
    logit_grad = (soft - (lanes == label).astype(F32)).astype(BF16)
    logit_wide = logit_grad.astype(F32)
    back = jnp.zeros((16, D), F32)
    for cls in range(CLASSES):
        picked = jnp.sum(jnp.where(lanes == cls, logit_wide, 0.0), -1, keepdims=True)
        back = back + picked * row(CW + cls)
    pool_grad = (back * (1.0 - pooled * pooled)).astype(BF16)
    first_grad_ref[...] = nt(pool_grad, pool_weight)[0:8]
    padded = jnp.concatenate([logit_wide[0:2], jnp.zeros((2, D - 128), F32)], -1)
    ramp = jnp.concatenate(
        [first.astype(F32)[0:2], pool_grad.astype(F32)[0:2], wide[0:2], padded], 0
    ).astype(BF16)
    if layer:
        out_ref[0] = prior_out[...]
        logits_ref[0] = prior_logits[...]
        ramp_ref[0] = prior_ramp[...]
        out_ref[1] = output
        logits_ref[1] = logits[0:8]
        ramp_ref[1] = ramp
    else:
        out_ref[...] = output
        logits_ref[...] = logits[0:8]
        ramp_ref[...] = ramp
    wait_copies(leaving)


def ffn_forward(line, layer, labels, class_bias, x, normed, low, small, in_bias, weights, prior):
    tokens = low.shape[0]
    smem = pl.BlockSpec(memory_space=pltpu.SMEM)
    stack = (2,) if layer else ()
    return line.call(
        "ffn_forward%d" % layer,
        12,
        functools.partial(ffn_forward_kernel, layer),
        [(labels, smem), (class_bias, smem)]
        + near(x, normed, low, small, in_bias)
        + fixed(*weights)
        + near(*prior),
        sent(
            ((2, tokens, WIDE), BF16),
            ((3, tokens, WIDE), BF16),
            ((4, tokens, D), F32),
        )
        + made(
            ((tokens, D), F32),
            ((tokens, 1), F32),
            ((8, D), F32),
            ((*stack, tokens, D), BF16),
            ((*stack, 8, 128), F32),
            ((*stack, 8, D), BF16),
        ),
        [
            pltpu.VMEM((4, D, D), BF16),
            pltpu.VMEM((SHARDS, D, D), BF16),
            pltpu.VMEM((D, D), BF16),
            pltpu.VMEM((4, tokens, D), BF16),
            pltpu.VMEM((4, tokens, WIDE - D), BF16),
            pltpu.VMEM((4, tokens, D), F32),
            pltpu.SemaphoreType.DMA((48,)),
            pltpu.SemaphoreType.DMA((13,)),
        ],
    )


def ffn_backward_kernel(
    layer, grad_ref, first_ref, normed_two_ref, rstd_two_ref, slope_ref, normed_ref, rstd_ref,
    small, *refs
):
    pairs_ref, rows_ref, low_ref, smalls_ref, up, down, pairs, sems, out_sems = refs[-9:]
    downs, ups, _ = load_ffn_weights(refs[:-9], up, down, None, sems, True)

    def row(index):
        return small[layer, index : index + 1].astype(F32)

    grad = grad_ref[...].astype(F32)
    index = lax.broadcasted_iota(jnp.int32, grad.shape, 0)
    grad = grad + jnp.where(index == 0, first_ref[0:1], 0.0)
    grad = grad + jnp.where(index == SEQ, first_ref[1:2], 0.0)
    res_two, gain_two, shift_two = norm_back(grad, normed_two_ref[...], rstd_two_ref[...], row(G1))
    ffn_grad = res_two.astype(BF16)
    pairs[4] = ffn_grad
    leaving = run_copies([(pairs.at[4], pairs_ref.at[4])], out_sems, 4)
    wait_copies(downs)
    middle_grad = res_two
    for block in range(4):
        act_grad = nt(ffn_grad, down[block])
        pre_grad = (act_grad * slope_ref[block]).astype(BF16)
        pairs[block] = pre_grad
        leaving += run_copies([(pairs.at[block], pairs_ref.at[block])], out_sems, block)
        if block == 0:
            wait_copies(ups)
        smalls_ref[block : block + 1] = jnp.sum(pre_grad.astype(F32), 0, keepdims=True)
        middle_grad = middle_grad + nt(pre_grad, up[block])
    res_one, gain_one, shift_one = norm_back(middle_grad, normed_ref[...], rstd_ref[...], row(G0))
    rows_ref[...] = res_one
    low = res_one.astype(BF16)
    low_ref[...] = low
    smalls_ref[4:5] = jnp.sum(ffn_grad.astype(F32), 0, keepdims=True)
    smalls_ref[5:6] = jnp.sum(low.astype(F32), 0, keepdims=True)
    smalls_ref[6:7] = gain_one
    smalls_ref[7:8] = gain_two
    smalls_ref[8:9] = shift_one
    smalls_ref[9:10] = shift_two
    wait_copies(leaving)


def ffn_backward(
    line, layer, grad, first_grad, normed_two, rstd_two, slope, normed, rstd, small, weights
):
    tokens = grad.shape[0]
    return line.call(
        "ffn_backward%d" % layer,
        11,
        functools.partial(ffn_backward_kernel, layer),
        near(grad, first_grad, normed_two, rstd_two, slope, normed, rstd, small)
        + away(*weights),
        sent(((5, tokens, D), BF16))
        + made(
            ((tokens, D), F32),
            ((tokens, D), BF16),
            ((10, D), F32),
        ),
        [
            pltpu.VMEM((4, D, D), BF16),
            pltpu.VMEM((SHARDS, D, D), BF16),
            pltpu.VMEM((5, tokens, D), BF16),
            pltpu.SemaphoreType.DMA((32,)),
            pltpu.SemaphoreType.DMA((5,)),
        ],
    )


def place_pieces(groups, natural, outs, y, sems):
    here = quarter_index()
    pairs = []
    for index, (order, first, count) in enumerate(groups):
        keep_ref, send_ref = outs[2 * index : 2 * index + 2]
        rows = slice(first, first + count)
        for x in range(2):
            for a in range(2):
                if not order:
                    target, unit, place = (send_ref if y else keep_ref), 2 * a + x, 2 * a + x
                else:
                    bits = {"y": y, "x": x, "a": a}
                    outer, middle, inner = (bits[dim] for dim in order)
                    target = send_ref if outer else keep_ref
                    unit, place = (2 * a + x) ^ here, 2 * middle + inner
                pairs.append((natural.at[y, unit, rows], target.at[place]))
    return run_copies(pairs, sems, y * len(pairs))


def piece_shapes(groups):
    shapes = []
    for _, _, count in groups:
        shapes += [((4, count, D), BF16)] * 2
    return shapes


def ffn_weights_kernel(groups, act_ref, act_near_ref, pairs_ref, pairs_near_ref, *refs):
    outs, (natural, sems) = refs[:-2], refs[-2:]
    leaving = []
    for slot in (1, 0):
        mine, other = act_ref[slot], act_near_ref[slot]
        down = tn(mine[:, 0:D], pairs_ref[4]) + tn(other[:, 0:D], pairs_near_ref[4])
        down = down.astype(BF16)
        for block in range(4):
            natural[slot, block, PART : 2 * PART] = down[block * PART : (block + 1) * PART]
            up = tn(mine[:, D : D + PART], pairs_ref[block])
            up = up + tn(other[:, D : D + PART], pairs_near_ref[block])
            natural[slot, block, 0:PART] = up.astype(BF16)
        leaving += place_pieces(groups, natural, outs, slot, sems)
    wait_copies(leaving)


def ffn_weight_grads(line, layer, groups, act, act_near, pairs, pairs_near):
    return line.call(
        "ffn_weight_grads%d" % layer,
        8,
        functools.partial(ffn_weights_kernel, groups),
        near(act, act_near, pairs, pairs_near),
        sent(*piece_shapes(groups)),
        [pltpu.VMEM((2, 4, 2 * PART, D), BF16), pltpu.SemaphoreType.DMA((8 * len(groups),))],
    )


def attn_weights_kernel(
    groups, x_ref, acts_near_ref, grad_ref, pairs_ref, near_ref, *refs
):
    outs, (natural, sems) = refs[-2 - 2 * len(groups) : -2], refs[-2:]
    leaving = []
    cut = 3 * PART
    tokens = x_ref.shape[0]
    x_near = acts_near_ref[2, :, 0:D]
    grad_near = near_ref[2 * tokens : 3 * tokens]
    if len(refs) > 2 + 2 * len(groups):
        smalls_ref, by_shard = refs[0], refs[-3]
        outs = refs[1:-3]
        smalls = []
        for layer in range(LAYERS):
            start = 3 * tokens + 32 * layer
            high = near_ref[start : start + 16].astype(F32)
            rest = near_ref[start + 16 : start + 32].astype(F32)
            smalls.append(smalls_ref[layer] + (high + rest)[0:12])
        for part in range(SHARDS):
            lanes = slice(part * PART, (part + 1) * PART)
            for layer in range(LAYERS):
                row = 3 * layer
                by_shard[part, row : row + 1] = smalls[layer][part : part + 1]
                for item in range(8):
                    target = slice((item % 4) * PART, (item % 4 + 1) * PART)
                    value = smalls[layer][4 + item : 5 + item, lanes]
                    by_shard[part, row + 1 + item // 4 : row + 2 + item // 4, target] = value
            by_shard[part, 6:16] = jnp.zeros((10, D), F32)
        shard = shard_index()
        for slot in range(2):
            natural[slot, 0, PART:TALL] = by_shard[shard ^ (2 * slot)].astype(BF16)
            for unit in range(1, 4):
                natural[slot, unit, PART:TALL] = jnp.zeros((TALL - PART, D), BF16)
    for slot in (1, 0):
        mine, other = pairs_ref[slot], near_ref[slot * tokens : (slot + 1) * tokens]
        value = tn(mine[:, 0:cut], x_ref[...]) + tn(other[:, 0:cut], x_near)
        value = value.astype(BF16)
        for unit in range(3):
            natural[slot, unit, 0:PART] = value[unit * PART : (unit + 1) * PART]
        value = tn(mine[:, cut:D], grad_ref[...]) + tn(other[:, cut:D], grad_near)
        natural[slot, 3, 0:PART] = value.astype(BF16)
        leaving += place_pieces(groups, natural, outs, slot, sems)
    wait_copies(leaving)


def attn_weight_grads(line, layer, groups, *operands):
    return line.call(
        "attn_weight_grads%d" % layer,
        5,
        functools.partial(attn_weights_kernel, groups),
        near(*operands),
        sent(*piece_shapes(groups)),
        ([pltpu.VMEM((SHARDS, 16, D), F32)] if len(operands) > 5 else [])
        + [
            pltpu.VMEM((2, 4, groups[0][2], D), BF16),
            pltpu.SemaphoreType.DMA((8 * len(groups),)),
        ],
    )


def attn_backward_kernel(
    layer, res_ref, grad_ref, smalls_in_ref, *refs
):
    count = 10 if layer or "pair0" not in FORWARD else 14
    kept, weights, refs = refs[:6], refs[6:count], refs[count:]
    if layer == 0:
        prior, refs = refs[0], refs[1:]
    pairs_ref, pairs_send_ref, rows_ref, smalls_ref, slots, sems, sums = refs
    tokens = grad_ref.shape[0]
    copies = load_attn_weights(weights[:2], slots.at[0:2], sems)
    copies += load_attn_weights(weights[2:], slots.at[2:4], sems, 2)
    shard = shard_index()
    grad = grad_ref[...]
    total = res_ref[...]
    for slot in range(4):
        wait_copies(copies[slot])
        half, index = slot >> 1, slot & 1
        qkv_ref, probs_ref, context_ref = kept[3 * half : 3 * half + 3]
        context_grad = nt(grad, slots[slot, 3]).astype(BF16)
        places = [
            (
                slice(seq * SEQ, (seq + 1) * SEQ),
                slice(head * HEAD_DIM, (head + 1) * HEAD_DIM),
            )
            for seq in range(2)
            for head in range(PART // HEAD_DIM)
        ]
        query, key, val = (qkv_ref[index, part] for part in range(3))
        probs = probs_ref[index]
        prob_grad = jnp.stack([nt(context_grad[at], val[at]) for at in places])
        mean = jnp.sum(prob_grad * probs, -1, keepdims=True)
        score_grad = (probs * (prob_grad - mean)).astype(BF16)
        probs_low = probs.astype(BF16)
        scale = HEAD_DIM ** (-0.5)
        heads = [
            [nn(score_grad[i], key[at]) * scale for i, at in enumerate(places)],
            [tn(score_grad[i], query[at]) * scale for i, at in enumerate(places)],
            [tn(probs_low[i], context_grad[at]) for i, at in enumerate(places)],
        ]
        half_heads = len(places) // 2
        seq_rows = [
            [jnp.concatenate(group[:half_heads], -1), jnp.concatenate(group[half_heads:], -1)]
            for group in heads
        ]
        for part in range(3):
            value = jnp.concatenate(seq_rows[part], 0).astype(BF16)
            if slot & 1:
                rows = slice(half * tokens, (half + 1) * tokens)
                pairs_send_ref[rows, part * PART : (part + 1) * PART] = value
            else:
                pairs_ref[half, :, part * PART : (part + 1) * PART] = value
            if part != 1:
                sums[shard ^ slot, part // 2] = jnp.sum(value.astype(F32), 0, keepdims=True)
            total = total + nn(value, slots[slot, part])
        if slot & 1:
            pairs_send_ref[half * tokens : (half + 1) * tokens, 3 * PART : D] = context_ref[index]
        else:
            pairs_ref[half, :, 3 * PART : D] = context_ref[index]
    pairs_send_ref[2 * tokens : 3 * tokens] = grad
    rows_ref[...] = total.astype(rows_ref.dtype)
    own = [
        jnp.concatenate([sums[part, index] for part in range(SHARDS)], -1) for index in range(2)
    ]
    if layer:
        smalls_ref[0:10] = smalls_in_ref[...]
        smalls_ref[10:11] = own[0]
        smalls_ref[11:12] = own[1]
    else:
        smalls_ref[1] = prior[...]
        smalls_ref[0, 0:10] = smalls_in_ref[...]
        smalls_ref[0, 10:11] = own[0]
        smalls_ref[0, 11:12] = own[1]
        for index in range(LAYERS):
            value = smalls_ref[index]
            high = value.astype(BF16)
            rest = (value - high.astype(F32)).astype(BF16)
            start = 3 * tokens + 32 * index
            pairs_send_ref[start : start + 16] = jnp.concatenate(
                [high, jnp.zeros((4, D), BF16)], 0
            )
            pairs_send_ref[start + 16 : start + 32] = jnp.concatenate(
                [rest, jnp.zeros((4, D), BF16)], 0
            )


def attn_backward(line, layer, res, grad, kept, smalls, weights, prior):
    tokens = grad.shape[0]
    return line.call(
        "attn_backward%d" % layer,
        15,
        functools.partial(attn_backward_kernel, layer),
        near(res, grad, smalls, *kept) + away(*weights) + near(*prior),
        made(
            ((2, tokens, D), BF16),
            ((3 * tokens + (0 if layer else 64), D), BF16),
            ((tokens, D), F32 if layer else BF16),
            ((12, D) if layer else (2, 12, D), F32),
        ),
        [
            pltpu.VMEM((4, 4, PART, D), BF16),
            pltpu.SemaphoreType.DMA((12,)),
            pltpu.VMEM((SHARDS, 2, 1, PART), F32),
        ],
    )


def halve_kernel(keep_ref, came_ref, low_ref, high_ref):
    half = low_ref.shape[0]
    low_ref[...] = keep_ref[0:half] + came_ref[0:half]
    high_ref[...] = keep_ref[half:] + came_ref[half:]


def add_kernel(keep_ref, came_ref, sum_ref):
    sum_ref[...] = keep_ref[...] + came_ref[...]


def reduction(line, moves, name, order, back, keep, send):
    shape = keep.shape
    micros = 1 + shape[1] / 192
    if not order:
        came = moves("y", send)
        yield
        total = line.call(
            "add_%s" % name, micros, add_kernel, near(keep, came), made((shape, BF16))
        )[0]
        yield (back, lax.psum(total, DP))
    came = moves(order[0], send)
    for step, dim in enumerate(order[1:]):
        yield
        half = (keep.shape[0] // 2, *shape[1:])
        keep, send = line.call(
            "halve_%s%d" % (name, step), micros, halve_kernel, near(keep, came),
            made((half, BF16), (half, BF16)),
        )
        came = moves(dim, send)
    yield
    keep, came = keep[0], came[0]
    total = line.call(
        "add_%s" % name, micros, add_kernel, near(keep, came), made((shape[1:], BF16))
    )[0]
    came = moves("b", total)
    for bit in moves.more():
        yield
        total = line.call(
            "more_%s%d" % (name, bit), micros, add_kernel, near(total, came),
            made((shape[1:], BF16)),
        )[0]
        came = moves.place(bit, total)
    yield
    total = line.call(
        "last_%s" % name, micros, add_kernel, near(total, came), made((shape[1:], BF16))
    )[0]
    came = moves(back[0], total)
    yield
    both = line.call(
        "both_%s" % name, micros, both_kernel, near(total, came), made(((2, *shape[1:]), BF16))
    )[0]
    yield (back, both, moves(back[1], both))


def join_kernel(one_ref, two_ref, joint_ref):
    count = one_ref.shape[0]
    joint_ref[0:count] = one_ref[...]
    joint_ref[count : 2 * count] = two_ref[...]


def join(line, one, two):
    shape = (2 * one.shape[0], *one.shape[1:])
    return line.call("join%d" % shape[0], 1, join_kernel, near(one, two), made((shape, BF16)))[0]


def both_kernel(one_ref, two_ref, both_ref):
    both_ref[0] = one_ref[...]
    both_ref[1] = two_ref[...]


def unpack_kernel(back, first, targets, prior, *refs):
    values = 2 if back else 1
    quarters = refs[:values]
    outs = refs[values + prior : -2]
    whole, sems = refs[-2:]
    here = quarter_index()
    count = whole.shape[1]
    for index in range(4):
        if not back:
            whole[index] = quarters[0][index, first : first + count].astype(F32)
            continue
        bits = {back[0]: index & 1, back[1]: index >> 1}
        relative = 2 * bits["a"] + bits["x"]
        quarter = quarters[index >> 1][index & 1, first : first + count]
        whole[relative ^ here] = quarter.astype(F32)
    if count == TALL:
        qkv_bias, out_bias, gain, shift, in_bias, down_bias = outs[len(targets) :]
        for layer in range(LAYERS):
            row = PART + 3 * layer

            def item(index):
                at = row + 1 + index // 4
                return whole[0, at : at + 1, (index % 4) * PART : (index % 4 + 1) * PART]

            in_bias[layer : layer + 1] = whole[0, row : row + 1]
            down_bias[layer : layer + 1] = item(0)
            out_bias[layer : layer + 1] = item(1)
            for index in range(2):
                gain[layer, index : index + 1] = item(2 + index)
                shift[layer, index : index + 1] = item(4 + index)
                qkv_bias[layer, index : index + 1] = item(6 + index)
    pairs = [
        (whole.at[unit, 0:PART], outs[which].at[where])
        for unit, which, where in targets_of(targets)
    ]
    wait_copies(run_copies(pairs, sems, 0))


def targets_of(targets):
    return [(unit, which, where) for which, places in enumerate(targets) for unit, where in places]


SMALL_SHAPES = (
    (LAYERS, 2, PART), (LAYERS, PART), (LAYERS, 2, PART), (LAYERS, 2, PART), (LAYERS, D), (LAYERS, PART)
)


def unpack(line, name, quarters, first, shapes, targets, prior):
    back, *values = quarters
    aliases = {len(values) + index: index for index in range(len(prior))}
    count = TALL if values[0].shape[1] == TALL else PART
    outs = [(shape, F32, anywhere()) for shape in shapes]
    if count == TALL:
        outs += made(*[(shape, F32) for shape in SMALL_SHAPES])
    return line.call(
        name,
        3,
        functools.partial(unpack_kernel, back, first, targets, len(prior)),
        near(*values) + away(*prior),
        outs,
        [pltpu.VMEM((4, count, D), F32), pltpu.SemaphoreType.DMA((4,))],
        aliases,
    )


def unpack_up(line, layer, quarters, first, prior):
    places = [(unit, (layer, slice(None), slice(unit * D, (unit + 1) * D))) for unit in range(4)]
    return unpack(
        line, "unpack_up%d" % layer, quarters, first, [(LAYERS, PART, FF)], [places], prior
    )


def unpack_down(line, layer, quarters, first, prior):
    places = [(unit, (layer, slice(unit * PART, (unit + 1) * PART))) for unit in range(4)]
    return unpack(
        line, "unpack_down%d" % layer, quarters, first, [(LAYERS, D, D)], [places], prior
    )


def unpack_attn(line, layer, quarters, first, prior):
    return unpack(
        line,
        "unpack_attn%d" % layer,
        quarters,
        first,
        [(LAYERS, 3, PART, D), (LAYERS, PART, D)],
        [[(unit, (layer, unit)) for unit in range(3)], [(3, (layer,))]],
        prior,
    )


def pool_grads(ramp, shard):
    ramp = ramp.reshape(ramp.shape[0], LAYERS, 4, 2, D)
    ramp = jnp.transpose(ramp, (1, 2, 0, 3, 4)).reshape(LAYERS, 4, -1, D)
    first, pool_grad, pooled, logit_grad = (ramp[:, part] for part in range(4))
    logit_grad = logit_grad[:, :, 0:CLASSES]
    own_first = lax.dynamic_slice_in_dim(first, shard * PART, PART, 2)
    own_pooled = lax.dynamic_slice_in_dim(pooled, shard * PART, PART, 2)
    pool_weight_grad = jnp.einsum("lnd,lne->lde", own_first, pool_grad, preferred_element_type=F32)
    class_weight_grad = jnp.einsum(
        "lnd,lnc->ldc", own_pooled, logit_grad, preferred_element_type=F32
    )
    class_bias_grad = jnp.sum(logit_grad.astype(F32), 1)
    own_pool = lax.dynamic_slice_in_dim(pool_grad, shard * PART, PART, 2)
    pool_bias_grad = jnp.sum(own_pool.astype(F32), 1)
    return pool_weight_grad, pool_bias_grad, class_weight_grad, class_bias_grad


ROUTES = {
    "f1": ("yxa", "ax"),
    "a1": ("axy", "ax"),
    "f0": ("axy", "xa"),
    "a0": ("xya", "xa"),
}
FORWARD_NAMES = (
    "ffn0", "small0", "arrange0", "attn0", "row0", "near0", "second0", "ffn1", "third0",
    "cross0", "swap0", "far0", "meet0", "second1", "fourth0", "row1", "block0", "third1",
    "near1", "cross1", "swap1", "far1", "fourth1", "block1",
)
FORWARD = [FORWARD_NAMES[index] for index in (
    0, 1, 2, 3, 4, 5, 6, 7, 8, 9, 10, 11, 12, 13, 14, 15, 16, 17, 18, 19, 20, 21, 22, 23,
)]
SCHEDULE_NAMES = (
    "R0", "F1", "R1", "A1", "FW1", "AW1", "F0", "A0", "FW0", "AW0", "a1", "f1", "a0", "f0",
    "Ua1", "Ua0", "P1", "Uf1", "Uf0",
)
SCHEDULE = [SCHEDULE_NAMES[index] for index in (
    0, 1, 2, 3, 2, 4, 2, 5, 2, 6, 2, 7, 8, 9, 10, 11, 12, 10, 12, 13, 10, 11, 10, 12, 11, 12,
    13, 10, 12, 13, 14, 11, 15, 16, 13, 11, 13, 17, 18,
)]


def on_device(
    mesh,
    hidden_in,
    out_cotangent,
    labels,
    qkv_weight,
    qkv_bias,
    out_weight,
    out_bias,
    norm_gain,
    norm_shift,
    ffn_in,
    ffn_in_bias,
    ffn_out,
    ffn_out_bias,
    pool_weight,
    pool_bias,
    class_weight,
    class_bias,
):
    moves = Moves(mesh)
    line = Line()
    shard = shard_index()
    qkv_turned = jnp.swapaxes(qkv_weight, 2, 3)

    class_bias_wide = class_bias.astype(F32)
    ffn_own, ffn_far, attn_own, attn_far = [None] * 2, [None] * 2, [None] * 2, [None] * 2
    kept, held = [None] * 2, {"x0": hidden_in}

    def go(name):
        layer = int(name[-1])
        part = name[:-1]
        if part == "small":
            held["packed"] = line.call(
                "pack_small",
                1,
                pack_small_kernel,
                near(
                    qkv_bias, out_bias, norm_gain, norm_shift, ffn_in_bias, ffn_out_bias, pool_bias,
                    jnp.transpose(class_weight, (2, 0, 1)),
                ),
                made(((LAYERS, 16, PART), F32)),
            )[0]
        elif part == "arrange":
            held["small"] = arrange(line, moves, held["packed"])
        elif part == "ffn":
            pack, quarter = pack_ffn(line, layer, ffn_in, ffn_out, pool_weight)
            ffn_own[layer] = [pack]
            ffn_far[layer] = Spread(line, moves, quarter, "a" if layer else "x")
        elif part == "attn":
            *own, quarter = pack_attn(line, qkv_turned, out_weight)
            held["leaving"] = own[2:]
            if "pair0" in FORWARD:
                attn_far[0] = Spread(line, moves, quarter, "a")
            for index, value in enumerate(own[:2]):
                attn_own[index] = [value, moves("c", value)]
        elif part == "second":
            ffn_far[layer].second()
        elif part == "third":
            ffn_far[layer].third()
        elif part == "fourth":
            ffn_far[layer].fourth()
        elif part == "pair":
            attn_far[0].second()
        elif part == "last":
            attn_far[0].third()
        elif part == "end":
            attn_far[0].fourth()
            attn_far[0] = attn_far[0].pieces()
        elif part == "row":
            held["far%d" % layer] = moves("y", line.gate(held["leaving"][layer])[0])
        elif part == "cross":
            far = line.gate(held["far%d" % layer])[0]
            attn_far[layer] = [far, moves("c", far)]
        elif part == "swap":
            pack = line.gate(ffn_own[layer][0])[0]
            ffn_own[layer] = [pack, moves("c", pack)]
        elif part == "meet":
            line.waits = (*line.waits, ffn_own[layer][1], ffn_far[layer].stack)
        elif part == "near":
            shard_small, small, in_bias = held["small"]
            *attn_near, total = attn_forward(
                line, layer, 0, held["x%d" % layer], (shard_small,), attn_own[layer]
            )
            kept[layer] = [attn_near, total]
        elif part == "far":
            shard_small, small, in_bias = held["small"]
            attn_near, total = kept[layer]
            *attn_rest, normed, rstd, low = attn_forward(
                line, layer, 1, held["x%d" % layer], (shard_small, small, total), attn_far[layer]
            )
            kept[layer] = [(attn_near + attn_rest, normed, rstd), low]
        elif part == "block":
            shard_small, small, in_bias = held["small"]
            attention, low = kept[layer]
            x = held["x%d" % layer]
            if layer:
                line.waits = (*line.waits, kept[0][2][1])
            act, act_send, slope, normed_two, rstd_two, first_grad, *prior = ffn_forward(
                line, layer, labels, class_bias_wide, x, attention[1], low, small, in_bias,
                ffn_own[layer] + ffn_far[layer].pieces(), held.get("prior", ()),
            )
            act_near = moves("c", act_send)
            kept[layer] = (
                x, attention, (act, act_near), (slope, normed_two, rstd_two, first_grad)
            )
            held["prior"] = prior
            held["x1"] = prior[0]

    for name in FORWARD:
        go(name)
    ffn_weights = [ffn_own[layer] + ffn_far[layer].pieces() for layer in range(LAYERS)]
    nears = [kept[layer][2][1] for layer in range(LAYERS)]
    small = held["small"][1]
    block_outputs, logits, ramp = held["prior"]

    chains, results, state = {}, {}, {"grad": out_cotangent, "prior": ()}
    ramp_value = [ramp[None]]
    ramp_steps = [(HEAD, 1), (HEAD, 2)]
    bit = 1
    while bit < mesh.shape[DP]:
        ramp_steps.append((DP, bit))
        bit *= 2

    def begin(names, pieces):
        for index, name in enumerate(names):
            keep, send = pieces[2 * index : 2 * index + 2]
            chains[name] = reduction(line, moves, name, *ROUTES[name], keep, send)
            next(chains[name])

    def step(name):
        layer = int(name[-1])
        if name == "R0":
            ramp_value[0] = line.gate(ramp_value[0])[0]
        elif name[:-1] == "F":
            _, (_, normed, rstd), _, (slope, normed_two, rstd_two, first_grad) = kept[layer]
            pairs, res, low, rows = ffn_backward(
                line, layer, state["grad"], first_grad, normed_two, rstd_two, slope, normed, rstd,
                small, ffn_weights[layer],
            )
            state["ffn"] = (pairs, moves("c", pairs))
            state["low"] = low
            state["res"], state["rows"] = res, rows
            line.waits = (*line.waits, nears[layer])
        elif name[:-1] == "A":
            pairs, send, grad, smalls = attn_backward(
                line, layer, state["res"], state["low"], kept[layer][1][0], state["rows"],
                attn_own[layer] + attn_far[layer], state["prior"],
            )
            state["attn"] = (pairs, moves("c", send))
            state["grad"], state["prior"] = grad, (smalls,)
        elif name[:-1] == "FW":
            names = [key for key in ROUTES if key[-1] == name[-1] and key[0] != "a"]
            spans = {"f": (0, 2 * PART), "u": (0, PART), "d": (PART, PART)}
            groups = [(ROUTES[key][0], *spans[key[0]]) for key in names]
            begin(names, ffn_weight_grads(line, layer, groups, *kept[layer][2], *state["ffn"]))
        elif name[:-1] == "AW":
            key = "a" + name[-1]
            groups = [(ROUTES[key][0], 0, PART if layer else TALL)]
            operands = (kept[layer][0], kept[layer][2][1], state["low"], *state["attn"])
            if layer == 0:
                operands += state["prior"]
            begin([key], attn_weight_grads(line, layer, groups, *operands))
        elif name == "R1":
            for _ in range(max(1, len(ramp_steps) - 4)):
                axis, bit = ramp_steps.pop(0)
                came = lax.ppermute(ramp_value[0], AXES, flip(mesh, axis, bit))
                ramp_value[0] = join(line, ramp_value[0], came)
        elif name == "P1":
            state["pool"] = pool_grads(line.gate(ramp_value[0])[0], shard)
            line.waits = (*line.waits, *state["pool"])
        elif name[0] == "U":
            key = name[1:]
            while key not in results:
                results[key] = next(chains[key])
                if results[key] is None:
                    del results[key]
            if key[0] in "uf":
                state["up"] = unpack_up(line, layer, results[key], 0, state.get("up", ()))
            if key[0] in "df":
                first = PART if key[0] == "f" else 0
                state["down"] = unpack_down(line, layer, results[key], first, state.get("down", ()))
            if key[0] == "a":
                state["attn_out"] = unpack_attn(
                    line, layer, results[key], 0, state.get("attn_out", ())
                )
        else:
            result = next(chains[name], None)
            if result is not None:
                results[name] = result

    for name in SCHEDULE:
        step(name)
    qkv_grad, out_grad, qkv_bias_grad, out_bias_grad, *smalls = state["attn_out"]
    gain_grad, shift_grad, in_bias_grad, down_bias_grad = smalls
    pool_weight_grad, pool_bias_grad, class_weight_grad, class_bias_grad = state["pool"]
    return (
        block_outputs,
        logits[:, 0:2, 0:CLASSES],
        state["grad"],
        jnp.swapaxes(qkv_grad, 2, 3),
        qkv_bias_grad,
        out_grad,
        out_bias_grad,
        gain_grad,
        shift_grad,
        state["up"][0],
        in_bias_grad,
        state["down"][0],
        down_bias_grad,
        pool_weight_grad,
        pool_bias_grad,
        class_weight_grad,
        class_bias_grad,
    )


def solution(mesh):
    return jax.shard_map(
        functools.partial(on_device, mesh),
        mesh=mesh,
        in_specs=(
            P((DP, HEAD), None),
            P((DP, HEAD), None),
            P((DP, HEAD)),
            P(None, None, None, HEAD),
            P(None, None, HEAD),
            P(None, HEAD, None),
            P(None, HEAD),
            P(None, None, HEAD),
            P(None, None, HEAD),
            P(None, HEAD, None),
            P(None, HEAD),
            P(None, HEAD, None),
            P(None, HEAD),
            P(None, HEAD, None),
            P(None, HEAD),
            P(None, HEAD, None),
            P(),
        ),
        out_specs=(
            P(None, (DP, HEAD), None),
            P(None, (DP, HEAD), None),
            P((DP, HEAD), None),
            P(None, None, None, HEAD),
            P(None, None, HEAD),
            P(None, HEAD, None),
            P(None, HEAD),
            P(None, None, HEAD),
            P(None, None, HEAD),
            P(None, HEAD, None),
            P(None, HEAD),
            P(None, HEAD, None),
            P(None, HEAD),
            P(None, HEAD, None),
            P(None, HEAD),
            P(None, HEAD, None),
            P(),
        ),
        check_vma=False,
    )
```
